512 devices in a mesh: blk: 32 (over z, y_lo), head: 16 (over y_hi, x, core).
Axes of the slice: x: 4, y: 4 (y_hi: 2, y_lo: 2; y = y_hi * 2 + y_lo), z: 16, core: 2. Of those that a mesh axis runs over, the one named last changes fastest.
Arguments:
- node_feats: bfloat16 [65536, 512], P(('blk', 'head')), may hold values from -16 to 16
- graph_ids: int32 [65536], replicated, may hold values from 0 to 4095, never falling along the last dimension, each value on 1 to 32 neighbouring positions
- pair_tiles: int32 [32, 32, 8], P('blk'), may hold values from 0 to 255, as said below
- pair_count: int32 [32, 32], P('blk'), may hold values from 0 to 8, as said below
- w_query: bfloat16 [512, 512], replicated, may hold values from -0.4375 to 0.4375
- w_key: bfloat16 [512, 512], replicated, may hold values from -0.4375 to 0.4375
- w_value: bfloat16 [512, 512], replicated, may hold values from -0.25 to 0.25
- w_out: bfloat16 [512, 512], replicated, may hold values from -0.5 to 0.5
- ln1_gain: float32 [512], replicated, may hold values from 0.1 to 1.9
- ln1_bias: float32 [512], replicated, may hold values from -2.4 to 2.4
- w_up: bfloat16 [512, 1024], replicated, may hold values from -0.25 to 0.25
- b_up: float32 [1024], replicated, may hold values from -3 to 3
- w_down: bfloat16 [1024, 512], replicated, may hold values from -0.25 to 0.25
- ln2_gain: float32 [512], replicated, may hold values from 0.1 to 1.9
- ln2_bias: float32 [512], replicated, may hold values from -2.4 to 2.4
Outputs:
- layer_out: float32 [65536, 512], P(('blk', 'head'))
The draws below stay inside these ranges and needn't reach their ends.
Inputs may be any that keep to these rules, and one draw needn't show every extreme that they name: `pair_tiles`: each entry is q * 16 + k for a query block q and key block k of the two groups; the entries of one list are distinct. `pair_count`: every query group has some key group with 8 pairs used. `graph_ids`: values never fall along the nodes.
All inputs are finite; a program needn't handle non-finite values.
Results may differ from the reference program's by a relative error of at most 0.0085.
The reference program's roundings to bfloat16 on the way (of `attended`, `normed` and `hidden`) count: a program that leaves them out, or rounds other values in their place, can miss the bound.
Values may be sent and summed in bfloat16 or wider, within the bound.
No kernel may reach another device: no remote copies, remote signals or barrier semaphores. Data moves between devices by JAX's collectives and lax.ppermute only.
A program may use at most 192 MiB of HBM per device.

```python
import math
from functools import reduce
import jax
import jax.numpy as jnp
import numpy as np
from jax import lax

D = 512
HEADS = 8
FF = 1024
BLOCK = 128
GROUPS = 32
GROUP_BLOCKS = 16
CAP = 8
NODES = 65536


def draw_node_feats(key, part):
    key = jax.random.fold_in(key, 11)
    first = jax.random.fold_in(key, 0)
    values = jnp.clip(jax.random.normal(first, (NODES, D), jnp.float32), -6.0, 6.0)
    return values.astype(jnp.bfloat16)


def draw_pair_tiles(key, part):
    key = jax.random.fold_in(key, 23)
    possible = GROUP_BLOCKS * GROUP_BLOCKS
    scores = jax.random.randint(key, (GROUPS, GROUPS, possible), 0, 1 << 20) * possible + jnp.arange(possible, dtype=jnp.int32)
    order = jnp.argsort(scores, axis=-1, stable=True)
    return order[:, :, :CAP].astype(jnp.int32)


def draw_pair_count(key, part):
    key = jax.random.fold_in(key, 37)
    first, second, third = jax.random.split(key, 3)
    counts = jax.random.randint(first, (GROUPS, GROUPS), 0, CAP + 1)
    used = jax.random.randint(third, (GROUPS, GROUPS), 0, 2) == 0
    counts = jnp.where(used, counts, 0)
    full_column = jax.random.randint(second, (GROUPS, 1), 0, GROUPS)
    return jnp.where(jnp.arange(GROUPS)[None, :] == full_column, CAP, counts).astype(jnp.int32)


def profile(number_of, total, bound, lean):
    loads = [(1 << 20) // math.isqrt(grade ** lean) + 1 for grade in range(2, number_of + 1)]
    rest, holding = total - bound - (number_of - 1), [1] * (number_of - 1)
    while rest > 0:
        candidates = [i for i in range(number_of - 1) if holding[i] < bound]
        whole, left = sum([loads[i] for i in candidates]), rest
        for i in candidates:
            extra = min(bound - holding[i], max(1, left * loads[i] // whole), rest)
            holding[i] = holding[i] + extra
            rest = rest - extra
    return np.array([bound] + holding)


def ragged_sizes(own_key, amount, total, reach, lean):
    if amount == 2:
        one = jax.random.randint(own_key, (), max(1, total - reach), min(reach, total - 1) + 1)
        return jnp.stack([one, total - one])
    lengths = jnp.asarray(profile(amount, total, reach, lean), jnp.int32)
    couples = (amount - 1) // 2
    source_of, sink = lengths[1:1 + 2 * couples:2], lengths[2:2 + 2 * couples:2]
    slack = jnp.minimum(source_of - 1, reach - sink)
    passed = jax.random.randint(jax.random.fold_in(own_key, 1), (couples,), 0, 1 << 20) % (slack + 1)
    lengths = lengths.at[1:1 + 2 * couples:2].set(source_of - passed).at[2:2 + 2 * couples:2].set(sink + passed)
    return lengths[jax.random.permutation(jax.random.fold_in(own_key, 2), amount)]


def bell_draw(own_key, extent, scale, limit, held_as=jnp.bfloat16):
    values = scale * jax.random.normal(own_key, extent, jnp.float32)
    return jnp.clip(values, min=-limit, max=limit).astype(held_as)


def setup_inputs(seed: int = 0) -> dict:
    arg_keys = jax.random.split(jax.random.key(seed), 16)
    node_feats = draw_node_feats(jax.random.fold_in(arg_keys[15], 71), 0)
    graph_ids = jnp.searchsorted(jnp.cumsum(ragged_sizes(arg_keys[1], NODES // 16, NODES, 32, 2)), jnp.arange(NODES), side="right").astype(jnp.int32)
    pair_tiles = draw_pair_tiles(jax.random.fold_in(arg_keys[15], 71), 0)
    pair_count = draw_pair_count(jax.random.fold_in(arg_keys[15], 71), 0)
    w_query = bell_draw(arg_keys[4], (D, D), (2 * D // 5) ** -0.5, 0.4375)
    w_key = bell_draw(arg_keys[5], (D, D), (2 * D // 5) ** -0.5, 0.4375)
    w_value = bell_draw(arg_keys[6], (D, D), D ** -0.5, 0.25)
    w_out = bell_draw(arg_keys[7], (D, D), (D // 4) ** -0.5, 0.5)
    ln1_gain = jnp.clip(1.0 + 0.18 * jax.random.normal(arg_keys[8], (D,), jnp.float32), 0.1, 1.9)
    ln1_bias = bell_draw(arg_keys[9], (D,), 0.4, 2.4, jnp.float32)
    w_up = bell_draw(arg_keys[10], (D, FF), D ** -0.5, 0.25)
    b_up = bell_draw(arg_keys[11], (FF,), 0.5, 3.0, jnp.float32)
    w_down = bell_draw(arg_keys[12], (FF, D), (FF // 2) ** -0.5, 0.25)
    ln2_gain = jnp.clip(1.0 + 0.18 * jax.random.normal(arg_keys[13], (D,), jnp.float32), 0.1, 1.9)
    ln2_bias = bell_draw(arg_keys[14], (D,), 0.4, 2.4, jnp.float32)
    return {"node_feats": node_feats, "graph_ids": graph_ids, "pair_tiles": pair_tiles, "pair_count": pair_count, "w_query": w_query, "w_key": w_key, "w_value": w_value, "w_out": w_out, "ln1_gain": ln1_gain, "ln1_bias": ln1_bias, "w_up": w_up, "b_up": b_up, "w_down": w_down, "ln2_gain": ln2_gain, "ln2_bias": ln2_bias}


floor_score = -1e+30

def layer_norm(value, gain, bias):
    mean = lax.optimization_barrier(jnp.mean(value, -1, keepdims=True))
    centred = value - mean
    spread = lax.optimization_barrier(jnp.mean(centred * centred, -1, keepdims=True))
    return centred * lax.rsqrt(spread + 1e-05) * gain + bias

def rounded(prob):
    return lax.optimization_barrier(prob.astype(jnp.bfloat16)).astype(jnp.float32)

def reference(node_feats, graph_ids, pair_tiles, pair_count, w_query, w_key, w_value, w_out, ln1_gain, ln1_bias, w_up, b_up, w_down, ln2_gain, ln2_bias):
    head_dim = D // HEADS
    blocks = GROUPS * GROUP_BLOCKS
    scale = 1.0 / math.sqrt(head_dim)
    query = jnp.dot(node_feats, w_query, preferred_element_type=jnp.float32).astype(jnp.bfloat16).reshape(blocks, BLOCK, HEADS, head_dim)
    keys = jnp.dot(node_feats, w_key, preferred_element_type=jnp.float32).astype(jnp.bfloat16).reshape(blocks, BLOCK, HEADS, head_dim)
    values = jnp.dot(node_feats, w_value, preferred_element_type=jnp.float32).astype(jnp.bfloat16).reshape(blocks, BLOCK, HEADS, head_dim)
    filler = jnp.zeros((1, BLOCK, HEADS, head_dim), jnp.bfloat16)
    key_pad = jnp.concatenate([filler, keys, filler], 0)
    value_pad = jnp.concatenate([filler, values, filler], 0)
    id_fill = jnp.full((1, BLOCK), -1, jnp.int32)
    id_pad = jnp.concatenate([id_fill, graph_ids.reshape(blocks, BLOCK).astype(jnp.int32), id_fill], 0)
    block_list = jnp.arange(GROUP_BLOCKS).astype(jnp.int32)
    slot_list = jnp.arange(CAP).astype(jnp.int32)

    def tile_scores(q_group, group, key_group):
        tiles = pair_tiles[group, key_group].astype(jnp.int32)
        count = pair_count[group, key_group].astype(jnp.int32)
        q_index = tiles // GROUP_BLOCKS
        k_index = tiles % GROUP_BLOCKS
        valid = slot_list < count
        k_tiles = keys[key_group * GROUP_BLOCKS + k_index]
        scores = jnp.einsum('cqhd,ckhd->chqk', q_group[q_index].astype(jnp.float32), k_tiles.astype(jnp.float32)) * scale
        select = (q_index[None, :] == block_list[:, None]) & valid[None, :]
        return (scores, q_index, k_index, valid, select)

    def one_group(group):
        group = group.astype(jnp.int32)
        start = (group * GROUP_BLOCKS).astype(jnp.int32)
        q_group = lax.dynamic_slice_in_dim(query, start, GROUP_BLOCKS, 0)
        near_k = lax.dynamic_slice_in_dim(key_pad, start, GROUP_BLOCKS + 2, 0)
        near_v = lax.dynamic_slice_in_dim(value_pad, start, GROUP_BLOCKS + 2, 0)
        near_ids = lax.dynamic_slice_in_dim(id_pad, start, GROUP_BLOCKS + 2, 0)
        q_ids = near_ids[1:GROUP_BLOCKS + 1]
        q_float = q_group.astype(jnp.float32)
        near_scores = [jnp.einsum('bqhd,bkhd->bhqk', q_float, near_k[t:t + GROUP_BLOCKS].astype(jnp.float32)) * scale for t in range(3)]
        near_masks = [q_ids[:, None, :, None] == near_ids[t:t + GROUP_BLOCKS][:, None, None, :] for t in range(3)]
        best = reduce(jnp.maximum, [lax.optimization_barrier(jnp.max(jnp.where(m, s, floor_score), -1)) for s, m in zip(near_scores, near_masks)])

        def seek(best, key_group):
            scores, q_index, k_index, valid, select = tile_scores(q_group, group, key_group)
            tile_best = lax.optimization_barrier(jnp.max(scores, -1))
            block_best = lax.optimization_barrier(jnp.max(jnp.where(select[:, :, None, None], tile_best[None], floor_score), 1))
            return (jnp.maximum(best, block_best), None)
        best, _ = lax.scan(seek, best, jnp.arange(GROUPS).astype(jnp.int32))
        total = jnp.zeros(best.shape, jnp.float32)
        accum = jnp.zeros(best.shape + (head_dim,), jnp.float32)
        for t in range(3):
            prob = jnp.where(near_masks[t], jnp.exp(near_scores[t] - best[..., None]), 0.0)
            total = total + lax.optimization_barrier(jnp.sum(prob, -1))
            accum = accum + jnp.einsum('bhqk,bkhd->bhqd', rounded(prob), near_v[t:t + GROUP_BLOCKS].astype(jnp.float32))

        def gather_terms(carry, key_group):
            total, accum = carry
            scores, q_index, k_index, valid, select = tile_scores(q_group, group, key_group)
            v_tiles = values[key_group * GROUP_BLOCKS + k_index].astype(jnp.float32)
            prob = jnp.where(valid[:, None, None, None], jnp.exp(scores - best[q_index][..., None]), 0.0)
            weights = select.astype(jnp.float32)
            total = total + jnp.einsum('gc,chq->ghq', weights, lax.optimization_barrier(jnp.sum(prob, -1)), precision=lax.Precision.HIGHEST)
            part = jnp.einsum('chqk,ckhd->chqd', rounded(prob), v_tiles)
            accum = accum + jnp.einsum('gc,chqd->ghqd', weights, part, precision=lax.Precision.HIGHEST)
            return ((total, accum), None)
        (total, accum), _ = lax.scan(gather_terms, (total, accum), jnp.arange(GROUPS).astype(jnp.int32))
        return (accum / total[..., None]).transpose(0, 2, 1, 3).astype(jnp.bfloat16)
    attended = lax.map(one_group, jnp.arange(GROUPS).astype(jnp.int32)).reshape(NODES, D)
    mixed = node_feats.astype(jnp.float32) + jnp.dot(attended, w_out, preferred_element_type=jnp.float32)
    normed = layer_norm(mixed, ln1_gain, ln1_bias).astype(jnp.bfloat16)
    hidden = jnp.maximum(jnp.dot(normed, w_up, preferred_element_type=jnp.float32) + b_up, 0.0).astype(jnp.bfloat16)
    second = normed.astype(jnp.float32) + jnp.dot(hidden, w_down, preferred_element_type=jnp.float32)
    return layer_norm(second, ln2_gain, ln2_bias).astype(jnp.float32)
```

```python
import jax
import jax.numpy as jnp
from jax import lax
from jax.experimental import pallas as pl
from jax.experimental.pallas import tpu as pltpu
from jax.sharding import Mesh
from jax.sharding import PartitionSpec as P

F32 = jnp.float32
BF16 = jnp.bfloat16

AXES = ("z", "ylo", "yhi", "x", "core")
SLAB = ("ylo", "yhi", "x", "core")
D = 512
FF = 1024
HEADS = 8
HEAD_DIM = 64
ROWS = 128
QUARTERS = 4
QROWS = ROWS // QUARTERS
MEMBERS = 16
SLAB_BLOCKS = 32
CAP = 8
STATE = 72
FIRST = 5
LATER = 8
FLOOR = -1e30


def holder(head, quarter):
    return (quarter // 2) * 16 + head * 2 + quarter % 2


def project_kernel(x_ref, wk_ref, wv_ref, wq_ref, kv_ref, q_ref):
    x = x_ref[...]
    keys = jnp.dot(x, wk_ref[...], preferred_element_type=F32)
    values = jnp.dot(x, wv_ref[...], preferred_element_type=F32)
    for head in range(HEADS):
        cols = slice(head * HEAD_DIM, (head + 1) * HEAD_DIM)
        tile = jnp.concatenate([keys[:, cols], values[:, cols]], axis=1).astype(BF16)
        for quarter in range(QUARTERS):
            kv_ref[holder(head, quarter)] = tile[quarter * QROWS : (quarter + 1) * QROWS]
    query = jnp.dot(x, wq_ref[...], preferred_element_type=F32).astype(BF16).astype(F32)
    query_t = (query.T * (1.0 / 8.0)).astype(BF16)
    for head in range(HEADS):
        for quarter in range(QUARTERS):
            q_ref[holder(head, quarter)] = query_t[head * HEAD_DIM : (head + 1) * HEAD_DIM]


def project(x, wk, wv, wq):
    return pl.pallas_call(
        project_kernel,
        out_shape=(
            jax.ShapeDtypeStruct((SLAB_BLOCKS, QROWS, 2 * HEAD_DIM), BF16),
            jax.ShapeDtypeStruct((SLAB_BLOCKS, HEAD_DIM, ROWS), BF16),
        ),
        compiler_params=pltpu.CompilerParams(vmem_limit_bytes=32 * 1024 * 1024),
        cost_estimate=pl.CostEstimate(
            flops=2 * ROWS * D * 3 * D, bytes_accessed=3 * D * D * 2 + 900000, transcendentals=0
        ),
        name="project",
    )(x, wk, wv, wq)


def attend_kernel(base_ref, start_ref, count_ref, list_ref, kv_ref, q_ref, kid_ref, qid_ref, out_ref):
    blocks = kv_ref.shape[0]
    base = base_ref[0]

    def padded_query(i):
        return jnp.concatenate([q_ref[i], jnp.zeros((HEAD_DIM, ROWS), BF16)], axis=0)

    def weighted(tile, prob):
        part = lax.dot_general(
            tile, prob.astype(BF16), (((0,), (0,)), ((), ())), preferred_element_type=F32
        )
        return part[HEAD_DIM:]

    def first(i):
        start = start_ref[i]
        count = count_ref[i]
        tiles = [kv_ref[jnp.clip(base + i + t - 1, 0, blocks - 1)] for t in range(3)]
        tiles += [kv_ref[list_ref[start + t]] for t in range(FIRST)]
        tile = jnp.concatenate(tiles, axis=0)
        scores = jnp.dot(tile, padded_query(i), preferred_element_type=F32)
        near = kid_ref[pl.ds(pl.multiple_of(i * QROWS, QROWS), 3 * QROWS), :] == qid_ref[i]
        parts = [jnp.where(near, scores[: 3 * QROWS], FLOOR)]
        for t in range(FIRST):
            rows = slice((3 + t) * QROWS, (4 + t) * QROWS)
            parts.append(jnp.where(t < count, scores[rows], FLOOR))
        scores = jnp.concatenate(parts, axis=0)
        top = jnp.max(scores, axis=0, keepdims=True)
        prob = jnp.exp(scores - top)
        total = jnp.sum(prob, axis=0, keepdims=True)
        out_ref[i, :HEAD_DIM] = weighted(tile, prob)
        out_ref[i, HEAD_DIM : HEAD_DIM + 1] = top
        out_ref[i, HEAD_DIM + 1 : HEAD_DIM + 2] = total

    def first_step(j, carry):
        for u in range(4):
            first(j * 4 + u)
        return carry

    lax.fori_loop(0, SLAB_BLOCKS // 4, first_step, 0)

    def rest(i, carry):
        start = start_ref[i] + FIRST
        count = count_ref[i] - FIRST

        @pl.when(count > 0)
        def _():
            query = padded_query(i)

            def chunk(c, state):
                top, total, accum = state
                at = start + c * LATER
                left = count - c * LATER
                tile = jnp.concatenate([kv_ref[list_ref[at + t]] for t in range(LATER)], axis=0)
                scores = jnp.dot(tile, query, preferred_element_type=F32)
                scores = jnp.concatenate(
                    [
                        jnp.where(t < left, scores[t * QROWS : (t + 1) * QROWS], FLOOR)
                        for t in range(LATER)
                    ],
                    axis=0,
                )
                new_top = jnp.maximum(top, jnp.max(scores, axis=0, keepdims=True))
                decay = jnp.exp(top - new_top)
                prob = jnp.exp(scores - new_top)
                total = total * decay + jnp.sum(prob, axis=0, keepdims=True)
                accum = accum * decay + weighted(tile, prob)
                return new_top, total, accum

            state = (
                out_ref[i, HEAD_DIM : HEAD_DIM + 1],
                out_ref[i, HEAD_DIM + 1 : HEAD_DIM + 2],
                out_ref[i, :HEAD_DIM],
            )
            top, total, accum = lax.fori_loop(0, (count + LATER - 1) // LATER, chunk, state)
            out_ref[i, :HEAD_DIM] = accum
            out_ref[i, HEAD_DIM : HEAD_DIM + 1] = top
            out_ref[i, HEAD_DIM + 1 : HEAD_DIM + 2] = total

        return carry

    lax.fori_loop(0, SLAB_BLOCKS, rest, 0)


def attend(base, start, count, pairs, kv_all, q_all, key_ids, query_ids):
    smem = pl.BlockSpec(memory_space=pltpu.SMEM)
    vmem = pl.BlockSpec(memory_space=pltpu.VMEM)
    return pl.pallas_call(
        attend_kernel,
        in_specs=[smem] * 4 + [vmem] * 4,
        out_specs=vmem,
        out_shape=jax.ShapeDtypeStruct((SLAB_BLOCKS, STATE, ROWS), F32),
        compiler_params=pltpu.CompilerParams(vmem_limit_bytes=40 * 1024 * 1024),
        cost_estimate=pl.CostEstimate(
            flops=SLAB_BLOCKS * 2 * 4 * 256 * 128 * 128,
            bytes_accessed=7 * 1024 * 1024,
            transcendentals=SLAB_BLOCKS * 2 * 256 * 128,
        ),
        name="attend",
    )(base, start, count, pairs, kv_all, q_all, key_ids, query_ids)


def layer_norm(value, gain, bias):
    mean = jnp.mean(value, -1, keepdims=True)
    centred = value - mean
    spread = jnp.mean(centred * centred, -1, keepdims=True)
    return centred * lax.rsqrt(spread + 1e-05) * gain + bias


def finish_kernel(
    part_ref, x_ref, w_out_ref, g1_ref, b1_ref, w_up_ref, b_up_ref, w_down_ref, g2_ref, b2_ref, out_ref
):
    columns = []
    for head in range(HEADS):
        held = [holder(head, quarter) for quarter in range(QUARTERS)]
        tops = [part_ref[s, HEAD_DIM : HEAD_DIM + 1] for s in held]
        totals = [part_ref[s, HEAD_DIM + 1 : HEAD_DIM + 2] for s in held]
        top = jnp.maximum(jnp.maximum(tops[0], tops[1]), jnp.maximum(tops[2], tops[3]))
        scales = [jnp.exp(t - top) for t in tops]
        total = sum(t * c for t, c in zip(totals, scales))
        accum = sum(part_ref[s, :HEAD_DIM] * c for s, c in zip(held, scales))
        columns.append((accum / total).astype(BF16))
    attended_t = jnp.concatenate(columns, axis=0)
    mixed = x_ref[...].astype(F32) + lax.dot_general(
        attended_t, w_out_ref[...], (((0,), (0,)), ((), ())), preferred_element_type=F32
    )
    normed = layer_norm(mixed, g1_ref[...], b1_ref[...]).astype(BF16)
    hidden = jnp.maximum(
        jnp.dot(normed, w_up_ref[...], preferred_element_type=F32) + b_up_ref[...], 0.0
    ).astype(BF16)
    second = normed.astype(F32) + jnp.dot(hidden, w_down_ref[...], preferred_element_type=F32)
    out_ref[...] = layer_norm(second, g2_ref[...], b2_ref[...])


def finish(parts, x, w_out, g1, b1, w_up, b_up, w_down, g2, b2):
    return pl.pallas_call(
        finish_kernel,
        out_shape=jax.ShapeDtypeStruct((ROWS, D), F32),
        compiler_params=pltpu.CompilerParams(vmem_limit_bytes=40 * 1024 * 1024),
        cost_estimate=pl.CostEstimate(
            flops=2 * ROWS * (D * D + 2 * D * FF), bytes_accessed=5 * 1024 * 1024, transcendentals=0
        ),
        name="finish",
    )(parts, x, w_out, g1[None], b1[None], w_up, b_up[None], w_down, g2[None], b2[None])


def pair_lists(pair_tiles, pair_count):
    tiles = pair_tiles[0]
    groups = tiles.shape[0]
    valid = jnp.arange(CAP, dtype=jnp.int32)[None, :] < pair_count[0][:, None]
    query_index = jnp.where(valid, tiles // MEMBERS, MEMBERS)
    key_block = jnp.arange(groups, dtype=jnp.int32)[:, None] * MEMBERS + tiles % MEMBERS
    held = jnp.stack([query_index.reshape(-1), key_block.reshape(-1)])
    held = lax.all_gather(held, "ylo")
    query_index, key_block = held[:, 0], held[:, 1]
    size = query_index.shape[1]
    slot = jnp.arange(size, dtype=jnp.int32)
    before = (query_index[:, None, :] < query_index[:, :, None]) | (
        (query_index[:, None, :] == query_index[:, :, None]) & (slot[None, None, :] < slot[None, :, None])
    )
    place = jnp.sum(before.astype(jnp.int32), axis=-1)
    pairs = jnp.sum(
        jnp.where(place[:, None, :] == slot[None, :, None], key_block[:, None, :], 0), axis=-1
    )
    pairs = jnp.concatenate([pairs.reshape(-1), jnp.zeros((16,), jnp.int32)])
    member = jnp.arange(MEMBERS, dtype=jnp.int32)
    start = jnp.sum((query_index[:, None, :] < member[None, :, None]).astype(jnp.int32), axis=-1)
    count = jnp.sum((query_index[:, None, :] == member[None, :, None]).astype(jnp.int32), axis=-1)
    start = start + size * jnp.arange(2, dtype=jnp.int32)[:, None]
    return start.reshape(-1), count.reshape(-1), pairs


def on_device(
    node_feats,
    graph_ids,
    pair_tiles,
    pair_count,
    w_query,
    w_key,
    w_value,
    w_out,
    ln1_gain,
    ln1_bias,
    w_up,
    b_up,
    w_down,
    ln2_gain,
    ln2_bias,
):
    kv_send, q_send = project(node_feats, w_key, w_value, w_query)
    kv_held = lax.all_to_all(kv_send, SLAB, split_axis=0, concat_axis=0, tiled=True)
    kv_all = lax.all_gather(kv_held, "z", axis=0, tiled=True)
    q_all = lax.all_to_all(q_send, SLAB, split_axis=0, concat_axis=0, tiled=True)

    start, count, pairs = pair_lists(pair_tiles, pair_count)
    first_block = lax.axis_index("z") * SLAB_BLOCKS
    quarter = lax.axis_index("ylo") * 2 + lax.axis_index("core")
    fill = jnp.full((ROWS,), -1, jnp.int32)
    ids = jnp.concatenate([fill, graph_ids, fill]).reshape(-1, ROWS)
    near_ids = lax.dynamic_slice_in_dim(ids, first_block, SLAB_BLOCKS + 2, 0)
    query_ids = near_ids[1 : SLAB_BLOCKS + 1, None, :]
    key_ids = lax.dynamic_slice_in_dim(near_ids, quarter * QROWS, QROWS, 1).reshape(-1, 1)

    base = first_block.reshape(1).astype(jnp.int32)
    parts = attend(base, start, count, pairs, kv_all, q_all, key_ids, query_ids)
    parts = lax.all_to_all(parts, SLAB, split_axis=0, concat_axis=0, tiled=True)
    return finish(
        parts, node_feats, w_out, ln1_gain, ln1_bias, w_up, b_up, w_down, ln2_gain, ln2_bias
    )


def solution(mesh):
    inner = Mesh(mesh.devices.reshape(-1, 2, 2, 4, 2), AXES)
    blk = ("z", "ylo")
    in_specs = (P(AXES, None), P(), P(blk, None, None), P(blk, None)) + (P(),) * 11
    return jax.shard_map(
        on_device, mesh=inner, in_specs=in_specs, out_specs=P(AXES, None), check_vma=False
    )
```

```python
import functools

import jax
import jax.numpy as jnp
from jax import lax
from jax.experimental import pallas as pl
from jax.experimental.pallas import tpu as pltpu
from jax.sharding import Mesh
from jax.sharding import PartitionSpec as P

F32 = jnp.float32
BF16 = jnp.bfloat16

AXES = ("z", "ylo", "yhi", "x", "core")
SLAB = ("ylo", "yhi", "x", "core")
D = 512
FF = 1024
HEADS = 8
HEAD_DIM = 64
ROWS = 128
PARTS = 4
HALF = ROWS // 2
QUARTER = ROWS // 4
NEAR = HALF + QUARTER
CHAINS = 2
MEMBERS = 16
SLAB_BLOCKS = 32
CAP = 8
STATE = 72
FIRST = 3
LATER = 4
FLOOR = -1e30


def holder(head, part):
    return (part // 2) * 16 + head * 2 + part % 2


def project_kernel(x_hbm, wk_hbm, wv_hbm, wq_hbm, kv_ref, q_ref, x_ref, wk_ref, wv_ref, wq_ref, sems):
    copies = [
        pltpu.make_async_copy(source, target, sems.at[i])
        for i, (source, target) in enumerate(
            ((x_hbm, x_ref), (wk_hbm, wk_ref), (wv_hbm, wv_ref), (wq_hbm, wq_ref))
        )
    ]
    for copy in copies:
        copy.start()
    copies[0].wait()
    copies[1].wait()
    x = x_ref[...]
    keys = jnp.dot(x, wk_ref[...], preferred_element_type=F32)
    copies[2].wait()
    values = jnp.dot(x, wv_ref[...], preferred_element_type=F32)
    for head in range(HEADS):
        cols = slice(head * HEAD_DIM, (head + 1) * HEAD_DIM)
        tile = jnp.concatenate([keys[:, cols], values[:, cols]], axis=1).astype(BF16)
        for part in range(PARTS):
            half = part // 2
            kv_ref[holder(head, part)] = tile[half * HALF : (half + 1) * HALF]
    copies[3].wait()
    query = jnp.dot(x, wq_ref[...], preferred_element_type=F32).astype(BF16).astype(F32)
    query_t = (query.T * (1.0 / 8.0)).astype(BF16)
    for head in range(HEADS):
        for part in range(PARTS):
            q_ref[holder(head, part)] = query_t[head * HEAD_DIM : (head + 1) * HEAD_DIM]


def project(x, wk, wv, wq):
    hbm = pl.BlockSpec(memory_space=pltpu.HBM)
    return pl.pallas_call(
        project_kernel,
        in_specs=[hbm] * 4,
        out_shape=(
            jax.ShapeDtypeStruct((SLAB_BLOCKS, HALF, 2 * HEAD_DIM), BF16),
            jax.ShapeDtypeStruct((SLAB_BLOCKS, HEAD_DIM, ROWS), BF16),
        ),
        scratch_shapes=[
            pltpu.VMEM((ROWS, D), BF16),
            pltpu.VMEM((D, D), BF16),
            pltpu.VMEM((D, D), BF16),
            pltpu.VMEM((D, D), BF16),
            pltpu.SemaphoreType.DMA((4,)),
        ],
        compiler_params=pltpu.CompilerParams(vmem_limit_bytes=60 * 1024 * 1024),
        cost_estimate=pl.CostEstimate(
            flops=2 * ROWS * D * 3 * D, bytes_accessed=3 * D * D * 2 + 900000, transcendentals=0
        ),
        name="project",
    )(x, wk, wv, wq)


def attend_kernel(pieces, core_ref, start_ref, count_ref, list_ref, q_ref, kid_ref, qid_ref, *rest_refs):
    sources = rest_refs[:pieces]
    out_ref, kv_ref, sems = rest_refs[pieces:]
    core = core_ref[0]
    copies = []
    at = 0
    for n, source in enumerate(sources):
        size = source.shape[0]
        copies.append(pltpu.make_async_copy(source, kv_ref.at[pl.ds(at, size)], sems.at[n]))
        at += size
    for copy in copies:
        copy.start()
    for copy in copies:
        copy.wait()

    def padded_query(i):
        return jnp.concatenate([q_ref[i], jnp.zeros((HEAD_DIM, ROWS), BF16)], axis=0)

    def weighted(tile, prob):
        part = lax.dot_general(
            tile, prob.astype(BF16), (((0,), (0,)), ((), ())), preferred_element_type=F32
        )
        return part[HEAD_DIM:]

    def first(i):
        start = start_ref[i]
        count = count_ref[i]
        before = jnp.where(i == 0, 2 * SLAB_BLOCKS - 1, i - 1)
        beside = jnp.where(core == 0, before, i + 1)
        tiles = [kv_ref[beside], kv_ref[i, pl.ds(pl.multiple_of(core * QUARTER, QUARTER), QUARTER)]]
        tiles += [kv_ref[list_ref[start + t]] for t in range(FIRST)]
        tile = jnp.concatenate(tiles, axis=0)
        scores = jnp.dot(tile, padded_query(i), preferred_element_type=F32)
        near = kid_ref[pl.ds(pl.multiple_of(i * NEAR, 8), NEAR), :] == qid_ref[i]
        parts = [jnp.where(near, scores[:NEAR], FLOOR)]
        for t in range(FIRST):
            rows = slice(NEAR + t * HALF, NEAR + (t + 1) * HALF)
            parts.append(jnp.where(t < count, scores[rows], FLOOR))
        scores = jnp.concatenate(parts, axis=0)
        top = jnp.max(scores, axis=0, keepdims=True)
        prob = jnp.exp(scores - top)
        total = jnp.sum(prob, axis=0, keepdims=True)
        out_ref[i, :HEAD_DIM] = weighted(tile, prob)
        out_ref[i, HEAD_DIM : HEAD_DIM + 1] = top
        out_ref[i, HEAD_DIM + 1 : HEAD_DIM + 2] = total

    def first_step(j, carry):
        for u in range(4):
            first(j * 4 + u)
        return carry

    lax.fori_loop(0, SLAB_BLOCKS // 4, first_step, 0)

    def rest(i, carry):
        start = start_ref[i] + FIRST
        count = count_ref[i] - FIRST

        @pl.when(count > 0)
        def _():
            query = padded_query(i)

            def chunk(c, state):
                top, total, accum = state
                at = start + c * LATER
                left = count - c * LATER
                tile = jnp.concatenate([kv_ref[list_ref[at + t]] for t in range(LATER)], axis=0)
                scores = jnp.dot(tile, query, preferred_element_type=F32)
                scores = jnp.concatenate(
                    [
                        jnp.where(t < left, scores[t * HALF : (t + 1) * HALF], FLOOR)
                        for t in range(LATER)
                    ],
                    axis=0,
                )
                new_top = jnp.maximum(top, jnp.max(scores, axis=0, keepdims=True))
                decay = jnp.exp(top - new_top)
                prob = jnp.exp(scores - new_top)
                total = total * decay + jnp.sum(prob, axis=0, keepdims=True)
                accum = accum * decay + weighted(tile, prob)
                return new_top, total, accum

            state = (
                out_ref[i, HEAD_DIM : HEAD_DIM + 1],
                out_ref[i, HEAD_DIM + 1 : HEAD_DIM + 2],
                out_ref[i, :HEAD_DIM],
            )
            top, total, accum = lax.fori_loop(0, (count + LATER - 1) // LATER, chunk, state)
            out_ref[i, :HEAD_DIM] = accum
            out_ref[i, HEAD_DIM : HEAD_DIM + 1] = top
            out_ref[i, HEAD_DIM + 1 : HEAD_DIM + 2] = total

        return carry

    lax.fori_loop(0, SLAB_BLOCKS, rest, 0)


def attend(core, start, count, pairs, q_all, key_ids, query_ids, held):
    smem = pl.BlockSpec(memory_space=pltpu.SMEM)
    vmem = pl.BlockSpec(memory_space=pltpu.VMEM)
    anywhere = pl.BlockSpec(memory_space=pl.ANY)
    slots = sum(piece.shape[0] for piece in held)
    return pl.pallas_call(
        functools.partial(attend_kernel, len(held)),
        in_specs=[smem] * 4 + [vmem] * 3 + [anywhere] * len(held),
        out_specs=vmem,
        out_shape=jax.ShapeDtypeStruct((SLAB_BLOCKS, STATE, ROWS), F32),
        scratch_shapes=[
            pltpu.VMEM((slots, HALF, 2 * HEAD_DIM), BF16),
            pltpu.SemaphoreType.DMA((len(held),)),
        ],
        compiler_params=pltpu.CompilerParams(vmem_limit_bytes=40 * 1024 * 1024),
        cost_estimate=pl.CostEstimate(
            flops=SLAB_BLOCKS * 2 * 4 * 256 * 128 * 128,
            bytes_accessed=7 * 1024 * 1024,
            transcendentals=SLAB_BLOCKS * 2 * 256 * 128,
        ),
        name="attend",
    )(core, start, count, pairs, q_all, key_ids, query_ids, *held)


def layer_norm(value, gain, bias):
    mean = jnp.mean(value, -1, keepdims=True)
    centred = value - mean
    spread = jnp.mean(centred * centred, -1, keepdims=True)
    return centred * lax.rsqrt(spread + 1e-05) * gain + bias


def finish_kernel(
    part_ref, x_ref, w_out_ref, g1_ref, b1_ref, w_up_ref, b_up_ref, w_down_ref, g2_ref, b2_ref, out_ref
):
    columns = []
    for head in range(HEADS):
        held = [holder(head, part) for part in range(PARTS)]
        tops = [part_ref[s, HEAD_DIM : HEAD_DIM + 1] for s in held]
        totals = [part_ref[s, HEAD_DIM + 1 : HEAD_DIM + 2] for s in held]
        top = jnp.maximum(jnp.maximum(tops[0], tops[1]), jnp.maximum(tops[2], tops[3]))
        scales = [jnp.exp(t - top) for t in tops]
        total = sum(t * c for t, c in zip(totals, scales))
        accum = sum(part_ref[s, :HEAD_DIM] * c for s, c in zip(held, scales))
        columns.append((accum / total).astype(BF16))
    attended_t = jnp.concatenate(columns, axis=0)
    mixed = x_ref[...].astype(F32) + lax.dot_general(
        attended_t, w_out_ref[...], (((0,), (0,)), ((), ())), preferred_element_type=F32
    )
    normed = layer_norm(mixed, g1_ref[...], b1_ref[...]).astype(BF16)
    hidden = jnp.maximum(
        jnp.dot(normed, w_up_ref[...], preferred_element_type=F32) + b_up_ref[...], 0.0
    ).astype(BF16)
    second = normed.astype(F32) + jnp.dot(hidden, w_down_ref[...], preferred_element_type=F32)
    out_ref[...] = layer_norm(second, g2_ref[...], b2_ref[...])


def finish(parts, x, w_out, g1, b1, w_up, b_up, w_down, g2, b2):
    return pl.pallas_call(
        finish_kernel,
        out_shape=jax.ShapeDtypeStruct((ROWS, D), F32),
        compiler_params=pltpu.CompilerParams(vmem_limit_bytes=40 * 1024 * 1024),
        cost_estimate=pl.CostEstimate(
            flops=2 * ROWS * (D * D + 2 * D * FF), bytes_accessed=5 * 1024 * 1024, transcendentals=0
        ),
        name="finish",
    )(parts, x, w_out, g1[None], b1[None], w_up, b_up[None], w_down, g2[None], b2[None])


def pair_lists(pair_tiles, pair_count, z, ylo, core):
    tiles = pair_tiles[0]
    groups = tiles.shape[0]
    valid = jnp.arange(CAP, dtype=jnp.int32)[None, :] < pair_count[0][:, None]
    mine = jnp.where(valid, tiles, MEMBERS * MEMBERS).reshape(1, -1)
    other = lax.ppermute(mine, "ylo", [(0, 1), (1, 0)])
    held = jnp.where(ylo == 0, jnp.concatenate([mine, other]), jnp.concatenate([other, mine]))
    size = held.shape[1]
    slot = jnp.arange(size, dtype=jnp.int32)
    key_group = slot // CAP
    key_z = key_group // 2
    steps = groups // 2
    distance = jnp.where(core == 0, z - key_z, key_z - z) % steps
    ours = jnp.where(core == 0, (distance >= 1) & (distance <= steps // 2), distance < steps // 2)
    query_index = jnp.where(ours[None, :], held // MEMBERS, MEMBERS)
    place_of = (distance * SLAB_BLOCKS + key_group % 2 * MEMBERS)[None, :] + held % MEMBERS
    before = (query_index[:, None, :] < query_index[:, :, None]) | (
        (query_index[:, None, :] == query_index[:, :, None]) & (slot[None, None, :] < slot[None, :, None])
    )
    place = jnp.sum(before.astype(jnp.int32), axis=-1)
    place_of = jnp.where(query_index < MEMBERS, place_of, 0)
    pairs = jnp.sum(
        jnp.where(place[:, None, :] == slot[None, :, None], place_of[:, None, :], 0), axis=-1
    )
    pairs = jnp.concatenate([pairs.reshape(-1), jnp.zeros((16,), jnp.int32)])
    member = jnp.arange(MEMBERS, dtype=jnp.int32)
    start = jnp.sum((query_index[:, None, :] < member[None, :, None]).astype(jnp.int32), axis=-1)
    count = jnp.sum((query_index[:, None, :] == member[None, :, None]).astype(jnp.int32), axis=-1)
    start = start + size * jnp.arange(2, dtype=jnp.int32)[:, None]
    return start.reshape(-1), count.reshape(-1), pairs


def ring(kv_own):
    size = lax.axis_size("z")
    up = [(2 * z, 2 * ((z + 1) % size)) for z in range(size)]
    down = [(2 * z + 1, 2 * ((z - 1) % size) + 1) for z in range(size)]
    width = SLAB_BLOCKS // CHAINS
    held = [kv_own[c * width : (c + 1) * width] for c in range(CHAINS)]
    slots = [kv_own]
    for step in range(size // 2):
        held = [lax.ppermute(piece, ("z", "core"), up + down) for piece in held]
        slots += held
    return slots


def on_device(
    node_feats,
    graph_ids,
    pair_tiles,
    pair_count,
    w_query,
    w_key,
    w_value,
    w_out,
    ln1_gain,
    ln1_bias,
    w_up,
    b_up,
    w_down,
    ln2_gain,
    ln2_bias,
):
    z, ylo, core = lax.axis_index("z"), lax.axis_index("ylo"), lax.axis_index("core")
    kv_send, q_send = project(node_feats, w_key, w_value, w_query)
    kv_own = lax.all_to_all(kv_send, SLAB, split_axis=0, concat_axis=0, tiled=True)
    held = ring(kv_own)
    q_all = lax.all_to_all(q_send, SLAB, split_axis=0, concat_axis=0, tiled=True)

    start, count, pairs = pair_lists(pair_tiles, pair_count, z, ylo, core)
    fill = jnp.full((ROWS,), -1, jnp.int32)
    ids = jnp.concatenate([fill, graph_ids, fill]).reshape(-1, ROWS)
    near_ids = lax.dynamic_slice_in_dim(ids, z * SLAB_BLOCKS, SLAB_BLOCKS + 2, 0)
    query_ids = near_ids[1 : SLAB_BLOCKS + 1]
    beside = jnp.where(core == 0, near_ids[:SLAB_BLOCKS], near_ids[2:])
    key_ids = jnp.concatenate(
        [
            lax.dynamic_slice_in_dim(beside, ylo * HALF, HALF, 1),
            lax.dynamic_slice_in_dim(query_ids, ylo * HALF + core * QUARTER, QUARTER, 1),
        ],
        axis=1,
    ).reshape(-1, 1)
    parts = attend(
        core.reshape(1).astype(jnp.int32), start, count, pairs, q_all, key_ids, query_ids[:, None, :], held
    )
    parts = lax.all_to_all(parts, SLAB, split_axis=0, concat_axis=0, tiled=True)
    return finish(
        parts, node_feats, w_out, ln1_gain, ln1_bias, w_up, b_up, w_down, ln2_gain, ln2_bias
    )


def solution(mesh):
    inner = Mesh(mesh.devices.reshape(-1, 2, 2, 4, 2), AXES)
    blk = ("z", "ylo")
    in_specs = (P(AXES, None), P(), P(blk, None, None), P(blk, None)) + (P(),) * 11
    return jax.shard_map(
        on_device, mesh=inner, in_specs=in_specs, out_specs=P(AXES, None), check_vma=False
    )
```

```python
import jax
import jax.numpy as jnp
from jax import lax
from jax.experimental import pallas as pl
from jax.experimental.pallas import tpu as pltpu
from jax.sharding import Mesh
from jax.sharding import PartitionSpec as P

F32 = jnp.float32
BF16 = jnp.bfloat16

AXES = ("z", "ylo", "yhi", "x", "core")
SLAB = ("ylo", "yhi", "x", "core")
D = 512
FF = 1024
HEADS = 8
HEAD_DIM = 64
COUPLES = HEADS // 2
ROWS = 128
MEMBERS = 16
SLAB_BLOCKS = 32
CAP = 8
TILE_ROWS = 16
TILE_COLS = 128
COL_TILES = D // TILE_COLS
EARLY = 6
LATE = 10
MIB = 1024 * 1024
FLOOR = -1e30

SMEM = pl.BlockSpec(memory_space=pltpu.SMEM)
VMEM = pl.BlockSpec(memory_space=pltpu.VMEM)


def absorb(state, keys, values, query_ref, mask):
    new = []
    for couple in range(COUPLES):
        top, total, accum = state[couple]
        cols = slice(couple * 2 * HEAD_DIM, (couple + 1) * 2 * HEAD_DIM)
        scores = jnp.dot(keys[:, cols], query_ref[couple], preferred_element_type=F32)
        if mask is not None:
            scores = jnp.where(mask, scores, FLOOR)
        new_top = jnp.maximum(top, jnp.max(scores, axis=0, keepdims=True))
        decay = jnp.exp(top - new_top)
        prob = jnp.exp(scores - new_top)
        total = total * decay + jnp.sum(prob, axis=0, keepdims=True)
        part = lax.dot_general(
            values[:, cols],
            prob.astype(BF16),
            (((0,), (0,)), ((), ())),
            preferred_element_type=F32,
        )
        accum = jnp.concatenate(
            [
                accum[:HEAD_DIM] * decay[:, :ROWS] + part[:HEAD_DIM, :ROWS],
                accum[HEAD_DIM:] * decay[:, ROWS:] + part[HEAD_DIM:, ROWS:],
            ],
            axis=0,
        )
        new.append((new_top, total, accum))
    return new


def read_state(top_ref, total_ref, accum_ref):
    return [
        (
            top_ref[c : c + 1, :],
            total_ref[c : c + 1, :],
            accum_ref[c * 2 * HEAD_DIM : (c + 1) * 2 * HEAD_DIM, :],
        )
        for c in range(COUPLES)
    ]


def write_state(state, top_ref, total_ref, accum_ref):
    for c, (top, total, accum) in enumerate(state):
        top_ref[c : c + 1, :] = top
        total_ref[c : c + 1, :] = total
        accum_ref[c * 2 * HEAD_DIM : (c + 1) * 2 * HEAD_DIM, :] = accum


def project(x, weight_ref):
    return jnp.dot(x, weight_ref[...], preferred_element_type=F32).astype(BF16)


STATE_SHAPES = (
    jax.ShapeDtypeStruct((COUPLES, 2 * ROWS), F32),
    jax.ShapeDtypeStruct((COUPLES, 2 * ROWS), F32),
    jax.ShapeDtypeStruct((D, ROWS), F32),
)


def near_kernel(
    before_ref, x_ref, after_ref, wq_ref, wk_ref, wv_ref, kid_ref, qid_ref, query_ref, top_ref, total_ref, accum_ref
):
    x = x_ref[...]
    query = jnp.dot(x, wq_ref[...], preferred_element_type=F32).astype(BF16).astype(F32)
    query_t = (query.T * (1.0 / 8.0)).astype(BF16)
    zero = jnp.zeros((HEAD_DIM, ROWS), BF16)
    for couple in range(COUPLES):
        at = couple * 2 * HEAD_DIM
        first = query_t[at : at + HEAD_DIM]
        second = query_t[at + HEAD_DIM : at + 2 * HEAD_DIM]
        query_ref[couple] = jnp.concatenate(
            [jnp.concatenate([first, zero], axis=1), jnp.concatenate([zero, second], axis=1)], axis=0
        )
    state = [
        (
            jnp.full((1, 2 * ROWS), FLOOR, F32),
            jnp.zeros((1, 2 * ROWS), F32),
            jnp.zeros((2 * HEAD_DIM, ROWS), F32),
        )
    ] * COUPLES
    sources = jnp.concatenate([before_ref[...], x, after_ref[...]], axis=0)
    mask = kid_ref[...] == qid_ref[...]
    state = absorb(state, project(sources, wk_ref), project(sources, wv_ref), query_ref, mask)
    write_state(state, top_ref, total_ref, accum_ref)


def near(before, x, after, wq, wk, wv, key_ids, query_ids):
    return pl.pallas_call(
        near_kernel,
        out_shape=(jax.ShapeDtypeStruct((COUPLES, 2 * HEAD_DIM, 2 * ROWS), BF16),) + STATE_SHAPES,
        compiler_params=pltpu.CompilerParams(vmem_limit_bytes=32 * MIB),
        cost_estimate=pl.CostEstimate(flops=10**9, bytes_accessed=3 * MIB, transcendentals=400000),
        name="near",
    )(before, x, after, wq, wk, wv, key_ids, query_ids)


def select_kernel(width, at_ref, list_ref, even_ref, odd_ref, out_ref):
    def one(dest, carry):
        at = at_ref[dest]
        for slot in range(width):
            block = list_ref[at + slot]
            place = (block // SLAB_BLOCKS) * MEMBERS + block % MEMBERS
            tile = even_ref[place]
            if odd_ref is not None:
                is_odd = (block // MEMBERS) % 2 == 1
                tile = jnp.where(is_odd, odd_ref[place], tile)
            out_ref[dest, slot] = tile
        return carry

    lax.fori_loop(0, SLAB_BLOCKS, one, 0)


def select(width, at, pairs, even, odd=None):
    if odd is None:
        kernel = lambda a, b, c, out: select_kernel(width, a, b, c, None, out)
        tiles = (even,)
    else:
        kernel = lambda a, b, c, d, out: select_kernel(width, a, b, c, d, out)
        tiles = (even, odd)
    return pl.pallas_call(
        kernel,
        in_specs=[SMEM] * 2 + [VMEM] * len(tiles),
        out_specs=VMEM,
        out_shape=jax.ShapeDtypeStruct((SLAB_BLOCKS, width, TILE_ROWS, TILE_COLS), BF16),
        compiler_params=pltpu.CompilerParams(vmem_limit_bytes=32 * MIB),
        cost_estimate=pl.CostEstimate(flops=0, bytes_accessed=4 * MIB, transcendentals=0),
        name="select",
    )(at, pairs, *tiles)


def far_kernel(
    count_ref, held_ref, query_ref, wk_ref, wv_ref, top_in, total_in, accum_in, top_ref, total_ref, accum_ref
):
    count = count_ref[0]
    top_ref[...] = top_in[...]
    total_ref[...] = total_in[...]
    accum_ref[...] = accum_in[...]

    def block(slot):
        rows = []
        for r in range(ROWS // TILE_ROWS):
            tiles = [held_ref[r * COL_TILES + c, slot] for c in range(COL_TILES)]
            rows.append(jnp.concatenate(tiles, axis=1))
        return jnp.concatenate(rows, axis=0)

    def step(i, carry):
        x = jnp.concatenate([block(2 * i), block(2 * i + 1)], axis=0)
        last = jnp.where(2 * i + 1 < count, 2 * ROWS, ROWS)
        mask = lax.broadcasted_iota(jnp.int32, (2 * ROWS, 2 * ROWS), 0) < last
        state = read_state(top_ref, total_ref, accum_ref)
        state = absorb(state, project(x, wk_ref), project(x, wv_ref), query_ref, mask)
        write_state(state, top_ref, total_ref, accum_ref)
        return carry

    lax.fori_loop(0, (count + 1) // 2, step, 0)


def far(count, held, query, wk, wv, state):
    width = held.shape[1]
    return pl.pallas_call(
        far_kernel,
        in_specs=[SMEM] + [VMEM] * 7,
        out_specs=(VMEM,) * 3,
        out_shape=STATE_SHAPES,
        compiler_params=pltpu.CompilerParams(vmem_limit_bytes=32 * MIB),
        cost_estimate=pl.CostEstimate(
            flops=width * 2 * 10**8, bytes_accessed=3 * MIB, transcendentals=width * 140000
        ),
        name="far",
    )(count, held, query, wk, wv, *state)


def layer_norm(value, gain, bias):
    mean = jnp.mean(value, -1, keepdims=True)
    centred = value - mean
    spread = jnp.mean(centred * centred, -1, keepdims=True)
    return centred * lax.rsqrt(spread + 1e-05) * gain + bias


def finish_kernel(
    total_ref, accum_ref, x_ref, w_out_ref, g1_ref, b1_ref, w_up_ref, b_up_ref, w_down_ref, g2_ref, b2_ref, out_ref
):
    columns = []
    for head in range(HEADS):
        lanes = slice(head % 2 * ROWS, (head % 2 + 1) * ROWS)
        total = total_ref[head // 2 : head // 2 + 1, lanes]
        accum = accum_ref[head * HEAD_DIM : (head + 1) * HEAD_DIM, :]
        columns.append((accum / total).astype(BF16))
    attended_t = jnp.concatenate(columns, axis=0)
    mixed = x_ref[...].astype(F32) + lax.dot_general(
        attended_t, w_out_ref[...], (((0,), (0,)), ((), ())), preferred_element_type=F32
    )
    normed = layer_norm(mixed, g1_ref[...], b1_ref[...]).astype(BF16)
    hidden = jnp.maximum(
        jnp.dot(normed, w_up_ref[...], preferred_element_type=F32) + b_up_ref[...], 0.0
    ).astype(BF16)
    second = normed.astype(F32) + jnp.dot(hidden, w_down_ref[...], preferred_element_type=F32)
    out_ref[...] = layer_norm(second, g2_ref[...], b2_ref[...])


def finish(total, accum, x, w_out, g1, b1, w_up, b_up, w_down, g2, b2):
    return pl.pallas_call(
        finish_kernel,
        out_shape=jax.ShapeDtypeStruct((ROWS, D), F32),
        compiler_params=pltpu.CompilerParams(vmem_limit_bytes=40 * MIB),
        cost_estimate=pl.CostEstimate(
            flops=2 * ROWS * (D * D + 2 * D * FF), bytes_accessed=4 * MIB, transcendentals=0
        ),
        name="finish",
    )(total, accum, x, w_out, g1[None], b1[None], w_up, b_up[None], w_down, g2[None], b2[None])


def pair_lists(pair_tiles, pair_count, ylo):
    tiles = pair_tiles[0]
    valid = jnp.arange(CAP, dtype=jnp.int32)[None, :] < pair_count[0][:, None]
    mine = jnp.where(valid, tiles, MEMBERS * MEMBERS).reshape(1, -1)
    other = lax.ppermute(mine, "ylo", [(0, 1), (1, 0)])
    held = jnp.where(ylo == 0, jnp.concatenate([mine, other]), jnp.concatenate([other, mine]))
    size = held.shape[1]
    slot = jnp.arange(size, dtype=jnp.int32)
    key_group = slot // CAP
    order = held // MEMBERS * 2 + (key_group % 2)[None, :]
    key_block = (key_group * MEMBERS)[None, :] + held % MEMBERS
    ahead = (order[:, None, :] < order[:, :, None]) | (
        (order[:, None, :] == order[:, :, None]) & (slot[None, None, :] < slot[None, :, None])
    )
    place = jnp.sum(ahead.astype(jnp.int32), axis=-1)
    pairs = jnp.sum(jnp.where(place[:, None, :] == slot[None, :, None], key_block[:, None, :], 0), axis=-1)
    pairs = jnp.concatenate([pairs.reshape(-1), jnp.zeros((16,), jnp.int32)])
    member = 2 * jnp.arange(MEMBERS, dtype=jnp.int32)[None, :, None]
    order = order[:, None, :]
    start = jnp.sum((order < member).astype(jnp.int32), axis=-1)
    even = jnp.sum((order == member).astype(jnp.int32), axis=-1)
    count = even + jnp.sum((order == member + 1).astype(jnp.int32), axis=-1)
    start = start + size * jnp.arange(2, dtype=jnp.int32)[:, None]
    return start.reshape(-1), even.reshape(-1), count.reshape(-1), pairs


def shift(x, step, size):
    pairs = [(i, i + step) for i in range(size) if 0 <= i + step < size]
    return lax.ppermute(x, AXES, pairs)


def on_device(
    node_feats,
    graph_ids,
    pair_tiles,
    pair_count,
    w_query,
    w_key,
    w_value,
    w_out,
    ln1_gain,
    ln1_bias,
    w_up,
    b_up,
    w_down,
    ln2_gain,
    ln2_bias,
):
    z, ylo = lax.axis_index("z"), lax.axis_index("ylo")
    own = lax.axis_index(SLAB)
    devices = lax.axis_size(AXES)

    def exchange(value):
        return lax.all_to_all(value, SLAB, split_axis=0, concat_axis=0, tiled=True)

    tiles = node_feats.reshape(ROWS // TILE_ROWS, TILE_ROWS, COL_TILES, TILE_COLS)
    tiles = exchange(tiles.transpose(0, 2, 1, 3).reshape(SLAB_BLOCKS, TILE_ROWS, TILE_COLS))
    even = lax.all_gather(tiles[:MEMBERS], "z", axis=0, tiled=True)
    odd = lax.all_gather(tiles[MEMBERS:], "z", axis=0, tiled=True)

    start, even_count, count, pairs = pair_lists(pair_tiles, pair_count, ylo)
    early_count = jnp.minimum(even_count, EARLY)
    left = count - early_count

    def mine(value):
        return lax.dynamic_slice_in_dim(value, own, 1, 0)

    fill = jnp.full((ROWS,), -1, jnp.int32)
    ids = jnp.concatenate([fill, graph_ids, fill])
    key_ids = lax.dynamic_slice_in_dim(ids, (z * SLAB_BLOCKS + own) * ROWS, 3 * ROWS, 0)
    query_ids = jnp.tile(key_ids[ROWS : 2 * ROWS], 2)[None, :]
    before = shift(node_feats, 1, devices)
    after = shift(node_feats, -1, devices)
    query, *state = near(
        before, node_feats, after, w_query, w_key, w_value, key_ids[:, None], query_ids
    )

    held = exchange(select(EARLY, start, pairs, even))
    state = far(mine(early_count), held, query, w_key, w_value, state)

    def late(at, state):
        ahead = start + early_count + jnp.minimum(at, left)
        held = exchange(select(LATE, ahead, pairs, even, odd))
        return tuple(far(jnp.clip(mine(left) - at, 0, LATE), held, query, w_key, w_value, state))

    state = late(jnp.int32(0), state)
    most = jnp.max(left)
    _, state = lax.while_loop(
        lambda carry: carry[0] < most,
        lambda carry: (carry[0] + LATE, late(*carry)),
        (jnp.int32(LATE), state),
    )
    return finish(
        state[1], state[2], node_feats, w_out, ln1_gain, ln1_bias, w_up, b_up, w_down, ln2_gain, ln2_bias
    )


def solution(mesh):
    inner = Mesh(mesh.devices.reshape(-1, 2, 2, 4, 2), AXES)
    blk = ("z", "ylo")
    in_specs = (P(AXES, None), P(), P(blk, None, None), P(blk, None)) + (P(),) * 11
    return jax.shard_map(
        on_device, mesh=inner, in_specs=in_specs, out_specs=P(AXES, None), check_vma=False
    )
```

```python
import jax
import jax.numpy as jnp
from jax import lax
from jax.experimental import pallas as pl
from jax.experimental.pallas import tpu as pltpu
from jax.sharding import Mesh
from jax.sharding import PartitionSpec as P

F32 = jnp.float32
BF16 = jnp.bfloat16

AXES = ("z", "ylo", "yhi", "x", "core")
SLAB = ("ylo", "yhi", "x", "core")
D = 512
FF = 1024
HEADS = 8
HEAD_DIM = 64
COUPLES = HEADS // 2
ROWS = 128
MEMBERS = 16
SLAB_BLOCKS = 32
CAP = 8
TILE_ROWS = 16
TILE_COLS = 128
COL_TILES = D // TILE_COLS
SLOTS = 16
MIB = 1024 * 1024
FLOOR = -1e30

SMEM = pl.BlockSpec(memory_space=pltpu.SMEM)
VMEM = pl.BlockSpec(memory_space=pltpu.VMEM)


def absorb(state, keys, values, query_ref, mask):
    new = []
    for couple in range(COUPLES):
        top, total, accum = state[couple]
        cols = slice(couple * 2 * HEAD_DIM, (couple + 1) * 2 * HEAD_DIM)
        scores = jnp.dot(keys[:, cols], query_ref[couple], preferred_element_type=F32)
        if mask is not None:
            scores = jnp.where(mask, scores, FLOOR)
        new_top = jnp.maximum(top, jnp.max(scores, axis=0, keepdims=True))
        decay = jnp.exp(top - new_top)
        prob = jnp.exp(scores - new_top)
        total = total * decay + jnp.sum(prob, axis=0, keepdims=True)
        part = lax.dot_general(
            values[:, cols],
            prob.astype(BF16),
            (((0,), (0,)), ((), ())),
            preferred_element_type=F32,
        )
        accum = jnp.concatenate(
            [
                accum[:HEAD_DIM] * decay[:, :ROWS] + part[:HEAD_DIM, :ROWS],
                accum[HEAD_DIM:] * decay[:, ROWS:] + part[HEAD_DIM:, ROWS:],
            ],
            axis=0,
        )
        new.append((new_top, total, accum))
    return new


def read_state(top_ref, total_ref, accum_ref):
    return [
        (
            top_ref[c : c + 1, :],
            total_ref[c : c + 1, :],
            accum_ref[c * 2 * HEAD_DIM : (c + 1) * 2 * HEAD_DIM, :],
        )
        for c in range(COUPLES)
    ]


def write_state(state, top_ref, total_ref, accum_ref):
    for c, (top, total, accum) in enumerate(state):
        top_ref[c : c + 1, :] = top
        total_ref[c : c + 1, :] = total
        accum_ref[c * 2 * HEAD_DIM : (c + 1) * 2 * HEAD_DIM, :] = accum


def project(x, weight_ref):
    return jnp.dot(x, weight_ref[...], preferred_element_type=F32).astype(BF16)


STATE_SHAPES = (
    jax.ShapeDtypeStruct((COUPLES, 2 * ROWS), F32),
    jax.ShapeDtypeStruct((COUPLES, 2 * ROWS), F32),
    jax.ShapeDtypeStruct((D, ROWS), F32),
)


def near_kernel(
    before_ref, x_ref, after_ref, wq_ref, wk_ref, wv_ref, kid_ref, qid_ref, query_ref, top_ref, total_ref, accum_ref
):
    x = x_ref[...]
    query = jnp.dot(x, wq_ref[...], preferred_element_type=F32).astype(BF16).astype(F32)
    query_t = (query.T * (1.0 / 8.0)).astype(BF16)
    zero = jnp.zeros((HEAD_DIM, ROWS), BF16)
    for couple in range(COUPLES):
        at = couple * 2 * HEAD_DIM
        first = query_t[at : at + HEAD_DIM]
        second = query_t[at + HEAD_DIM : at + 2 * HEAD_DIM]
        query_ref[couple] = jnp.concatenate(
            [jnp.concatenate([first, zero], axis=1), jnp.concatenate([zero, second], axis=1)], axis=0
        )
    state = [
        (
            jnp.full((1, 2 * ROWS), FLOOR, F32),
            jnp.zeros((1, 2 * ROWS), F32),
            jnp.zeros((2 * HEAD_DIM, ROWS), F32),
        )
    ] * COUPLES
    sources = jnp.concatenate([before_ref[...], x, after_ref[...]], axis=0)
    mask = kid_ref[...] == qid_ref[...]
    state = absorb(state, project(sources, wk_ref), project(sources, wv_ref), query_ref, mask)
    write_state(state, top_ref, total_ref, accum_ref)


def near(before, x, after, wq, wk, wv, key_ids, query_ids):
    return pl.pallas_call(
        near_kernel,
        out_shape=(jax.ShapeDtypeStruct((COUPLES, 2 * HEAD_DIM, 2 * ROWS), BF16),) + STATE_SHAPES,
        compiler_params=pltpu.CompilerParams(vmem_limit_bytes=32 * MIB),
        cost_estimate=pl.CostEstimate(flops=10**9, bytes_accessed=3 * MIB, transcendentals=400000),
        name="near",
    )(before, x, after, wq, wk, wv, key_ids, query_ids)


def select_kernel(at_ref, list_ref, *refs):
    sources, out_ref, all_ref = refs[:-2], refs[-2], refs[-1]
    for n, source in enumerate(sources):
        all_ref[n * SLAB_BLOCKS : (n + 1) * SLAB_BLOCKS] = source[...]

    def one(dest, carry):
        at = at_ref[dest]
        for slot in range(SLOTS):
            out_ref[dest, slot] = all_ref[list_ref[at + slot]]
        return carry

    lax.fori_loop(0, SLAB_BLOCKS, one, 0)


def select(at, pairs, gathered):
    return pl.pallas_call(
        select_kernel,
        in_specs=[SMEM] * 2 + [VMEM] * len(gathered),
        out_specs=VMEM,
        out_shape=jax.ShapeDtypeStruct((SLAB_BLOCKS, SLOTS, TILE_ROWS, TILE_COLS), BF16),
        scratch_shapes=[pltpu.VMEM((len(gathered) * SLAB_BLOCKS, TILE_ROWS, TILE_COLS), BF16)],
        compiler_params=pltpu.CompilerParams(vmem_limit_bytes=32 * MIB),
        cost_estimate=pl.CostEstimate(flops=0, bytes_accessed=8 * MIB, transcendentals=0),
        name="select",
    )(at, pairs, *gathered)


def far_kernel(
    count_ref, held_ref, query_ref, wk_ref, wv_ref, top_in, total_in, accum_in, top_ref, total_ref, accum_ref
):
    count = count_ref[0]
    top_ref[...] = top_in[...]
    total_ref[...] = total_in[...]
    accum_ref[...] = accum_in[...]

    def block(slot):
        rows = []
        for r in range(ROWS // TILE_ROWS):
            tiles = [held_ref[r * COL_TILES + c, slot] for c in range(COL_TILES)]
            rows.append(jnp.concatenate(tiles, axis=1))
        return jnp.concatenate(rows, axis=0)

    def step(i, carry):
        x = jnp.concatenate([block(2 * i), block(2 * i + 1)], axis=0)
        last = jnp.where(2 * i + 1 < count, 2 * ROWS, ROWS)
        mask = lax.broadcasted_iota(jnp.int32, (2 * ROWS, 2 * ROWS), 0) < last
        state = read_state(top_ref, total_ref, accum_ref)
        state = absorb(state, project(x, wk_ref), project(x, wv_ref), query_ref, mask)
        write_state(state, top_ref, total_ref, accum_ref)
        return carry

    lax.fori_loop(0, (count + 1) // 2, step, 0)


def far(count, held, query, wk, wv, state):
    width = held.shape[1]
    return pl.pallas_call(
        far_kernel,
        in_specs=[SMEM] + [VMEM] * 7,
        out_specs=(VMEM,) * 3,
        out_shape=STATE_SHAPES,
        compiler_params=pltpu.CompilerParams(vmem_limit_bytes=32 * MIB),
        cost_estimate=pl.CostEstimate(
            flops=width * 2 * 10**8, bytes_accessed=3 * MIB, transcendentals=width * 140000
        ),
        name="far",
    )(count, held, query, wk, wv, *state)


def layer_norm(value, gain, bias):
    mean = jnp.mean(value, -1, keepdims=True)
    centred = value - mean
    spread = jnp.mean(centred * centred, -1, keepdims=True)
    return centred * lax.rsqrt(spread + 1e-05) * gain + bias


def finish_kernel(
    total_ref, accum_ref, x_ref, w_out_ref, g1_ref, b1_ref, w_up_ref, b_up_ref, w_down_ref, g2_ref, b2_ref, out_ref
):
    columns = []
    for head in range(HEADS):
        lanes = slice(head % 2 * ROWS, (head % 2 + 1) * ROWS)
        total = total_ref[head // 2 : head // 2 + 1, lanes]
        accum = accum_ref[head * HEAD_DIM : (head + 1) * HEAD_DIM, :]
        columns.append((accum / total).astype(BF16))
    attended_t = jnp.concatenate(columns, axis=0)
    mixed = x_ref[...].astype(F32) + lax.dot_general(
        attended_t, w_out_ref[...], (((0,), (0,)), ((), ())), preferred_element_type=F32
    )
    normed = layer_norm(mixed, g1_ref[...], b1_ref[...]).astype(BF16)
    hidden = jnp.maximum(
        jnp.dot(normed, w_up_ref[...], preferred_element_type=F32) + b_up_ref[...], 0.0
    ).astype(BF16)
    second = normed.astype(F32) + jnp.dot(hidden, w_down_ref[...], preferred_element_type=F32)
    out_ref[...] = layer_norm(second, g2_ref[...], b2_ref[...])


def finish(total, accum, x, w_out, g1, b1, w_up, b_up, w_down, g2, b2):
    return pl.pallas_call(
        finish_kernel,
        out_shape=jax.ShapeDtypeStruct((ROWS, D), F32),
        compiler_params=pltpu.CompilerParams(vmem_limit_bytes=40 * MIB),
        cost_estimate=pl.CostEstimate(
            flops=2 * ROWS * (D * D + 2 * D * FF), bytes_accessed=4 * MIB, transcendentals=0
        ),
        name="finish",
    )(total, accum, x, w_out, g1[None], b1[None], w_up, b_up[None], w_down, g2[None], b2[None])


def pair_lists(pair_tiles, pair_count, z, ylo):
    tiles = pair_tiles[0]
    groups = tiles.shape[0]
    valid = jnp.arange(CAP, dtype=jnp.int32)[None, :] < pair_count[0][:, None]
    mine = jnp.where(valid, tiles, MEMBERS * MEMBERS).reshape(1, -1)
    other = lax.ppermute(mine, "ylo", [(0, 1), (1, 0)])
    held = jnp.where(ylo == 0, jnp.concatenate([mine, other]), jnp.concatenate([other, mine]))
    size = held.shape[1]
    slot = jnp.arange(size, dtype=jnp.int32)
    key_group = slot // CAP
    distance = (z - key_group // 2) % (groups // 2)
    query_index = held // MEMBERS
    key_slot = (distance * SLAB_BLOCKS + key_group % 2 * MEMBERS)[None, :] + held % MEMBERS
    ahead = (query_index[:, None, :] < query_index[:, :, None]) | (
        (query_index[:, None, :] == query_index[:, :, None]) & (slot[None, None, :] < slot[None, :, None])
    )
    place = jnp.sum(ahead.astype(jnp.int32), axis=-1)
    pairs = jnp.sum(jnp.where(place[:, None, :] == slot[None, :, None], key_slot[:, None, :], 0), axis=-1)
    pairs = jnp.concatenate([pairs.reshape(-1), jnp.zeros((SLOTS,), jnp.int32)])
    member = jnp.arange(MEMBERS, dtype=jnp.int32)[None, :, None]
    start = jnp.sum((query_index[:, None, :] < member).astype(jnp.int32), axis=-1)
    count = jnp.sum((query_index[:, None, :] == member).astype(jnp.int32), axis=-1)
    start = start + size * jnp.arange(2, dtype=jnp.int32)[:, None]
    return start.reshape(-1), count.reshape(-1), pairs


def gather_rings(tiles):
    size = lax.axis_size("z")
    up = [(z, (z + 1) % size) for z in range(size)]
    down = [(z, (z - 1) % size) for z in range(size)]
    below, above = [tiles], [tiles]
    for step in range(size // 2):
        below.append(lax.ppermute(below[-1], "z", up))
        if step < (size - 1) // 2:
            above.append(lax.ppermute(above[-1], "z", down))
    return below + above[:0:-1]


def shift(x, step, size):
    pairs = [(i, i + step) for i in range(size) if 0 <= i + step < size]
    return lax.ppermute(x, AXES, pairs)


def on_device(
    node_feats,
    graph_ids,
    pair_tiles,
    pair_count,
    w_query,
    w_key,
    w_value,
    w_out,
    ln1_gain,
    ln1_bias,
    w_up,
    b_up,
    w_down,
    ln2_gain,
    ln2_bias,
):
    z, ylo = lax.axis_index("z"), lax.axis_index("ylo")
    own = lax.axis_index(SLAB)
    devices = lax.axis_size(AXES)

    def exchange(value):
        return lax.all_to_all(value, SLAB, split_axis=0, concat_axis=0, tiled=True)

    tiles = node_feats.reshape(ROWS // TILE_ROWS, TILE_ROWS, COL_TILES, TILE_COLS)
    tiles = exchange(tiles.transpose(0, 2, 1, 3).reshape(SLAB_BLOCKS, TILE_ROWS, TILE_COLS))
    gathered = gather_rings(tiles)
    start, count, pairs = pair_lists(pair_tiles, pair_count, z, ylo)

    def mine(value):
        return lax.dynamic_slice_in_dim(value, own, 1, 0)

    fill = jnp.full((ROWS,), -1, jnp.int32)
    ids = jnp.concatenate([fill, graph_ids, fill])
    key_ids = lax.dynamic_slice_in_dim(ids, (z * SLAB_BLOCKS + own) * ROWS, 3 * ROWS, 0)
    query_ids = jnp.tile(key_ids[ROWS : 2 * ROWS], 2)[None, :]
    before = shift(node_feats, 1, devices)
    after = shift(node_feats, -1, devices)
    query, *state = near(
        before, node_feats, after, w_query, w_key, w_value, key_ids[:, None], query_ids
    )

    def add(at, state):
        held = exchange(select(start + jnp.minimum(at, count), pairs, gathered))
        return tuple(far(jnp.clip(mine(count) - at, 0, SLOTS), held, query, w_key, w_value, state))

    state = add(jnp.int32(0), state)
    most = jnp.max(count)
    _, state = lax.while_loop(
        lambda carry: carry[0] < most,
        lambda carry: (carry[0] + SLOTS, add(*carry)),
        (jnp.int32(SLOTS), state),
    )
    return finish(
        state[1], state[2], node_feats, w_out, ln1_gain, ln1_bias, w_up, b_up, w_down, ln2_gain, ln2_bias
    )


def solution(mesh):
    inner = Mesh(mesh.devices.reshape(-1, 2, 2, 4, 2), AXES)
    blk = ("z", "ylo")
    in_specs = (P(AXES, None), P(), P(blk, None, None), P(blk, None)) + (P(),) * 11
    return jax.shard_map(
        on_device, mesh=inner, in_specs=in_specs, out_specs=P(AXES, None), check_vma=False
    )
```

```python
import jax
import jax.numpy as jnp
from jax import lax
from jax.experimental import pallas as pl
from jax.experimental.pallas import tpu as pltpu
from jax.sharding import Mesh
from jax.sharding import PartitionSpec as P

F32 = jnp.float32
BF16 = jnp.bfloat16

AXES = ("zhi", "zlo", "ylo", "yhi", "x", "core")
SLAB = ("zlo", "ylo", "yhi", "x", "core")
D = 512
FF = 1024
HEADS = 8
HEAD_DIM = 64
COUPLES = HEADS // 2
ROWS = 128
MEMBERS = 16
SLAB_GROUPS = 4
SLAB_BLOCKS = 64
CAP = 8
TILE_ROWS = 8
TILE_COLS = 128
COL_TILES = D // TILE_COLS
SLOTS = 16
MIB = 1024 * 1024
FLOOR = -1e30

SMEM = pl.BlockSpec(memory_space=pltpu.SMEM)
VMEM = pl.BlockSpec(memory_space=pltpu.VMEM)


def absorb(state, keys, values, query_ref, mask):
    new = []
    for couple in range(COUPLES):
        top, total, accum = state[couple]
        cols = slice(couple * 2 * HEAD_DIM, (couple + 1) * 2 * HEAD_DIM)
        scores = jnp.dot(keys[:, cols], query_ref[couple], preferred_element_type=F32)
        if mask is not None:
            scores = jnp.where(mask, scores, FLOOR)
        new_top = jnp.maximum(top, jnp.max(scores, axis=0, keepdims=True))
        decay = jnp.exp(top - new_top)
        prob = jnp.exp(scores - new_top)
        total = total * decay + jnp.sum(prob, axis=0, keepdims=True)
        part = lax.dot_general(
            values[:, cols],
            prob.astype(BF16),
            (((0,), (0,)), ((), ())),
            preferred_element_type=F32,
        )
        accum = jnp.concatenate(
            [
                accum[:HEAD_DIM] * decay[:, :ROWS] + part[:HEAD_DIM, :ROWS],
                accum[HEAD_DIM:] * decay[:, ROWS:] + part[HEAD_DIM:, ROWS:],
            ],
            axis=0,
        )
        new.append((new_top, total, accum))
    return new


def read_state(top_ref, total_ref, accum_ref):
    return [
        (
            top_ref[c : c + 1, :],
            total_ref[c : c + 1, :],
            accum_ref[c * 2 * HEAD_DIM : (c + 1) * 2 * HEAD_DIM, :],
        )
        for c in range(COUPLES)
    ]


def write_state(state, top_ref, total_ref, accum_ref):
    for c, (top, total, accum) in enumerate(state):
        top_ref[c : c + 1, :] = top
        total_ref[c : c + 1, :] = total
        accum_ref[c * 2 * HEAD_DIM : (c + 1) * 2 * HEAD_DIM, :] = accum


def project(x, weight_ref):
    return jnp.dot(x, weight_ref[...], preferred_element_type=F32).astype(BF16)


STATE_SHAPES = (
    jax.ShapeDtypeStruct((COUPLES, 2 * ROWS), F32),
    jax.ShapeDtypeStruct((COUPLES, 2 * ROWS), F32),
    jax.ShapeDtypeStruct((D, ROWS), F32),
)


def near_kernel(
    before_ref, x_ref, after_ref, wq_ref, wk_ref, wv_ref, kid_ref, qid_ref, query_ref, top_ref, total_ref, accum_ref
):
    x = x_ref[...]
    query = jnp.dot(x, wq_ref[...], preferred_element_type=F32).astype(BF16).astype(F32)
    query_t = (query.T * (1.0 / 8.0)).astype(BF16)
    zero = jnp.zeros((HEAD_DIM, ROWS), BF16)
    for couple in range(COUPLES):
        at = couple * 2 * HEAD_DIM
        first = query_t[at : at + HEAD_DIM]
        second = query_t[at + HEAD_DIM : at + 2 * HEAD_DIM]
        query_ref[couple] = jnp.concatenate(
            [jnp.concatenate([first, zero], axis=1), jnp.concatenate([zero, second], axis=1)], axis=0
        )
    state = [
        (
            jnp.full((1, 2 * ROWS), FLOOR, F32),
            jnp.zeros((1, 2 * ROWS), F32),
            jnp.zeros((2 * HEAD_DIM, ROWS), F32),
        )
    ] * COUPLES
    sources = jnp.concatenate([before_ref[...], x, after_ref[...]], axis=0)
    mask = kid_ref[...] == qid_ref[...]
    state = absorb(state, project(sources, wk_ref), project(sources, wv_ref), query_ref, mask)
    write_state(state, top_ref, total_ref, accum_ref)


def near(before, x, after, wq, wk, wv, key_ids, query_ids):
    return pl.pallas_call(
        near_kernel,
        out_shape=(jax.ShapeDtypeStruct((COUPLES, 2 * HEAD_DIM, 2 * ROWS), BF16),) + STATE_SHAPES,
        compiler_params=pltpu.CompilerParams(vmem_limit_bytes=32 * MIB),
        cost_estimate=pl.CostEstimate(flops=10**9, bytes_accessed=3 * MIB, transcendentals=400000),
        name="near",
    )(before, x, after, wq, wk, wv, key_ids, query_ids)


def select_kernel(at_ref, list_ref, *refs):
    sources, out_ref, all_ref = refs[:-2], refs[-2], refs[-1]
    for n, source in enumerate(sources):
        all_ref[n * SLAB_BLOCKS : (n + 1) * SLAB_BLOCKS] = source[...]

    def one(dest, carry):
        at = at_ref[dest]
        for slot in range(SLOTS):
            out_ref[dest, slot] = all_ref[list_ref[at + slot]]
        return carry

    lax.fori_loop(0, SLAB_BLOCKS, one, 0)


def select(at, pairs, gathered):
    return pl.pallas_call(
        select_kernel,
        in_specs=[SMEM] * 2 + [VMEM] * len(gathered),
        out_specs=VMEM,
        out_shape=jax.ShapeDtypeStruct((SLAB_BLOCKS, SLOTS, TILE_ROWS, TILE_COLS), BF16),
        scratch_shapes=[pltpu.VMEM((len(gathered) * SLAB_BLOCKS, TILE_ROWS, TILE_COLS), BF16)],
        compiler_params=pltpu.CompilerParams(vmem_limit_bytes=32 * MIB),
        cost_estimate=pl.CostEstimate(flops=0, bytes_accessed=8 * MIB, transcendentals=0),
        name="select",
    )(at, pairs, *gathered)


def far_kernel(
    count_ref, held_ref, query_ref, wk_ref, wv_ref, top_in, total_in, accum_in, top_ref, total_ref, accum_ref
):
    count = count_ref[0]
    top_ref[...] = top_in[...]
    total_ref[...] = total_in[...]
    accum_ref[...] = accum_in[...]

    def block(slot):
        rows = []
        for r in range(ROWS // TILE_ROWS):
            tiles = [held_ref[r * COL_TILES + c, slot].astype(F32) for c in range(COL_TILES)]
            rows.append(jnp.concatenate(tiles, axis=1))
        return jnp.concatenate(rows, axis=0).astype(BF16)

    def step(i, carry):
        x = jnp.concatenate([block(2 * i), block(2 * i + 1)], axis=0)
        last = jnp.where(2 * i + 1 < count, 2 * ROWS, ROWS)
        mask = lax.broadcasted_iota(jnp.int32, (2 * ROWS, 2 * ROWS), 0) < last
        state = read_state(top_ref, total_ref, accum_ref)
        state = absorb(state, project(x, wk_ref), project(x, wv_ref), query_ref, mask)
        write_state(state, top_ref, total_ref, accum_ref)
        return carry

    lax.fori_loop(0, (count + 1) // 2, step, 0)


def far(count, held, query, wk, wv, state):
    width = held.shape[1]
    return pl.pallas_call(
        far_kernel,
        in_specs=[SMEM] + [VMEM] * 7,
        out_specs=(VMEM,) * 3,
        out_shape=STATE_SHAPES,
        compiler_params=pltpu.CompilerParams(vmem_limit_bytes=32 * MIB),
        cost_estimate=pl.CostEstimate(
            flops=width * 2 * 10**8, bytes_accessed=3 * MIB, transcendentals=width * 140000
        ),
        name="far",
    )(count, held, query, wk, wv, *state)


def layer_norm(value, gain, bias):
    mean = jnp.mean(value, -1, keepdims=True)
    centred = value - mean
    spread = jnp.mean(centred * centred, -1, keepdims=True)
    return centred * lax.rsqrt(spread + 1e-05) * gain + bias


def finish_kernel(
    total_ref, accum_ref, x_ref, w_out_ref, g1_ref, b1_ref, w_up_ref, b_up_ref, w_down_ref, g2_ref, b2_ref, out_ref
):
    columns = []
    for head in range(HEADS):
        lanes = slice(head % 2 * ROWS, (head % 2 + 1) * ROWS)
        total = total_ref[head // 2 : head // 2 + 1, lanes]
        accum = accum_ref[head * HEAD_DIM : (head + 1) * HEAD_DIM, :]
        columns.append((accum / total).astype(BF16))
    attended_t = jnp.concatenate(columns, axis=0)
    mixed = x_ref[...].astype(F32) + lax.dot_general(
        attended_t, w_out_ref[...], (((0,), (0,)), ((), ())), preferred_element_type=F32
    )
    normed = layer_norm(mixed, g1_ref[...], b1_ref[...]).astype(BF16)
    hidden = jnp.maximum(
        jnp.dot(normed, w_up_ref[...], preferred_element_type=F32) + b_up_ref[...], 0.0
    ).astype(BF16)
    second = normed.astype(F32) + jnp.dot(hidden, w_down_ref[...], preferred_element_type=F32)
    out_ref[...] = layer_norm(second, g2_ref[...], b2_ref[...])


def finish(total, accum, x, w_out, g1, b1, w_up, b_up, w_down, g2, b2):
    return pl.pallas_call(
        finish_kernel,
        out_shape=jax.ShapeDtypeStruct((ROWS, D), F32),
        compiler_params=pltpu.CompilerParams(vmem_limit_bytes=40 * MIB),
        cost_estimate=pl.CostEstimate(
            flops=2 * ROWS * (D * D + 2 * D * FF), bytes_accessed=4 * MIB, transcendentals=0
        ),
        name="finish",
    )(total, accum, x, w_out, g1[None], b1[None], w_up, b_up[None], w_down, g2[None], b2[None])


def pair_codes(pair_tiles, pair_count):
    valid = jnp.arange(CAP, dtype=jnp.int32)[None, :] < pair_count[0][:, None]
    return jnp.where(valid, pair_tiles[0], MEMBERS * MEMBERS).reshape(-1)


def pair_lists(held, z_high):
    size = held.shape[1]
    planes = lax.axis_size("zhi")
    slot = jnp.arange(size, dtype=jnp.int32)
    key_group = slot // CAP
    distance = (z_high - key_group // SLAB_GROUPS) % planes
    query_index = held // MEMBERS
    key_slot = (distance * SLAB_BLOCKS + key_group % SLAB_GROUPS * MEMBERS)[None, :] + held % MEMBERS
    ahead = (query_index[:, None, :] < query_index[:, :, None]) | (
        (query_index[:, None, :] == query_index[:, :, None]) & (slot[None, None, :] < slot[None, :, None])
    )
    place = jnp.sum(ahead.astype(jnp.int32), axis=-1)
    pairs = jnp.sum(jnp.where(place[:, None, :] == slot[None, :, None], key_slot[:, None, :], 0), axis=-1)
    pairs = jnp.concatenate([pairs.reshape(-1), jnp.zeros((SLOTS,), jnp.int32)])
    member = jnp.arange(MEMBERS, dtype=jnp.int32)[None, :, None]
    start = jnp.sum((query_index[:, None, :] < member).astype(jnp.int32), axis=-1)
    count = jnp.sum((query_index[:, None, :] == member).astype(jnp.int32), axis=-1)
    start = start + size * jnp.arange(SLAB_GROUPS, dtype=jnp.int32)[:, None]
    return start.reshape(-1), count.reshape(-1), pairs


def gather_rings(tiles):
    size = lax.axis_size("zhi")
    up = [(z, (z + 1) % size) for z in range(size)]
    down = [(z, (z - 1) % size) for z in range(size)]
    below, above = [tiles], [tiles]
    for step in range(size // 2):
        below.append(lax.ppermute(below[-1], "zhi", up))
        if step < (size - 1) // 2:
            above.append(lax.ppermute(above[-1], "zhi", down))
    return below + above[:0:-1]


def shift(x, step, size):
    pairs = [(i, i + step) for i in range(size) if 0 <= i + step < size]
    return lax.ppermute(x, AXES, pairs)


def on_device(
    node_feats,
    graph_ids,
    pair_tiles,
    pair_count,
    w_query,
    w_key,
    w_value,
    w_out,
    ln1_gain,
    ln1_bias,
    w_up,
    b_up,
    w_down,
    ln2_gain,
    ln2_bias,
):
    z_high, own = lax.axis_index("zhi"), lax.axis_index(SLAB)
    devices = lax.axis_size(AXES)

    def exchange(value):
        return lax.all_to_all(value, SLAB, split_axis=0, concat_axis=0, tiled=True)

    tiles = node_feats.reshape(ROWS // TILE_ROWS, TILE_ROWS, COL_TILES, TILE_COLS)
    tiles = tiles.transpose(0, 2, 1, 3).reshape(SLAB_BLOCKS, TILE_ROWS, TILE_COLS)
    codes = pair_codes(pair_tiles, pair_count).astype(BF16).reshape(-1, TILE_COLS)
    codes = jnp.pad(codes, ((0, TILE_ROWS - codes.shape[0]), (0, 0)))
    codes = jnp.broadcast_to(codes[None], tiles.shape)
    got = exchange(jnp.concatenate([tiles, codes], axis=1))
    gathered = gather_rings(got[:, :TILE_ROWS])
    codes = got[::MEMBERS, TILE_ROWS : TILE_ROWS + pair_tiles.size // TILE_COLS].astype(jnp.int32)
    start, count, pairs = pair_lists(codes.reshape(SLAB_GROUPS, -1), z_high)

    def mine(value):
        return lax.dynamic_slice_in_dim(value, own, 1, 0)

    fill = jnp.full((ROWS,), -1, jnp.int32)
    ids = jnp.concatenate([fill, graph_ids, fill])
    key_ids = lax.dynamic_slice_in_dim(ids, (z_high * SLAB_BLOCKS + own) * ROWS, 3 * ROWS, 0)
    query_ids = jnp.tile(key_ids[ROWS : 2 * ROWS], 2)[None, :]
    before = shift(node_feats, 1, devices)
    after = shift(node_feats, -1, devices)
    query, *state = near(
        before, node_feats, after, w_query, w_key, w_value, key_ids[:, None], query_ids
    )

    def add(at, state):
        held = exchange(select(start + jnp.minimum(at, count), pairs, gathered))
        return tuple(far(jnp.clip(mine(count) - at, 0, SLOTS), held, query, w_key, w_value, state))

    state = add(jnp.int32(0), state)
    most = jnp.max(count)
    _, state = lax.while_loop(
        lambda carry: carry[0] < most,
        lambda carry: (carry[0] + SLOTS, add(*carry)),
        (jnp.int32(SLOTS), state),
    )
    return finish(
        state[1], state[2], node_feats, w_out, ln1_gain, ln1_bias, w_up, b_up, w_down, ln2_gain, ln2_bias
    )


def solution(mesh):
    inner = Mesh(mesh.devices.reshape(-1, 2, 2, 2, 4, 2), AXES)
    blk = ("zhi", "zlo", "ylo")
    in_specs = (P(AXES, None), P(), P(blk, None, None), P(blk, None)) + (P(),) * 11
    return jax.shard_map(
        on_device, mesh=inner, in_specs=in_specs, out_specs=P(AXES, None), check_vma=False
    )
```

```python
import jax
import jax.numpy as jnp
from jax import lax
from jax.experimental import pallas as pl
from jax.experimental.pallas import tpu as pltpu
from jax.sharding import Mesh
from jax.sharding import PartitionSpec as P

F32 = jnp.float32
BF16 = jnp.bfloat16

AXES = ("zhi", "zlo", "ylo", "yhi", "x", "core")
SLAB = ("zlo", "ylo", "yhi", "x", "core")
D = 512
FF = 1024
HEADS = 8
HEAD_DIM = 64
COUPLES = HEADS // 2
ROWS = 128
MEMBERS = 16
SLAB_GROUPS = 4
SLAB_BLOCKS = 64
CAP = 8
TILE_ROWS = 8
TILE_COLS = 128
COL_TILES = D // TILE_COLS
SLOTS = 16
GULP = 4
MIB = 1024 * 1024
FLOOR = -1e30

SMEM = pl.BlockSpec(memory_space=pltpu.SMEM)
VMEM = pl.BlockSpec(memory_space=pltpu.VMEM)


def absorb(state, keys, values, query_ref, mask, bias=()):
    new = []
    for couple in range(COUPLES):
        top, total, accum = state[couple]
        cols = slice(couple * 2 * HEAD_DIM, (couple + 1) * 2 * HEAD_DIM)
        scores = jnp.dot(keys[:, cols], query_ref[couple], preferred_element_type=F32)
        if mask is not None:
            scores = jnp.where(mask, scores, FLOOR)
        if bias:
            scores = jnp.concatenate(
                [scores[n * ROWS : (n + 1) * ROWS] + part for n, part in enumerate(bias)], axis=0
            )
        new_top = jnp.maximum(top, jnp.max(scores, axis=0, keepdims=True))
        decay = jnp.exp(top - new_top)
        prob = jnp.exp(scores - new_top)
        total = total * decay + jnp.sum(prob, axis=0, keepdims=True)
        part = lax.dot_general(
            values[:, cols],
            prob.astype(BF16),
            (((0,), (0,)), ((), ())),
            preferred_element_type=F32,
        )
        accum = jnp.concatenate(
            [
                accum[:HEAD_DIM] * decay[:, :ROWS] + part[:HEAD_DIM, :ROWS],
                accum[HEAD_DIM:] * decay[:, ROWS:] + part[HEAD_DIM:, ROWS:],
            ],
            axis=0,
        )
        new.append((new_top, total, accum))
    return new


def read_state(top_ref, total_ref, accum_ref):
    return [
        (
            top_ref[c : c + 1, :],
            total_ref[c : c + 1, :],
            accum_ref[c * 2 * HEAD_DIM : (c + 1) * 2 * HEAD_DIM, :],
        )
        for c in range(COUPLES)
    ]


def write_state(state, top_ref, total_ref, accum_ref):
    for c, (top, total, accum) in enumerate(state):
        top_ref[c : c + 1, :] = top
        total_ref[c : c + 1, :] = total
        accum_ref[c * 2 * HEAD_DIM : (c + 1) * 2 * HEAD_DIM, :] = accum


def project(x, weight_ref):
    return jnp.dot(x, weight_ref[...], preferred_element_type=F32).astype(BF16)


STATE_SHAPES = (
    jax.ShapeDtypeStruct((COUPLES, 2 * ROWS), F32),
    jax.ShapeDtypeStruct((COUPLES, 2 * ROWS), F32),
    jax.ShapeDtypeStruct((D, ROWS), F32),
)


def near_kernel(
    before_ref, x_ref, after_ref, wq_ref, wk_ref, wv_ref, kid_ref, qid_ref, query_ref, top_ref, total_ref, accum_ref
):
    x = x_ref[...]
    query = jnp.dot(x, wq_ref[...], preferred_element_type=F32).astype(BF16).astype(F32)
    query_t = (query.T * (1.0 / 8.0)).astype(BF16)
    zero = jnp.zeros((HEAD_DIM, ROWS), BF16)
    for couple in range(COUPLES):
        at = couple * 2 * HEAD_DIM
        first = query_t[at : at + HEAD_DIM]
        second = query_t[at + HEAD_DIM : at + 2 * HEAD_DIM]
        query_ref[couple] = jnp.concatenate(
            [jnp.concatenate([first, zero], axis=1), jnp.concatenate([zero, second], axis=1)], axis=0
        )
    state = [
        (
            jnp.full((1, 2 * ROWS), FLOOR, F32),
            jnp.zeros((1, 2 * ROWS), F32),
            jnp.zeros((2 * HEAD_DIM, ROWS), F32),
        )
    ] * COUPLES
    sources = jnp.concatenate([before_ref[...], x, after_ref[...]], axis=0)
    mask = kid_ref[...] == qid_ref[...]
    state = absorb(state, project(sources, wk_ref), project(sources, wv_ref), query_ref, mask)
    write_state(state, top_ref, total_ref, accum_ref)


def near(before, x, after, wq, wk, wv, key_ids, query_ids):
    return pl.pallas_call(
        near_kernel,
        out_shape=(jax.ShapeDtypeStruct((COUPLES, 2 * HEAD_DIM, 2 * ROWS), BF16),) + STATE_SHAPES,
        compiler_params=pltpu.CompilerParams(vmem_limit_bytes=32 * MIB),
        cost_estimate=pl.CostEstimate(flops=10**9, bytes_accessed=3 * MIB, transcendentals=400000),
        name="near",
    )(before, x, after, wq, wk, wv, key_ids, query_ids)


def pack_kernel(x_ref, tiles_ref, counts_ref, out_ref):
    x = x_ref[...].astype(F32)
    used = lax.broadcasted_iota(jnp.int32, tiles_ref.shape, 0) < counts_ref[...]
    codes = jnp.where(used, tiles_ref[...], MEMBERS * MEMBERS).astype(F32)
    for n in range(SLAB_BLOCKS):
        row, col = n // COL_TILES * TILE_ROWS, n % COL_TILES * TILE_COLS
        tile = x[row : row + TILE_ROWS, col : col + TILE_COLS]
        out_ref[n] = jnp.concatenate([tile, codes], axis=0).astype(BF16)


def pack(x, pair_tiles, pair_count):
    groups = pair_tiles.shape[1]
    pad = ((0, 0), (0, TILE_COLS - groups))
    return pl.pallas_call(
        pack_kernel,
        out_shape=jax.ShapeDtypeStruct((SLAB_BLOCKS, TILE_ROWS + CAP, TILE_COLS), BF16),
        compiler_params=pltpu.CompilerParams(vmem_limit_bytes=60 * MIB),
        name="pack",
    )(x, jnp.pad(pair_tiles[0].T, pad), jnp.pad(pair_count, pad))


def select_kernel(at_ref, list_ref, *refs):
    sources, out_ref, all_ref = refs[:-2], refs[-2], refs[-1]
    for n, source in enumerate(sources):
        all_ref[n * SLAB_BLOCKS : (n + 1) * SLAB_BLOCKS] = source[...]

    def one(dest, carry):
        at = at_ref[dest]
        for slot in range(SLOTS):
            out_ref[dest, slot] = all_ref[list_ref[at + slot]]
        return carry

    lax.fori_loop(0, SLAB_BLOCKS, one, 0, unroll=4)


def select(at, pairs, gathered):
    return pl.pallas_call(
        select_kernel,
        in_specs=[SMEM] * 2 + [VMEM] * len(gathered),
        out_specs=VMEM,
        out_shape=jax.ShapeDtypeStruct((SLAB_BLOCKS, SLOTS, TILE_ROWS, TILE_COLS), BF16),
        scratch_shapes=[pltpu.VMEM((len(gathered) * SLAB_BLOCKS, TILE_ROWS, TILE_COLS), BF16)],
        compiler_params=pltpu.CompilerParams(vmem_limit_bytes=32 * MIB),
        cost_estimate=pl.CostEstimate(flops=0, bytes_accessed=8 * MIB, transcendentals=0),
        name="select",
    )(at, pairs, *gathered)


def gather_block(held_ref, slot):
    rows = []
    for r in range(ROWS // TILE_ROWS):
        tiles = [held_ref[r * COL_TILES + c, slot].astype(F32) for c in range(COL_TILES)]
        rows.append(jnp.concatenate(tiles, axis=1))
    return jnp.concatenate(rows, axis=0).astype(BF16)


def far_steps(count, held_ref, query_ref, wk_ref, wv_ref, state_refs):
    def step(i, carry):
        slots = [GULP * i + u for u in range(GULP)]
        x = jnp.concatenate([gather_block(held_ref, slot) for slot in slots], axis=0)
        bias = [jnp.where(slot < count, 0.0, FLOOR).astype(F32) for slot in slots]
        state = read_state(*state_refs)
        state = absorb(state, project(x, wk_ref), project(x, wv_ref), query_ref, None, bias)
        write_state(state, *state_refs)
        return carry

    lax.fori_loop(0, (count + GULP - 1) // GULP, step, 0)


def far_kernel(
    count_ref, held_ref, query_ref, wk_ref, wv_ref, top_in, total_in, accum_in, top_ref, total_ref, accum_ref
):
    top_ref[...] = top_in[...]
    total_ref[...] = total_in[...]
    accum_ref[...] = accum_in[...]
    far_steps(count_ref[0], held_ref, query_ref, wk_ref, wv_ref, (top_ref, total_ref, accum_ref))


def far(count, held, query, wk, wv, state):
    return pl.pallas_call(
        far_kernel,
        in_specs=[SMEM] + [VMEM] * 7,
        out_specs=(VMEM,) * 3,
        out_shape=STATE_SHAPES,
        compiler_params=pltpu.CompilerParams(vmem_limit_bytes=32 * MIB),
        name="far",
    )(count, held, query, wk, wv, *state)


def layer_norm(value, gain, bias):
    mean = jnp.mean(value, -1, keepdims=True)
    centred = value - mean
    spread = jnp.mean(centred * centred, -1, keepdims=True)
    return centred * lax.rsqrt(spread + 1e-05) * gain + bias


def finish_kernel(
    count_ref,
    held_ref,
    query_ref,
    wk_ref,
    wv_ref,
    top_in,
    total_in,
    accum_in,
    x_ref,
    g1_ref,
    b1_ref,
    b_up_ref,
    g2_ref,
    b2_ref,
    w_out_hbm,
    w_up_hbm,
    w_down_hbm,
    out_ref,
    top_ref,
    total_ref,
    accum_ref,
    w_out_ref,
    w_up_ref,
    w_down_ref,
    sems,
):
    weights = ((w_out_hbm, w_out_ref), (w_up_hbm, w_up_ref), (w_down_hbm, w_down_ref))
    copies = [pltpu.make_async_copy(a, b, sems.at[n]) for n, (a, b) in enumerate(weights)]
    for copy in copies:
        copy.start()
    far_kernel(
        count_ref,
        held_ref,
        query_ref,
        wk_ref,
        wv_ref,
        top_in,
        total_in,
        accum_in,
        top_ref,
        total_ref,
        accum_ref,
    )
    columns = []
    for head in range(HEADS):
        lanes = slice(head % 2 * ROWS, (head % 2 + 1) * ROWS)
        total = total_ref[head // 2 : head // 2 + 1, lanes]
        accum = accum_ref[head * HEAD_DIM : (head + 1) * HEAD_DIM, :]
        columns.append((accum / total).astype(BF16))
    attended_t = jnp.concatenate(columns, axis=0)
    copies[0].wait()
    mixed = x_ref[...].astype(F32) + lax.dot_general(
        attended_t, w_out_ref[...], (((0,), (0,)), ((), ())), preferred_element_type=F32
    )
    normed = layer_norm(mixed, g1_ref[...], b1_ref[...]).astype(BF16)
    copies[1].wait()
    hidden = jnp.maximum(
        jnp.dot(normed, w_up_ref[...], preferred_element_type=F32) + b_up_ref[...], 0.0
    ).astype(BF16)
    copies[2].wait()
    second = normed.astype(F32) + jnp.dot(hidden, w_down_ref[...], preferred_element_type=F32)
    out_ref[...] = layer_norm(second, g2_ref[...], b2_ref[...])


def finish(count, held, query, wk, wv, state, x, g1, b1, b_up, g2, b2, w_out, w_up, w_down):
    hbm = pl.BlockSpec(memory_space=pltpu.HBM)
    return pl.pallas_call(
        finish_kernel,
        in_specs=[SMEM] + [VMEM] * 13 + [hbm] * 3,
        out_specs=(VMEM,) * 4,
        out_shape=(jax.ShapeDtypeStruct((ROWS, D), F32),) + STATE_SHAPES,
        scratch_shapes=[
            pltpu.VMEM((D, D), BF16),
            pltpu.VMEM((D, FF), BF16),
            pltpu.VMEM((FF, D), BF16),
            pltpu.SemaphoreType.DMA((3,)),
        ],
        compiler_params=pltpu.CompilerParams(vmem_limit_bytes=44 * MIB),
        cost_estimate=pl.CostEstimate(flops=4 * 10**9, bytes_accessed=8 * MIB, transcendentals=10**6),
        name="finish",
    )(
        count,
        held,
        query,
        wk,
        wv,
        *state,
        x,
        g1[None],
        b1[None],
        b_up[None],
        g2[None],
        b2[None],
        w_out,
        w_up,
        w_down,
    )


def pair_lists(held, z_high):
    size = held.shape[1]
    planes = lax.axis_size("zhi")
    slot = jnp.arange(size, dtype=jnp.int32)
    key_group = slot % (size // CAP)
    distance = (z_high - key_group // SLAB_GROUPS) % planes
    query_index = held // MEMBERS
    key_slot = (distance * SLAB_BLOCKS + key_group % SLAB_GROUPS * MEMBERS)[None, :] + held % MEMBERS
    ahead = (query_index[:, None, :] < query_index[:, :, None]) | (
        (query_index[:, None, :] == query_index[:, :, None]) & (slot[None, None, :] < slot[None, :, None])
    )
    place = jnp.sum(ahead.astype(jnp.int32), axis=-1)
    pairs = jnp.sum(jnp.where(place[:, None, :] == slot[None, :, None], key_slot[:, None, :], 0), axis=-1)
    pairs = jnp.concatenate([pairs.reshape(-1), jnp.zeros((SLOTS,), jnp.int32)])
    member = jnp.arange(MEMBERS, dtype=jnp.int32)[None, :, None]
    start = jnp.sum((query_index[:, None, :] < member).astype(jnp.int32), axis=-1)
    count = jnp.sum((query_index[:, None, :] == member).astype(jnp.int32), axis=-1)
    start = start + size * jnp.arange(SLAB_GROUPS, dtype=jnp.int32)[:, None]
    return start.reshape(-1), count.reshape(-1), pairs


def gather_rings(tiles):
    size = lax.axis_size("zhi")
    up = [(z, (z + 1) % size) for z in range(size)]
    down = [(z, (z - 1) % size) for z in range(size)]
    below, above = [tiles], [tiles]
    for step in range(size // 2):
        below.append(lax.ppermute(below[-1], "zhi", up))
        if step < (size - 1) // 2:
            above.append(lax.ppermute(above[-1], "zhi", down))
    return below + above[:0:-1]


def shift(x, step, size):
    pairs = [(i, i + step) for i in range(size) if 0 <= i + step < size]
    return lax.ppermute(x, AXES, pairs)


def on_device(
    node_feats,
    graph_ids,
    pair_tiles,
    pair_count,
    w_query,
    w_key,
    w_value,
    w_out,
    ln1_gain,
    ln1_bias,
    w_up,
    b_up,
    w_down,
    ln2_gain,
    ln2_bias,
):
    z_high, own = lax.axis_index("zhi"), lax.axis_index(SLAB)
    devices = lax.axis_size(AXES)

    def exchange(value):
        return lax.all_to_all(value, SLAB, split_axis=0, concat_axis=0, tiled=True)

    got = exchange(pack(node_feats, pair_tiles, pair_count))
    before = shift(node_feats, 1, devices)
    after = shift(node_feats, -1, devices)
    tiles, before, after = lax.optimization_barrier((got[:, :TILE_ROWS], before, after))
    gathered = gather_rings(tiles)
    codes = got[::MEMBERS, TILE_ROWS:, : pair_tiles.shape[1]].astype(jnp.int32)
    start, count, pairs = pair_lists(codes.reshape(SLAB_GROUPS, -1), z_high)

    def mine(value):
        return lax.dynamic_slice_in_dim(value, own, 1, 0)

    fill = jnp.full((ROWS,), -1, jnp.int32)
    ids = jnp.concatenate([fill, graph_ids, fill])
    key_ids = lax.dynamic_slice_in_dim(ids, (z_high * SLAB_BLOCKS + own) * ROWS, 3 * ROWS, 0)
    query_ids = jnp.tile(key_ids[ROWS : 2 * ROWS], 2)[None, :]
    query, *state = near(
        before, node_feats, after, w_query, w_key, w_value, key_ids[:, None], query_ids
    )

    def fetch(at):
        held = exchange(select(start + jnp.minimum(at, count), pairs, gathered))
        return jnp.clip(mine(count) - at, 0, SLOTS), held

    def close(part, held, state):
        return finish(
            part,
            held,
            query,
            w_key,
            w_value,
            state,
            node_feats,
            ln1_gain,
            ln1_bias,
            b_up,
            ln2_gain,
            ln2_bias,
            w_out,
            w_up,
            w_down,
        )

    part, held = fetch(jnp.int32(0))
    out, *state = close(part, held, state)
    most = jnp.max(count)

    def go_on(state):
        def more(carry):
            at, state = carry
            part, held = fetch(at)
            return at + SLOTS, tuple(far(part, held, query, w_key, w_value, state))

        _, state = lax.while_loop(lambda carry: carry[0] < most, more, (jnp.int32(SLOTS), state))
        return close(jnp.zeros_like(part), held, state)[0]

    return lax.cond(most > SLOTS, go_on, lambda state: out, tuple(state))


def solution(mesh):
    inner = Mesh(mesh.devices.reshape(-1, 2, 2, 2, 4, 2), AXES)
    blk = ("zhi", "zlo", "ylo")
    in_specs = (P(AXES, None), P(), P(blk, None, None), P(blk, None)) + (P(),) * 11
    return jax.shard_map(
        on_device, mesh=inner, in_specs=in_specs, out_specs=P(AXES, None), check_vma=False
    )
```

```python
import jax
import jax.numpy as jnp
from jax import lax
from jax.experimental import pallas as pl
from jax.experimental.pallas import tpu as pltpu
from jax.sharding import Mesh
from jax.sharding import PartitionSpec as P

F32 = jnp.float32
BF16 = jnp.bfloat16

AXES = ("zhi", "zlo", "ylo", "yhi", "x", "core")
SLAB = ("zlo", "ylo", "yhi", "x", "core")
D = 512
FF = 1024
HEADS = 8
HEAD_DIM = 64
COUPLES = HEADS // 2
ROWS = 128
MEMBERS = 16
SLAB_GROUPS = 4
SLAB_BLOCKS = 64
CAP = 8
TILE_ROWS = 8
TILE_COLS = 128
COL_TILES = D // TILE_COLS
EARLY = 10
LATE = 6
GULPS = 2
MIB = 1024 * 1024
FLOOR = -1e30

SMEM = pl.BlockSpec(memory_space=pltpu.SMEM)
VMEM = pl.BlockSpec(memory_space=pltpu.VMEM)


def absorb(state, keys, values, query_ref, mask, bias=()):
    new = []
    for couple in range(COUPLES):
        top, total, accum = state[couple]
        cols = slice(couple * 2 * HEAD_DIM, (couple + 1) * 2 * HEAD_DIM)
        scores = jnp.dot(keys[:, cols], query_ref[couple], preferred_element_type=F32)
        if mask is not None:
            scores = jnp.where(mask, scores, FLOOR)
        if bias:
            scores = jnp.concatenate(
                [scores[n * ROWS : (n + 1) * ROWS] + part for n, part in enumerate(bias)], axis=0
            )
        new_top = jnp.maximum(top, jnp.max(scores, axis=0, keepdims=True))
        decay = jnp.exp(top - new_top)
        prob = jnp.exp(scores - new_top)
        total = total * decay + jnp.sum(prob, axis=0, keepdims=True)
        part = lax.dot_general(
            values[:, cols],
            prob.astype(BF16),
            (((0,), (0,)), ((), ())),
            preferred_element_type=F32,
        )
        accum = jnp.concatenate(
            [
                accum[:HEAD_DIM] * decay[:, :ROWS] + part[:HEAD_DIM, :ROWS],
                accum[HEAD_DIM:] * decay[:, ROWS:] + part[HEAD_DIM:, ROWS:],
            ],
            axis=0,
        )
        new.append((new_top, total, accum))
    return new


def read_state(top_ref, total_ref, accum_ref):
    return [
        (
            top_ref[c : c + 1, :],
            total_ref[c : c + 1, :],
            accum_ref[c * 2 * HEAD_DIM : (c + 1) * 2 * HEAD_DIM, :],
        )
        for c in range(COUPLES)
    ]


def write_state(state, top_ref, total_ref, accum_ref):
    for c, (top, total, accum) in enumerate(state):
        top_ref[c : c + 1, :] = top
        total_ref[c : c + 1, :] = total
        accum_ref[c * 2 * HEAD_DIM : (c + 1) * 2 * HEAD_DIM, :] = accum


def project(x, weight_ref):
    return jnp.dot(x, weight_ref[...], preferred_element_type=F32).astype(BF16)


STATE_SHAPES = (
    jax.ShapeDtypeStruct((COUPLES, 2 * ROWS), F32),
    jax.ShapeDtypeStruct((COUPLES, 2 * ROWS), F32),
    jax.ShapeDtypeStruct((D, ROWS), F32),
)


def near_kernel(
    before_ref, x_ref, after_ref, wq_ref, wk_ref, wv_ref, kid_ref, qid_ref, query_ref, top_ref, total_ref, accum_ref
):
    x = x_ref[...]
    query = jnp.dot(x, wq_ref[...], preferred_element_type=F32).astype(BF16).astype(F32)
    query_t = (query.T * (1.0 / 8.0)).astype(BF16)
    zero = jnp.zeros((HEAD_DIM, ROWS), BF16)
    for couple in range(COUPLES):
        at = couple * 2 * HEAD_DIM
        first = query_t[at : at + HEAD_DIM]
        second = query_t[at + HEAD_DIM : at + 2 * HEAD_DIM]
        query_ref[couple] = jnp.concatenate(
            [jnp.concatenate([first, zero], axis=1), jnp.concatenate([zero, second], axis=1)], axis=0
        )
    state = [
        (
            jnp.full((1, 2 * ROWS), FLOOR, F32),
            jnp.zeros((1, 2 * ROWS), F32),
            jnp.zeros((2 * HEAD_DIM, ROWS), F32),
        )
    ] * COUPLES
    sources = jnp.concatenate([before_ref[...], x, after_ref[...]], axis=0)
    mask = kid_ref[...] == qid_ref[...]
    state = absorb(state, project(sources, wk_ref), project(sources, wv_ref), query_ref, mask)
    write_state(state, top_ref, total_ref, accum_ref)


def near(before, x, after, wq, wk, wv, key_ids, query_ids):
    return pl.pallas_call(
        near_kernel,
        out_shape=(jax.ShapeDtypeStruct((COUPLES, 2 * HEAD_DIM, 2 * ROWS), BF16),) + STATE_SHAPES,
        compiler_params=pltpu.CompilerParams(vmem_limit_bytes=32 * MIB),
        cost_estimate=pl.CostEstimate(flops=10**9, bytes_accessed=3 * MIB, transcendentals=400000),
        name="near",
    )(before, x, after, wq, wk, wv, key_ids, query_ids)


def pack_kernel(x_ref, tiles_ref, counts_ref, out_ref):
    x = x_ref[...].astype(F32)
    used = lax.broadcasted_iota(jnp.int32, tiles_ref.shape, 0) < counts_ref[...]
    codes = jnp.where(used, tiles_ref[...], MEMBERS * MEMBERS).astype(F32)
    codes = jnp.concatenate([codes, jnp.zeros((CAP, TILE_COLS - codes.shape[1]), F32)], axis=1)
    for n in range(SLAB_BLOCKS):
        row, col = n // COL_TILES * TILE_ROWS, n % COL_TILES * TILE_COLS
        tile = x[row : row + TILE_ROWS, col : col + TILE_COLS]
        out_ref[n] = jnp.concatenate([tile, codes], axis=0).astype(BF16)


def pack(x, pair_tiles, pair_count):
    return pl.pallas_call(
        pack_kernel,
        out_shape=jax.ShapeDtypeStruct((SLAB_BLOCKS, TILE_ROWS + CAP, TILE_COLS), BF16),
        compiler_params=pltpu.CompilerParams(vmem_limit_bytes=60 * MIB),
        name="pack",
    )(x, pair_tiles[0].T, pair_count)


def select_kernel(at_ref, list_ref, *refs):
    slots = refs[-2].shape[1]
    sources, out_ref, all_ref = refs[:-2], refs[-2], refs[-1]
    for n, source in enumerate(sources):
        all_ref[n * SLAB_BLOCKS : (n + 1) * SLAB_BLOCKS] = source[...]

    def one(dest, carry):
        at = at_ref[dest]
        for slot in range(slots):
            out_ref[dest, slot] = all_ref[list_ref[at + slot]]
        return carry

    lax.fori_loop(0, SLAB_BLOCKS, one, 0, unroll=4)


def select(slots, at, pairs, gathered):
    return pl.pallas_call(
        select_kernel,
        in_specs=[SMEM] * 2 + [VMEM] * len(gathered),
        out_specs=VMEM,
        out_shape=jax.ShapeDtypeStruct((SLAB_BLOCKS, slots, TILE_ROWS, TILE_COLS), BF16),
        scratch_shapes=[pltpu.VMEM((len(gathered) * SLAB_BLOCKS, TILE_ROWS, TILE_COLS), BF16)],
        compiler_params=pltpu.CompilerParams(vmem_limit_bytes=32 * MIB),
        cost_estimate=pl.CostEstimate(flops=0, bytes_accessed=8 * MIB, transcendentals=0),
        name="select",
    )(at, pairs, *gathered)


def gather_block(held_ref, slot):
    rows = []
    for r in range(ROWS // TILE_ROWS):
        tiles = [held_ref[r * COL_TILES + c, slot].astype(F32) for c in range(COL_TILES)]
        rows.append(jnp.concatenate(tiles, axis=1))
    return jnp.concatenate(rows, axis=0).astype(BF16)


def far_steps(count, held_ref, query_ref, wk_ref, wv_ref, state_refs):
    gulp = held_ref.shape[1] // GULPS

    def step(i, carry):
        slots = [gulp * i + u for u in range(gulp)]
        x = jnp.concatenate([gather_block(held_ref, slot) for slot in slots], axis=0)
        bias = [jnp.where(slot < count, 0.0, FLOOR).astype(F32) for slot in slots]
        state = read_state(*state_refs)
        state = absorb(state, project(x, wk_ref), project(x, wv_ref), query_ref, None, bias)
        write_state(state, *state_refs)
        return carry

    lax.fori_loop(0, (count + gulp - 1) // gulp, step, 0)


def far_kernel(
    count_ref, held_ref, query_ref, wk_ref, wv_ref, top_in, total_in, accum_in, top_ref, total_ref, accum_ref
):
    top_ref[...] = top_in[...]
    total_ref[...] = total_in[...]
    accum_ref[...] = accum_in[...]
    far_steps(count_ref[0], held_ref, query_ref, wk_ref, wv_ref, (top_ref, total_ref, accum_ref))


def far(count, held, query, wk, wv, state):
    return pl.pallas_call(
        far_kernel,
        in_specs=[SMEM] + [VMEM] * 7,
        out_specs=(VMEM,) * 3,
        out_shape=STATE_SHAPES,
        compiler_params=pltpu.CompilerParams(vmem_limit_bytes=32 * MIB),
        cost_estimate=pl.CostEstimate(flops=10**9, bytes_accessed=4 * MIB, transcendentals=10**6),
        name="far",
    )(count, held, query, wk, wv, *state)


def layer_norm(value, gain, bias):
    mean = jnp.mean(value, -1, keepdims=True)
    centred = value - mean
    spread = jnp.mean(centred * centred, -1, keepdims=True)
    return centred * lax.rsqrt(spread + 1e-05) * gain + bias


def finish_kernel(
    count_ref,
    held_ref,
    query_ref,
    wk_ref,
    wv_ref,
    top_in,
    total_in,
    accum_in,
    x_ref,
    g1_ref,
    b1_ref,
    b_up_ref,
    g2_ref,
    b2_ref,
    w_out_hbm,
    w_up_hbm,
    w_down_hbm,
    out_ref,
    top_ref,
    total_ref,
    accum_ref,
    w_out_ref,
    w_up_ref,
    w_down_ref,
    sems,
):
    weights = ((w_out_hbm, w_out_ref), (w_up_hbm, w_up_ref), (w_down_hbm, w_down_ref))
    copies = [pltpu.make_async_copy(a, b, sems.at[n]) for n, (a, b) in enumerate(weights)]
    for copy in copies:
        copy.start()
    far_kernel(
        count_ref,
        held_ref,
        query_ref,
        wk_ref,
        wv_ref,
        top_in,
        total_in,
        accum_in,
        top_ref,
        total_ref,
        accum_ref,
    )
    columns = []
    for head in range(HEADS):
        lanes = slice(head % 2 * ROWS, (head % 2 + 1) * ROWS)
        total = total_ref[head // 2 : head // 2 + 1, lanes]
        accum = accum_ref[head * HEAD_DIM : (head + 1) * HEAD_DIM, :]
        columns.append((accum / total).astype(BF16))
    attended_t = jnp.concatenate(columns, axis=0)
    copies[0].wait()
    mixed = x_ref[...].astype(F32) + lax.dot_general(
        attended_t, w_out_ref[...], (((0,), (0,)), ((), ())), preferred_element_type=F32
    )
    normed = layer_norm(mixed, g1_ref[...], b1_ref[...]).astype(BF16)
    copies[1].wait()
    hidden = jnp.maximum(
        jnp.dot(normed, w_up_ref[...], preferred_element_type=F32) + b_up_ref[...], 0.0
    ).astype(BF16)
    copies[2].wait()
    second = normed.astype(F32) + jnp.dot(hidden, w_down_ref[...], preferred_element_type=F32)
    out_ref[...] = layer_norm(second, g2_ref[...], b2_ref[...])


def finish(count, held, query, wk, wv, state, x, g1, b1, b_up, g2, b2, w_out, w_up, w_down):
    hbm = pl.BlockSpec(memory_space=pltpu.HBM)
    return pl.pallas_call(
        finish_kernel,
        in_specs=[SMEM] + [VMEM] * 13 + [hbm] * 3,
        out_specs=(VMEM,) * 4,
        out_shape=(jax.ShapeDtypeStruct((ROWS, D), F32),) + STATE_SHAPES,
        scratch_shapes=[
            pltpu.VMEM((D, D), BF16),
            pltpu.VMEM((D, FF), BF16),
            pltpu.VMEM((FF, D), BF16),
            pltpu.SemaphoreType.DMA((3,)),
        ],
        compiler_params=pltpu.CompilerParams(vmem_limit_bytes=44 * MIB),
        cost_estimate=pl.CostEstimate(flops=4 * 10**9, bytes_accessed=8 * MIB, transcendentals=10**6),
        name="finish",
    )(
        count,
        held,
        query,
        wk,
        wv,
        *state,
        x,
        g1[None],
        b1[None],
        b_up[None],
        g2[None],
        b2[None],
        w_out,
        w_up,
        w_down,
    )


def pair_lists(held, z_high):
    size = held.shape[1]
    planes = lax.axis_size("zhi")
    slot = jnp.arange(size, dtype=jnp.int32)
    key_group = slot % (size // CAP)
    distance = (z_high - key_group // SLAB_GROUPS) % planes
    order = held // MEMBERS * 2 + (distance == planes // 2).astype(jnp.int32)[None, :]
    key_slot = (distance * SLAB_BLOCKS + key_group % SLAB_GROUPS * MEMBERS)[None, :] + held % MEMBERS
    ahead = (order[:, None, :] < order[:, :, None]) | (
        (order[:, None, :] == order[:, :, None]) & (slot[None, None, :] < slot[None, :, None])
    )
    place = jnp.sum(ahead.astype(jnp.int32), axis=-1)
    pairs = jnp.sum(jnp.where(place[:, None, :] == slot[None, :, None], key_slot[:, None, :], 0), axis=-1)
    pairs = jnp.concatenate([pairs.reshape(-1), jnp.zeros((EARLY,), jnp.int32)])
    member = 2 * jnp.arange(MEMBERS, dtype=jnp.int32)[None, :, None]
    order = order[:, None, :]
    start = jnp.sum((order < member).astype(jnp.int32), axis=-1)
    early = jnp.sum((order == member).astype(jnp.int32), axis=-1)
    count = early + jnp.sum((order == member + 1).astype(jnp.int32), axis=-1)
    start = start + size * jnp.arange(SLAB_GROUPS, dtype=jnp.int32)[:, None]
    return start.reshape(-1), jnp.minimum(early, EARLY).reshape(-1), count.reshape(-1), pairs


def gather_rings(tiles):
    size = lax.axis_size("zhi")
    up = [(z, (z + 1) % size) for z in range(size)]
    down = [(z, (z - 1) % size) for z in range(size)]
    below, above = [tiles], [tiles]
    for step in range(size // 2):
        below.append(lax.ppermute(below[-1], "zhi", up))
        if step < (size - 1) // 2:
            above.append(lax.ppermute(above[-1], "zhi", down))
    above = above[:0:-1]
    return below[:-1] + [tiles] + above, below + above


def shift(x, step, size):
    pairs = [(i, i + step) for i in range(size) if 0 <= i + step < size]
    return lax.ppermute(x, AXES, pairs)


def on_device(
    node_feats,
    graph_ids,
    pair_tiles,
    pair_count,
    w_query,
    w_key,
    w_value,
    w_out,
    ln1_gain,
    ln1_bias,
    w_up,
    b_up,
    w_down,
    ln2_gain,
    ln2_bias,
):
    z_high, own = lax.axis_index("zhi"), lax.axis_index(SLAB)
    devices = lax.axis_size(AXES)

    def exchange(value):
        return lax.all_to_all(value, SLAB, split_axis=0, concat_axis=0, tiled=True)

    got = exchange(pack(node_feats, pair_tiles, pair_count))
    before = shift(node_feats, 1, devices)
    after = shift(node_feats, -1, devices)
    tiles, before, after = lax.optimization_barrier((got[:, :TILE_ROWS], before, after))
    before_last, gathered = gather_rings(tiles)
    codes = got[::MEMBERS, TILE_ROWS:, : pair_tiles.shape[1]].astype(jnp.int32)
    start, early, count, pairs = pair_lists(codes.reshape(SLAB_GROUPS, -1), z_high)

    def mine(value):
        return lax.dynamic_slice_in_dim(value, own, 1, 0)

    fill = jnp.full((ROWS,), -1, jnp.int32)
    ids = jnp.concatenate([fill, graph_ids, fill])
    key_ids = lax.dynamic_slice_in_dim(ids, (z_high * SLAB_BLOCKS + own) * ROWS, 3 * ROWS, 0)
    query_ids = jnp.tile(key_ids[ROWS : 2 * ROWS], 2)[None, :]
    early_held = exchange(select(EARLY, start, pairs, before_last))
    left = count - early

    def fetch(at):
        held = exchange(select(LATE, start + early + jnp.minimum(at, left), pairs, gathered))
        return jnp.clip(mine(left) - at, 0, LATE), held

    part, held = fetch(jnp.int32(0))
    query, *state = near(
        before, node_feats, after, w_query, w_key, w_value, key_ids[:, None], query_ids
    )
    state = far(mine(early), early_held, query, w_key, w_value, state)

    def close(part, held, state):
        return finish(
            part,
            held,
            query,
            w_key,
            w_value,
            state,
            node_feats,
            ln1_gain,
            ln1_bias,
            b_up,
            ln2_gain,
            ln2_bias,
            w_out,
            w_up,
            w_down,
        )

    out, *state = close(part, held, state)
    most = jnp.max(left)

    def go_on(state):
        def more(carry):
            at, state = carry
            part, held = fetch(at)
            return at + LATE, tuple(far(part, held, query, w_key, w_value, state))

        _, state = lax.while_loop(lambda carry: carry[0] < most, more, (jnp.int32(LATE), state))
        return close(jnp.zeros_like(part), held, state)[0]

    return lax.cond(most > LATE, go_on, lambda state: out, tuple(state))


def solution(mesh):
    inner = Mesh(mesh.devices.reshape(-1, 2, 2, 2, 4, 2), AXES)
    blk = ("zhi", "zlo", "ylo")
    in_specs = (P(AXES, None), P(), P(blk, None, None), P(blk, None)) + (P(),) * 11
    return jax.shard_map(
        on_device, mesh=inner, in_specs=in_specs, out_specs=P(AXES, None), check_vma=False
    )
```

```python
import jax
import jax.numpy as jnp
from jax import lax
from jax.experimental import pallas as pl
from jax.experimental.pallas import tpu as pltpu
from jax.sharding import Mesh
from jax.sharding import PartitionSpec as P

F32 = jnp.float32
BF16 = jnp.bfloat16

AXES = ("zhi", "zlo", "ylo", "yhi", "x", "core")
SLAB = ("zlo", "ylo", "yhi", "x", "core")
D = 512
FF = 1024
HEADS = 8
HEAD_DIM = 64
COUPLES = HEADS // 2
ROWS = 128
MEMBERS = 16
SLAB_GROUPS = 4
SLAB_BLOCKS = 64
CAP = 8
TILE_ROWS = 8
TILE_COLS = 128
COL_TILES = D // TILE_COLS
SLOTS = 16
GULP = 4
MIB = 1024 * 1024
FLOOR = -1e30

SMEM = pl.BlockSpec(memory_space=pltpu.SMEM)
VMEM = pl.BlockSpec(memory_space=pltpu.VMEM)


def absorb(state, keys, values, query_ref, mask, bias=()):
    new = []
    for couple in range(COUPLES):
        top, total, accum = state[couple]
        cols = slice(couple * 2 * HEAD_DIM, (couple + 1) * 2 * HEAD_DIM)
        scores = jnp.dot(keys[:, cols], query_ref[couple], preferred_element_type=F32)
        if mask is not None:
            scores = jnp.where(mask, scores, FLOOR)
        if bias:
            scores = jnp.concatenate(
                [scores[n * ROWS : (n + 1) * ROWS] + part for n, part in enumerate(bias)], axis=0
            )
        new_top = jnp.maximum(top, jnp.max(scores, axis=0, keepdims=True))
        decay = jnp.exp(top - new_top)
        prob = jnp.exp(scores - new_top)
        total = total * decay + jnp.sum(prob, axis=0, keepdims=True)
        part = lax.dot_general(
            values[:, cols],
            prob.astype(BF16),
            (((0,), (0,)), ((), ())),
            preferred_element_type=F32,
        )
        accum = jnp.concatenate(
            [
                accum[:HEAD_DIM] * decay[:, :ROWS] + part[:HEAD_DIM, :ROWS],
                accum[HEAD_DIM:] * decay[:, ROWS:] + part[HEAD_DIM:, ROWS:],
            ],
            axis=0,
        )
        new.append((new_top, total, accum))
    return new


def read_state(top_ref, total_ref, accum_ref):
    return [
        (
            top_ref[c : c + 1, :],
            total_ref[c : c + 1, :],
            accum_ref[c * 2 * HEAD_DIM : (c + 1) * 2 * HEAD_DIM, :],
        )
        for c in range(COUPLES)
    ]


def write_state(state, top_ref, total_ref, accum_ref):
    for c, (top, total, accum) in enumerate(state):
        top_ref[c : c + 1, :] = top
        total_ref[c : c + 1, :] = total
        accum_ref[c * 2 * HEAD_DIM : (c + 1) * 2 * HEAD_DIM, :] = accum


def project(x, weight_ref):
    return jnp.dot(x, weight_ref[...], preferred_element_type=F32).astype(BF16)


STATE_SHAPES = (
    jax.ShapeDtypeStruct((COUPLES, 2 * ROWS), F32),
    jax.ShapeDtypeStruct((COUPLES, 2 * ROWS), F32),
    jax.ShapeDtypeStruct((D, ROWS), F32),
)


def near_kernel(
    before_ref, x_ref, after_ref, wq_ref, wk_ref, wv_ref, kid_ref, qid_ref, query_ref, top_ref, total_ref, accum_ref
):
    x = x_ref[...]
    query = jnp.dot(x, wq_ref[...], preferred_element_type=F32).astype(BF16).astype(F32)
    query_t = (query.T * (1.0 / 8.0)).astype(BF16)
    zero = jnp.zeros((HEAD_DIM, ROWS), BF16)
    for couple in range(COUPLES):
        at = couple * 2 * HEAD_DIM
        first = query_t[at : at + HEAD_DIM]
        second = query_t[at + HEAD_DIM : at + 2 * HEAD_DIM]
        query_ref[couple] = jnp.concatenate(
            [jnp.concatenate([first, zero], axis=1), jnp.concatenate([zero, second], axis=1)], axis=0
        )
    state = [
        (
            jnp.full((1, 2 * ROWS), FLOOR, F32),
            jnp.zeros((1, 2 * ROWS), F32),
            jnp.zeros((2 * HEAD_DIM, ROWS), F32),
        )
    ] * COUPLES
    sources = jnp.concatenate([before_ref[...], x, after_ref[...]], axis=0)
    mask = kid_ref[...] == qid_ref[...]
    state = absorb(state, project(sources, wk_ref), project(sources, wv_ref), query_ref, mask)
    write_state(state, top_ref, total_ref, accum_ref)


def near(before, x, after, wq, wk, wv, key_ids, query_ids):
    return pl.pallas_call(
        near_kernel,
        out_shape=(jax.ShapeDtypeStruct((COUPLES, 2 * HEAD_DIM, 2 * ROWS), BF16),) + STATE_SHAPES,
        compiler_params=pltpu.CompilerParams(vmem_limit_bytes=32 * MIB),
        cost_estimate=pl.CostEstimate(flops=10**9, bytes_accessed=3 * MIB, transcendentals=400000),
        name="near",
    )(before, x, after, wq, wk, wv, key_ids, query_ids)


def pack_kernel(x_ref, tiles_ref, counts_ref, out_ref):
    x = x_ref[...].astype(F32)
    used = lax.broadcasted_iota(jnp.int32, tiles_ref.shape, 0) < counts_ref[...]
    codes = jnp.where(used, tiles_ref[...], MEMBERS * MEMBERS).astype(F32)
    codes = jnp.concatenate([codes, jnp.zeros((CAP, TILE_COLS - codes.shape[1]), F32)], axis=1)
    for n in range(SLAB_BLOCKS):
        row, col = n // COL_TILES * TILE_ROWS, n % COL_TILES * TILE_COLS
        tile = x[row : row + TILE_ROWS, col : col + TILE_COLS]
        out_ref[n] = jnp.concatenate([tile, codes], axis=0).astype(BF16)


def pack(x, pair_tiles, pair_count):
    return pl.pallas_call(
        pack_kernel,
        out_shape=jax.ShapeDtypeStruct((SLAB_BLOCKS, TILE_ROWS + CAP, TILE_COLS), BF16),
        compiler_params=pltpu.CompilerParams(vmem_limit_bytes=60 * MIB),
        name="pack",
    )(x, pair_tiles[0].T, pair_count)


def select_kernel(at_ref, list_ref, *refs):
    sources, out_ref, all_ref = refs[:-2], refs[-2], refs[-1]
    at = 0
    for source in sources:
        all_ref[at : at + source.shape[0]] = source[...]
        at += source.shape[0]

    def one(dest, carry):
        at = at_ref[dest]
        for slot in range(SLOTS):
            out_ref[dest, slot] = all_ref[list_ref[at + slot]]
        return carry

    lax.fori_loop(0, SLAB_BLOCKS, one, 0, unroll=4)


def select(at, pairs, gathered):
    return pl.pallas_call(
        select_kernel,
        in_specs=[SMEM] * 2 + [VMEM] * len(gathered),
        out_specs=VMEM,
        out_shape=jax.ShapeDtypeStruct((SLAB_BLOCKS, SLOTS, TILE_ROWS, TILE_COLS), BF16),
        scratch_shapes=[pltpu.VMEM((sum(g.shape[0] for g in gathered), TILE_ROWS, TILE_COLS), BF16)],
        compiler_params=pltpu.CompilerParams(vmem_limit_bytes=32 * MIB),
        cost_estimate=pl.CostEstimate(flops=0, bytes_accessed=8 * MIB, transcendentals=0),
        name="select",
    )(at, pairs, *gathered)


def gather_block(held_ref, slot):
    rows = []
    for r in range(ROWS // TILE_ROWS):
        tiles = [held_ref[r * COL_TILES + c, slot].astype(F32) for c in range(COL_TILES)]
        rows.append(jnp.concatenate(tiles, axis=1))
    return jnp.concatenate(rows, axis=0).astype(BF16)


def far_steps(count, held_ref, query_ref, wk_ref, wv_ref, state_refs):
    def step(i, carry):
        slots = [GULP * i + u for u in range(GULP)]
        x = jnp.concatenate([gather_block(held_ref, slot) for slot in slots], axis=0)
        bias = [jnp.where(slot < count, 0.0, FLOOR).astype(F32) for slot in slots]
        state = read_state(*state_refs)
        state = absorb(state, project(x, wk_ref), project(x, wv_ref), query_ref, None, bias)
        write_state(state, *state_refs)
        return carry

    lax.fori_loop(0, (count + GULP - 1) // GULP, step, 0)


def far_kernel(
    count_ref, held_ref, query_ref, wk_ref, wv_ref, top_in, total_in, accum_in, top_ref, total_ref, accum_ref
):
    top_ref[...] = top_in[...]
    total_ref[...] = total_in[...]
    accum_ref[...] = accum_in[...]
    far_steps(count_ref[0], held_ref, query_ref, wk_ref, wv_ref, (top_ref, total_ref, accum_ref))


def far(count, held, query, wk, wv, state):
    return pl.pallas_call(
        far_kernel,
        in_specs=[SMEM] + [VMEM] * 7,
        out_specs=(VMEM,) * 3,
        out_shape=STATE_SHAPES,
        compiler_params=pltpu.CompilerParams(vmem_limit_bytes=32 * MIB),
        name="far",
    )(count, held, query, wk, wv, *state)


def layer_norm(value, gain, bias):
    mean = jnp.mean(value, -1, keepdims=True)
    centred = value - mean
    spread = jnp.mean(centred * centred, -1, keepdims=True)
    return centred * lax.rsqrt(spread + 1e-05) * gain + bias


def finish_kernel(
    count_ref,
    held_ref,
    query_ref,
    wk_ref,
    wv_ref,
    top_in,
    total_in,
    accum_in,
    x_ref,
    g1_ref,
    b1_ref,
    b_up_ref,
    g2_ref,
    b2_ref,
    w_out_hbm,
    w_up_hbm,
    w_down_hbm,
    out_ref,
    top_ref,
    total_ref,
    accum_ref,
    w_out_ref,
    w_up_ref,
    w_down_ref,
    sems,
):
    weights = ((w_out_hbm, w_out_ref), (w_up_hbm, w_up_ref), (w_down_hbm, w_down_ref))
    copies = [pltpu.make_async_copy(a, b, sems.at[n]) for n, (a, b) in enumerate(weights)]
    for copy in copies:
        copy.start()
    far_kernel(
        count_ref,
        held_ref,
        query_ref,
        wk_ref,
        wv_ref,
        top_in,
        total_in,
        accum_in,
        top_ref,
        total_ref,
        accum_ref,
    )
    columns = []
    for head in range(HEADS):
        lanes = slice(head % 2 * ROWS, (head % 2 + 1) * ROWS)
        total = total_ref[head // 2 : head // 2 + 1, lanes]
        accum = accum_ref[head * HEAD_DIM : (head + 1) * HEAD_DIM, :]
        columns.append((accum / total).astype(BF16))
    attended_t = jnp.concatenate(columns, axis=0)
    copies[0].wait()
    mixed = x_ref[...].astype(F32) + lax.dot_general(
        attended_t, w_out_ref[...], (((0,), (0,)), ((), ())), preferred_element_type=F32
    )
    normed = layer_norm(mixed, g1_ref[...], b1_ref[...]).astype(BF16)
    copies[1].wait()
    hidden = jnp.maximum(
        jnp.dot(normed, w_up_ref[...], preferred_element_type=F32) + b_up_ref[...], 0.0
    ).astype(BF16)
    copies[2].wait()
    second = normed.astype(F32) + jnp.dot(hidden, w_down_ref[...], preferred_element_type=F32)
    out_ref[...] = layer_norm(second, g2_ref[...], b2_ref[...])


def finish(count, held, query, wk, wv, state, x, g1, b1, b_up, g2, b2, w_out, w_up, w_down):
    hbm = pl.BlockSpec(memory_space=pltpu.HBM)
    return pl.pallas_call(
        finish_kernel,
        in_specs=[SMEM] + [VMEM] * 13 + [hbm] * 3,
        out_specs=(VMEM,) * 4,
        out_shape=(jax.ShapeDtypeStruct((ROWS, D), F32),) + STATE_SHAPES,
        scratch_shapes=[
            pltpu.VMEM((D, D), BF16),
            pltpu.VMEM((D, FF), BF16),
            pltpu.VMEM((FF, D), BF16),
            pltpu.SemaphoreType.DMA((3,)),
        ],
        compiler_params=pltpu.CompilerParams(vmem_limit_bytes=44 * MIB),
        cost_estimate=pl.CostEstimate(flops=4 * 10**9, bytes_accessed=8 * MIB, transcendentals=10**6),
        name="finish",
    )(
        count,
        held,
        query,
        wk,
        wv,
        *state,
        x,
        g1[None],
        b1[None],
        b_up[None],
        g2[None],
        b2[None],
        w_out,
        w_up,
        w_down,
    )


def pair_lists(held, z_high):
    size = held.shape[1]
    planes = lax.axis_size("zhi")
    slot = jnp.arange(size, dtype=jnp.int32)
    key_group = slot % (size // CAP)
    distance = (z_high - key_group // SLAB_GROUPS) % planes
    query_index = held // MEMBERS
    key_slot = (distance * SLAB_BLOCKS + key_group % SLAB_GROUPS * MEMBERS)[None, :] + held % MEMBERS
    ahead = (query_index[:, None, :] < query_index[:, :, None]) | (
        (query_index[:, None, :] == query_index[:, :, None]) & (slot[None, None, :] < slot[None, :, None])
    )
    place = jnp.sum(ahead.astype(jnp.int32), axis=-1)
    pairs = jnp.sum(jnp.where(place[:, None, :] == slot[None, :, None], key_slot[:, None, :], 0), axis=-1)
    pairs = jnp.concatenate([pairs.reshape(-1), jnp.zeros((SLOTS,), jnp.int32)])
    member = jnp.arange(MEMBERS, dtype=jnp.int32)[None, :, None]
    start = jnp.sum((query_index[:, None, :] < member).astype(jnp.int32), axis=-1)
    count = jnp.sum((query_index[:, None, :] == member).astype(jnp.int32), axis=-1)
    start = start + size * jnp.arange(SLAB_GROUPS, dtype=jnp.int32)[:, None]
    return start.reshape(-1), count.reshape(-1), pairs


def gather_rings(tiles):
    size = lax.axis_size("zhi")
    assert size == 8

    def move(value, steps):
        return lax.ppermute(value, "zhi", [(z, (z + steps) % size) for z in range(size)])

    below_two, above_two = move(tiles, 2), move(tiles, -2)
    below_one, above_one = move(tiles, 1), move(tiles, -1)
    half = tiles.shape[0] // 2
    below_three, above_three = move(below_two, 1), move(above_two, -1)
    first_half, second_half = move(below_two[:half], 2), move(above_two[half:], -2)
    return [
        tiles,
        below_one,
        below_two,
        below_three,
        first_half,
        second_half,
        above_three,
        above_two,
        above_one,
    ]


def shift(x, step, size):
    pairs = [(i, i + step) for i in range(size) if 0 <= i + step < size]
    return lax.ppermute(x, AXES, pairs)


def on_device(
    node_feats,
    graph_ids,
    pair_tiles,
    pair_count,
    w_query,
    w_key,
    w_value,
    w_out,
    ln1_gain,
    ln1_bias,
    w_up,
    b_up,
    w_down,
    ln2_gain,
    ln2_bias,
):
    z_high, own = lax.axis_index("zhi"), lax.axis_index(SLAB)
    devices = lax.axis_size(AXES)

    def exchange(value):
        return lax.all_to_all(value, SLAB, split_axis=0, concat_axis=0, tiled=True)

    got = exchange(pack(node_feats, pair_tiles, pair_count))
    before = shift(node_feats, 1, devices)
    after = shift(node_feats, -1, devices)
    tiles, before, after = lax.optimization_barrier((got[:, :TILE_ROWS], before, after))
    gathered = gather_rings(tiles)
    codes = got[::MEMBERS, TILE_ROWS:, : pair_tiles.shape[1]].astype(jnp.int32)
    start, count, pairs = pair_lists(codes.reshape(SLAB_GROUPS, -1), z_high)

    def mine(value):
        return lax.dynamic_slice_in_dim(value, own, 1, 0)

    fill = jnp.full((ROWS,), -1, jnp.int32)
    ids = jnp.concatenate([fill, graph_ids, fill])
    key_ids = lax.dynamic_slice_in_dim(ids, (z_high * SLAB_BLOCKS + own) * ROWS, 3 * ROWS, 0)
    query_ids = jnp.tile(key_ids[ROWS : 2 * ROWS], 2)[None, :]
    query, *state = near(
        before, node_feats, after, w_query, w_key, w_value, key_ids[:, None], query_ids
    )

    def fetch(at):
        held = exchange(select(start + jnp.minimum(at, count), pairs, gathered))
        return jnp.clip(mine(count) - at, 0, SLOTS), held

    def close(part, held, state):
        return finish(
            part,
            held,
            query,
            w_key,
            w_value,
            state,
            node_feats,
            ln1_gain,
            ln1_bias,
            b_up,
            ln2_gain,
            ln2_bias,
            w_out,
            w_up,
            w_down,
        )

    part, held = fetch(jnp.int32(0))
    out, *state = close(part, held, state)
    most = jnp.max(count)

    def go_on(state):
        def more(carry):
            at, state = carry
            part, held = fetch(at)
            return at + SLOTS, tuple(far(part, held, query, w_key, w_value, state))

        _, state = lax.while_loop(lambda carry: carry[0] < most, more, (jnp.int32(SLOTS), state))
        return close(jnp.zeros_like(part), held, state)[0]

    return lax.cond(most > SLOTS, go_on, lambda state: out, tuple(state))


def solution(mesh):
    inner = Mesh(mesh.devices.reshape(-1, 2, 2, 2, 4, 2), AXES)
    blk = ("zhi", "zlo", "ylo")
    in_specs = (P(AXES, None), P(), P(blk, None, None), P(blk, None)) + (P(),) * 11
    return jax.shard_map(
        on_device, mesh=inner, in_specs=in_specs, out_specs=P(AXES, None), check_vma=False
    )
```

```python
import jax
import jax.numpy as jnp
from jax import lax
from jax.experimental import pallas as pl
from jax.experimental.pallas import tpu as pltpu
from jax.sharding import Mesh
from jax.sharding import PartitionSpec as P

F32 = jnp.float32
BF16 = jnp.bfloat16

AXES = ("zhi", "zlo", "ylo", "yhi", "x", "core")
SLAB = ("zlo", "ylo", "yhi", "x", "core")
D = 512
FF = 1024
HEADS = 8
HEAD_DIM = 64
COUPLES = HEADS // 2
ROWS = 128
MEMBERS = 16
SLAB_GROUPS = 4
SLAB_BLOCKS = 64
CAP = 8
TILE_ROWS = 8
TILE_COLS = 128
COL_TILES = D // TILE_COLS
SLOTS = 16
GULP = 4
MIB = 1024 * 1024
FLOOR = -1e30

SMEM = pl.BlockSpec(memory_space=pltpu.SMEM)
VMEM = pl.BlockSpec(memory_space=pltpu.VMEM)


def absorb(state, keys, values, query_ref, mask, bias=()):
    new = []
    for couple in range(COUPLES):
        top, total, accum = state[couple]
        cols = slice(couple * 2 * HEAD_DIM, (couple + 1) * 2 * HEAD_DIM)
        scores = jnp.dot(keys[:, cols], query_ref[couple], preferred_element_type=F32)
        if mask is not None:
            scores = jnp.where(mask, scores, FLOOR)
        if bias:
            scores = jnp.concatenate(
                [scores[n * ROWS : (n + 1) * ROWS] + part for n, part in enumerate(bias)], axis=0
            )
        new_top = jnp.maximum(top, jnp.max(scores, axis=0, keepdims=True))
        decay = jnp.exp(top - new_top)
        prob = jnp.exp(scores - new_top)
        total = total * decay + jnp.sum(prob, axis=0, keepdims=True)
        part = lax.dot_general(
            values[:, cols],
            prob.astype(BF16),
            (((0,), (0,)), ((), ())),
            preferred_element_type=F32,
        )
        accum = jnp.concatenate(
            [
                accum[:HEAD_DIM] * decay[:, :ROWS] + part[:HEAD_DIM, :ROWS],
                accum[HEAD_DIM:] * decay[:, ROWS:] + part[HEAD_DIM:, ROWS:],
            ],
            axis=0,
        )
        new.append((new_top, total, accum))
    return new


def read_state(top_ref, total_ref, accum_ref):
    return [
        (
            top_ref[c : c + 1, :],
            total_ref[c : c + 1, :],
            accum_ref[c * 2 * HEAD_DIM : (c + 1) * 2 * HEAD_DIM, :],
        )
        for c in range(COUPLES)
    ]


def write_state(state, top_ref, total_ref, accum_ref):
    for c, (top, total, accum) in enumerate(state):
        top_ref[c : c + 1, :] = top
        total_ref[c : c + 1, :] = total
        accum_ref[c * 2 * HEAD_DIM : (c + 1) * 2 * HEAD_DIM, :] = accum


def project(x, weight_ref):
    return jnp.dot(x, weight_ref[...], preferred_element_type=F32).astype(BF16)


STATE_SHAPES = (
    jax.ShapeDtypeStruct((COUPLES, 2 * ROWS), F32),
    jax.ShapeDtypeStruct((COUPLES, 2 * ROWS), F32),
    jax.ShapeDtypeStruct((D, ROWS), F32),
)


def near_kernel(
    before_ref, x_ref, after_ref, wq_ref, wk_ref, wv_ref, kid_ref, qid_ref, query_ref, top_ref, total_ref, accum_ref
):
    x = x_ref[...]
    query = jnp.dot(x, wq_ref[...], preferred_element_type=F32).astype(BF16).astype(F32)
    query_t = (query.T * (1.0 / 8.0)).astype(BF16)
    zero = jnp.zeros((HEAD_DIM, ROWS), BF16)
    for couple in range(COUPLES):
        at = couple * 2 * HEAD_DIM
        first = query_t[at : at + HEAD_DIM]
        second = query_t[at + HEAD_DIM : at + 2 * HEAD_DIM]
        query_ref[couple] = jnp.concatenate(
            [jnp.concatenate([first, zero], axis=1), jnp.concatenate([zero, second], axis=1)], axis=0
        )
    state = [
        (
            jnp.full((1, 2 * ROWS), FLOOR, F32),
            jnp.zeros((1, 2 * ROWS), F32),
            jnp.zeros((2 * HEAD_DIM, ROWS), F32),
        )
    ] * COUPLES
    sources = jnp.concatenate([before_ref[...], x, after_ref[...]], axis=0)
    mask = kid_ref[...] == qid_ref[...]
    state = absorb(state, project(sources, wk_ref), project(sources, wv_ref), query_ref, mask)
    write_state(state, top_ref, total_ref, accum_ref)


def near(before, x, after, wq, wk, wv, key_ids, query_ids):
    return pl.pallas_call(
        near_kernel,
        out_shape=(jax.ShapeDtypeStruct((COUPLES, 2 * HEAD_DIM, 2 * ROWS), BF16),) + STATE_SHAPES,
        compiler_params=pltpu.CompilerParams(vmem_limit_bytes=32 * MIB),
        cost_estimate=pl.CostEstimate(flops=10**9, bytes_accessed=3 * MIB, transcendentals=400000),
        name="near",
    )(before, x, after, wq, wk, wv, key_ids, query_ids)


def pack_kernel(x_ref, tiles_ref, counts_ref, out_ref):
    x = x_ref[...].astype(F32)
    used = lax.broadcasted_iota(jnp.int32, tiles_ref.shape, 0) < counts_ref[...]
    codes = jnp.where(used, tiles_ref[...], MEMBERS * MEMBERS).astype(F32)
    codes = jnp.concatenate([codes, jnp.zeros((CAP, TILE_COLS - codes.shape[1]), F32)], axis=1)
    for n in range(SLAB_BLOCKS):
        row, col = n // COL_TILES * TILE_ROWS, n % COL_TILES * TILE_COLS
        tile = x[row : row + TILE_ROWS, col : col + TILE_COLS]
        out_ref[n] = jnp.concatenate([tile, codes], axis=0).astype(BF16)


def pack(x, pair_tiles, pair_count):
    return pl.pallas_call(
        pack_kernel,
        out_shape=jax.ShapeDtypeStruct((SLAB_BLOCKS, TILE_ROWS + CAP, TILE_COLS), BF16),
        compiler_params=pltpu.CompilerParams(vmem_limit_bytes=60 * MIB),
        name="pack",
    )(x, pair_tiles[0].T, pair_count)


def select_kernel(at_ref, list_ref, all_ref, out_ref):
    def one(dest, carry):
        at = at_ref[dest]
        for slot in range(SLOTS):
            out_ref[dest, slot] = all_ref[list_ref[at + slot]]
        return carry

    lax.fori_loop(0, SLAB_BLOCKS, one, 0, unroll=4)


def select(at, pairs, gathered):
    return pl.pallas_call(
        select_kernel,
        in_specs=[SMEM] * 2 + [VMEM],
        out_specs=VMEM,
        out_shape=jax.ShapeDtypeStruct((SLAB_BLOCKS, SLOTS, TILE_ROWS, TILE_COLS), BF16),
        compiler_params=pltpu.CompilerParams(vmem_limit_bytes=32 * MIB),
        cost_estimate=pl.CostEstimate(flops=0, bytes_accessed=8 * MIB, transcendentals=0),
        name="select",
    )(at, pairs, gathered)


def gather_block(held_ref, slot):
    rows = []
    for r in range(ROWS // TILE_ROWS):
        tiles = [held_ref[r * COL_TILES + c, slot].astype(F32) for c in range(COL_TILES)]
        rows.append(jnp.concatenate(tiles, axis=1))
    return jnp.concatenate(rows, axis=0).astype(BF16)


def far_steps(count, held_ref, query_ref, wk_ref, wv_ref, state_refs):
    def step(i, carry):
        slots = [GULP * i + u for u in range(GULP)]
        x = jnp.concatenate([gather_block(held_ref, slot) for slot in slots], axis=0)
        bias = [jnp.where(slot < count, 0.0, FLOOR).astype(F32) for slot in slots]
        state = read_state(*state_refs)
        state = absorb(state, project(x, wk_ref), project(x, wv_ref), query_ref, None, bias)
        write_state(state, *state_refs)
        return carry

    lax.fori_loop(0, (count + GULP - 1) // GULP, step, 0)


def far_kernel(
    count_ref, held_ref, query_ref, wk_ref, wv_ref, top_in, total_in, accum_in, top_ref, total_ref, accum_ref
):
    top_ref[...] = top_in[...]
    total_ref[...] = total_in[...]
    accum_ref[...] = accum_in[...]
    far_steps(count_ref[0], held_ref, query_ref, wk_ref, wv_ref, (top_ref, total_ref, accum_ref))


def far(count, held, query, wk, wv, state):
    return pl.pallas_call(
        far_kernel,
        in_specs=[SMEM] + [VMEM] * 7,
        out_specs=(VMEM,) * 3,
        out_shape=STATE_SHAPES,
        compiler_params=pltpu.CompilerParams(vmem_limit_bytes=32 * MIB),
        name="far",
    )(count, held, query, wk, wv, *state)


def layer_norm(value, gain, bias):
    mean = jnp.mean(value, -1, keepdims=True)
    centred = value - mean
    spread = jnp.mean(centred * centred, -1, keepdims=True)
    return centred * lax.rsqrt(spread + 1e-05) * gain + bias


def finish_kernel(
    count_ref,
    held_ref,
    query_ref,
    wk_ref,
    wv_ref,
    top_in,
    total_in,
    accum_in,
    x_ref,
    g1_ref,
    b1_ref,
    b_up_ref,
    g2_ref,
    b2_ref,
    w_out_hbm,
    w_up_hbm,
    w_down_hbm,
    out_ref,
    top_ref,
    total_ref,
    accum_ref,
    w_out_ref,
    w_up_ref,
    w_down_ref,
    sems,
):
    weights = ((w_out_hbm, w_out_ref), (w_up_hbm, w_up_ref), (w_down_hbm, w_down_ref))
    copies = [pltpu.make_async_copy(a, b, sems.at[n]) for n, (a, b) in enumerate(weights)]
    for copy in copies:
        copy.start()
    far_kernel(
        count_ref,
        held_ref,
        query_ref,
        wk_ref,
        wv_ref,
        top_in,
        total_in,
        accum_in,
        top_ref,
        total_ref,
        accum_ref,
    )
    columns = []
    for head in range(HEADS):
        lanes = slice(head % 2 * ROWS, (head % 2 + 1) * ROWS)
        total = total_ref[head // 2 : head // 2 + 1, lanes]
        accum = accum_ref[head * HEAD_DIM : (head + 1) * HEAD_DIM, :]
        columns.append((accum / total).astype(BF16))
    attended_t = jnp.concatenate(columns, axis=0)
    copies[0].wait()
    mixed = x_ref[...].astype(F32) + lax.dot_general(
        attended_t, w_out_ref[...], (((0,), (0,)), ((), ())), preferred_element_type=F32
    )
    normed = layer_norm(mixed, g1_ref[...], b1_ref[...]).astype(BF16)
    copies[1].wait()
    hidden = jnp.maximum(
        jnp.dot(normed, w_up_ref[...], preferred_element_type=F32) + b_up_ref[...], 0.0
    ).astype(BF16)
    copies[2].wait()
    second = normed.astype(F32) + jnp.dot(hidden, w_down_ref[...], preferred_element_type=F32)
    out_ref[...] = layer_norm(second, g2_ref[...], b2_ref[...])


def finish(count, held, query, wk, wv, state, x, g1, b1, b_up, g2, b2, w_out, w_up, w_down):
    hbm = pl.BlockSpec(memory_space=pltpu.HBM)
    return pl.pallas_call(
        finish_kernel,
        in_specs=[SMEM] + [VMEM] * 13 + [hbm] * 3,
        out_specs=(VMEM,) * 4,
        out_shape=(jax.ShapeDtypeStruct((ROWS, D), F32),) + STATE_SHAPES,
        scratch_shapes=[
            pltpu.VMEM((D, D), BF16),
            pltpu.VMEM((D, FF), BF16),
            pltpu.VMEM((FF, D), BF16),
            pltpu.SemaphoreType.DMA((3,)),
        ],
        compiler_params=pltpu.CompilerParams(vmem_limit_bytes=44 * MIB),
        cost_estimate=pl.CostEstimate(flops=4 * 10**9, bytes_accessed=8 * MIB, transcendentals=10**6),
        name="finish",
    )(
        count,
        held,
        query,
        wk,
        wv,
        *state,
        x,
        g1[None],
        b1[None],
        b_up[None],
        g2[None],
        b2[None],
        w_out,
        w_up,
        w_down,
    )


def pair_lists(held):
    size = held.shape[1]
    slot = jnp.arange(size, dtype=jnp.int32)
    key_group = slot % (size // CAP)
    query_index = held // MEMBERS
    key_slot = (key_group * MEMBERS)[None, :] + held % MEMBERS
    ahead = (query_index[:, None, :] < query_index[:, :, None]) | (
        (query_index[:, None, :] == query_index[:, :, None]) & (slot[None, None, :] < slot[None, :, None])
    )
    place = jnp.sum(ahead.astype(jnp.int32), axis=-1)
    pairs = jnp.sum(jnp.where(place[:, None, :] == slot[None, :, None], key_slot[:, None, :], 0), axis=-1)
    pairs = jnp.concatenate([pairs.reshape(-1), jnp.zeros((SLOTS,), jnp.int32)])
    member = jnp.arange(MEMBERS, dtype=jnp.int32)[None, :, None]
    start = jnp.sum((query_index[:, None, :] < member).astype(jnp.int32), axis=-1)
    count = jnp.sum((query_index[:, None, :] == member).astype(jnp.int32), axis=-1)
    start = start + size * jnp.arange(SLAB_GROUPS, dtype=jnp.int32)[:, None]
    return start.reshape(-1), count.reshape(-1), pairs


def shift(x, step, size):
    pairs = [(i, i + step) for i in range(size) if 0 <= i + step < size]
    return lax.ppermute(x, AXES, pairs)


def on_device(
    node_feats,
    graph_ids,
    pair_tiles,
    pair_count,
    w_query,
    w_key,
    w_value,
    w_out,
    ln1_gain,
    ln1_bias,
    w_up,
    b_up,
    w_down,
    ln2_gain,
    ln2_bias,
):
    z_high, own = lax.axis_index("zhi"), lax.axis_index(SLAB)
    devices = lax.axis_size(AXES)

    def exchange(value):
        return lax.all_to_all(value, SLAB, split_axis=0, concat_axis=0, tiled=True)

    got = exchange(pack(node_feats, pair_tiles, pair_count))
    gathered = lax.all_gather(got[:, :TILE_ROWS], "zhi", axis=0, tiled=True)
    before = shift(node_feats, 1, devices)
    after = shift(node_feats, -1, devices)
    codes = got[::MEMBERS, TILE_ROWS:, : pair_tiles.shape[1]].astype(jnp.int32)
    start, count, pairs = pair_lists(codes.reshape(SLAB_GROUPS, -1))

    def mine(value):
        return lax.dynamic_slice_in_dim(value, own, 1, 0)

    fill = jnp.full((ROWS,), -1, jnp.int32)
    ids = jnp.concatenate([fill, graph_ids, fill])
    key_ids = lax.dynamic_slice_in_dim(ids, (z_high * SLAB_BLOCKS + own) * ROWS, 3 * ROWS, 0)
    query_ids = jnp.tile(key_ids[ROWS : 2 * ROWS], 2)[None, :]
    query, *state = near(
        before, node_feats, after, w_query, w_key, w_value, key_ids[:, None], query_ids
    )

    def fetch(at):
        held = exchange(select(start + jnp.minimum(at, count), pairs, gathered))
        return jnp.clip(mine(count) - at, 0, SLOTS), held

    def close(part, held, state):
        return finish(
            part,
            held,
            query,
            w_key,
            w_value,
            state,
            node_feats,
            ln1_gain,
            ln1_bias,
            b_up,
            ln2_gain,
            ln2_bias,
            w_out,
            w_up,
            w_down,
        )

    part, held = fetch(jnp.int32(0))
    out, *state = close(part, held, state)
    most = jnp.max(count)

    def go_on(state):
        def more(carry):
            at, state = carry
            part, held = fetch(at)
            return at + SLOTS, tuple(far(part, held, query, w_key, w_value, state))

        _, state = lax.while_loop(lambda carry: carry[0] < most, more, (jnp.int32(SLOTS), state))
        return close(jnp.zeros_like(part), held, state)[0]

    return lax.cond(most > SLOTS, go_on, lambda state: out, tuple(state))


def solution(mesh):
    inner = Mesh(mesh.devices.reshape(-1, 2, 2, 2, 4, 2), AXES)
    blk = ("zhi", "zlo", "ylo")
    in_specs = (P(AXES, None), P(), P(blk, None, None), P(blk, None)) + (P(),) * 11
    return jax.shard_map(
        on_device, mesh=inner, in_specs=in_specs, out_specs=P(AXES, None), check_vma=False
    )
```

```python
import jax
import jax.numpy as jnp
from jax import lax
from jax.experimental import pallas as pl
from jax.experimental.pallas import tpu as pltpu
from jax.sharding import Mesh
from jax.sharding import PartitionSpec as P

F32 = jnp.float32
BF16 = jnp.bfloat16

AXES = ("zhi", "zlo", "ylo", "yhi", "x", "core")
SLAB = ("zlo", "ylo", "yhi", "x", "core")
D = 512
FF = 1024
HEADS = 8
HEAD_DIM = 64
COUPLES = HEADS // 2
ROWS = 128
MEMBERS = 16
SLAB_GROUPS = 4
SLAB_BLOCKS = 64
CAP = 8
TILE_ROWS = 8
TILE_COLS = 128
COL_TILES = D // TILE_COLS
SLOTS = 16
GULP = 4
MIB = 1024 * 1024
FLOOR = -1e30

SMEM = pl.BlockSpec(memory_space=pltpu.SMEM)
VMEM = pl.BlockSpec(memory_space=pltpu.VMEM)


def absorb(state, keys, values, query_ref, mask, bias=()):
    new = []
    for couple in range(COUPLES):
        top, total, accum = state[couple]
        cols = slice(couple * 2 * HEAD_DIM, (couple + 1) * 2 * HEAD_DIM)
        scores = jnp.dot(keys[:, cols], query_ref[couple], preferred_element_type=F32)
        if mask is not None:
            scores = jnp.where(mask, scores, FLOOR)
        if bias:
            scores = jnp.concatenate(
                [scores[n * ROWS : (n + 1) * ROWS] + part for n, part in enumerate(bias)], axis=0
            )
        new_top = jnp.maximum(top, jnp.max(scores, axis=0, keepdims=True))
        decay = jnp.exp(top - new_top)
        prob = jnp.exp(scores - new_top)
        total = total * decay + jnp.sum(prob, axis=0, keepdims=True)
        part = lax.dot_general(
            values[:, cols],
            prob.astype(BF16),
            (((0,), (0,)), ((), ())),
            preferred_element_type=F32,
        )
        accum = jnp.concatenate(
            [
                accum[:HEAD_DIM] * decay[:, :ROWS] + part[:HEAD_DIM, :ROWS],
                accum[HEAD_DIM:] * decay[:, ROWS:] + part[HEAD_DIM:, ROWS:],
            ],
            axis=0,
        )
        new.append((new_top, total, accum))
    return new


def read_state(top_ref, total_ref, accum_ref):
    return [
        (
            top_ref[c : c + 1, :],
            total_ref[c : c + 1, :],
            accum_ref[c * 2 * HEAD_DIM : (c + 1) * 2 * HEAD_DIM, :],
        )
        for c in range(COUPLES)
    ]


def write_state(state, top_ref, total_ref, accum_ref):
    for c, (top, total, accum) in enumerate(state):
        top_ref[c : c + 1, :] = top
        total_ref[c : c + 1, :] = total
        accum_ref[c * 2 * HEAD_DIM : (c + 1) * 2 * HEAD_DIM, :] = accum


def project(x, weight_ref):
    return jnp.dot(x, weight_ref[...], preferred_element_type=F32).astype(BF16)


STATE_SHAPES = (
    jax.ShapeDtypeStruct((COUPLES, 2 * ROWS), F32),
    jax.ShapeDtypeStruct((COUPLES, 2 * ROWS), F32),
    jax.ShapeDtypeStruct((D, ROWS), F32),
)


def near_kernel(
    before_ref, x_ref, after_ref, wq_ref, wk_ref, wv_ref, kid_ref, qid_ref, query_ref, top_ref, total_ref, accum_ref
):
    x = x_ref[...]
    query = jnp.dot(x, wq_ref[...], preferred_element_type=F32).astype(BF16).astype(F32)
    query_t = (query.T * (1.0 / 8.0)).astype(BF16)
    zero = jnp.zeros((HEAD_DIM, ROWS), BF16)
    for couple in range(COUPLES):
        at = couple * 2 * HEAD_DIM
        first = query_t[at : at + HEAD_DIM]
        second = query_t[at + HEAD_DIM : at + 2 * HEAD_DIM]
        query_ref[couple] = jnp.concatenate(
            [jnp.concatenate([first, zero], axis=1), jnp.concatenate([zero, second], axis=1)], axis=0
        )
    state = [
        (
            jnp.full((1, 2 * ROWS), FLOOR, F32),
            jnp.zeros((1, 2 * ROWS), F32),
            jnp.zeros((2 * HEAD_DIM, ROWS), F32),
        )
    ] * COUPLES
    sources = jnp.concatenate([before_ref[...], x, after_ref[...]], axis=0)
    mask = kid_ref[...] == qid_ref[...]
    state = absorb(state, project(sources, wk_ref), project(sources, wv_ref), query_ref, mask)
    write_state(state, top_ref, total_ref, accum_ref)


def near(before, x, after, wq, wk, wv, key_ids, query_ids):
    return pl.pallas_call(
        near_kernel,
        out_shape=(jax.ShapeDtypeStruct((COUPLES, 2 * HEAD_DIM, 2 * ROWS), BF16),) + STATE_SHAPES,
        compiler_params=pltpu.CompilerParams(vmem_limit_bytes=32 * MIB),
        cost_estimate=pl.CostEstimate(flops=10**9, bytes_accessed=3 * MIB, transcendentals=400000),
        name="near",
    )(before, x, after, wq, wk, wv, key_ids, query_ids)


def pack_kernel(x_ref, tiles_ref, counts_ref, out_ref):
    x = x_ref[...].astype(F32)
    used = lax.broadcasted_iota(jnp.int32, tiles_ref.shape, 0) < counts_ref[...]
    codes = jnp.where(used, tiles_ref[...], MEMBERS * MEMBERS).astype(F32)
    codes = jnp.concatenate([codes, jnp.zeros((CAP, TILE_COLS - codes.shape[1]), F32)], axis=1)
    for n in range(SLAB_BLOCKS):
        row, col = n // COL_TILES * TILE_ROWS, n % COL_TILES * TILE_COLS
        tile = x[row : row + TILE_ROWS, col : col + TILE_COLS]
        out_ref[n] = jnp.concatenate([tile, codes], axis=0).astype(BF16)


def pack(x, pair_tiles, pair_count):
    return pl.pallas_call(
        pack_kernel,
        out_shape=jax.ShapeDtypeStruct((SLAB_BLOCKS, TILE_ROWS + CAP, TILE_COLS), BF16),
        compiler_params=pltpu.CompilerParams(vmem_limit_bytes=60 * MIB),
        name="pack",
    )(x, pair_tiles[0].T, pair_count)


def select_kernel(at_ref, list_ref, *refs):
    sources, out_ref, all_ref = refs[:-2], refs[-2], refs[-1]
    at = 0
    for source in sources:
        all_ref[at : at + source.shape[0]] = source[...]
        at += source.shape[0]

    def one(dest, carry):
        at = at_ref[dest]
        for slot in range(SLOTS):
            out_ref[dest, slot] = all_ref[list_ref[at + slot]]
        return carry

    lax.fori_loop(0, SLAB_BLOCKS, one, 0, unroll=4)


def select(at, pairs, gathered):
    return pl.pallas_call(
        select_kernel,
        in_specs=[SMEM] * 2 + [VMEM] * len(gathered),
        out_specs=VMEM,
        out_shape=jax.ShapeDtypeStruct((SLAB_BLOCKS, SLOTS, TILE_ROWS, TILE_COLS), BF16),
        scratch_shapes=[pltpu.VMEM((sum(g.shape[0] for g in gathered), TILE_ROWS, TILE_COLS), BF16)],
        compiler_params=pltpu.CompilerParams(vmem_limit_bytes=32 * MIB),
        cost_estimate=pl.CostEstimate(flops=0, bytes_accessed=8 * MIB, transcendentals=0),
        name="select",
    )(at, pairs, *gathered)


def gather_block(held_ref, slot):
    rows = []
    for r in range(ROWS // TILE_ROWS):
        tiles = [held_ref[r * COL_TILES + c, slot].astype(F32) for c in range(COL_TILES)]
        rows.append(jnp.concatenate(tiles, axis=1))
    return jnp.concatenate(rows, axis=0).astype(BF16)


def far_steps(count, held_ref, query_ref, wk_ref, wv_ref, state_refs):
    def step(i, carry):
        slots = [GULP * i + u for u in range(GULP)]
        x = jnp.concatenate([gather_block(held_ref, slot) for slot in slots], axis=0)
        bias = [jnp.where(slot < count, 0.0, FLOOR).astype(F32) for slot in slots]
        state = read_state(*state_refs)
        state = absorb(state, project(x, wk_ref), project(x, wv_ref), query_ref, None, bias)
        write_state(state, *state_refs)
        return carry

    lax.fori_loop(0, (count + GULP - 1) // GULP, step, 0)


def far_kernel(
    count_ref, held_ref, query_ref, wk_ref, wv_ref, top_in, total_in, accum_in, top_ref, total_ref, accum_ref
):
    top_ref[...] = top_in[...]
    total_ref[...] = total_in[...]
    accum_ref[...] = accum_in[...]
    far_steps(count_ref[0], held_ref, query_ref, wk_ref, wv_ref, (top_ref, total_ref, accum_ref))


def far(count, held, query, wk, wv, state):
    return pl.pallas_call(
        far_kernel,
        in_specs=[SMEM] + [VMEM] * 7,
        out_specs=(VMEM,) * 3,
        out_shape=STATE_SHAPES,
        compiler_params=pltpu.CompilerParams(vmem_limit_bytes=32 * MIB),
        name="far",
    )(count, held, query, wk, wv, *state)


def layer_norm(value, gain, bias):
    mean = jnp.mean(value, -1, keepdims=True)
    centred = value - mean
    spread = jnp.mean(centred * centred, -1, keepdims=True)
    return centred * lax.rsqrt(spread + 1e-05) * gain + bias


def finish_kernel(
    count_ref,
    held_ref,
    query_ref,
    wk_ref,
    wv_ref,
    top_in,
    total_in,
    accum_in,
    x_ref,
    g1_ref,
    b1_ref,
    b_up_ref,
    g2_ref,
    b2_ref,
    w_out_hbm,
    w_up_hbm,
    w_down_hbm,
    out_ref,
    top_ref,
    total_ref,
    accum_ref,
    w_out_ref,
    w_up_ref,
    w_down_ref,
    sems,
):
    weights = ((w_out_hbm, w_out_ref), (w_up_hbm, w_up_ref), (w_down_hbm, w_down_ref))
    copies = [pltpu.make_async_copy(a, b, sems.at[n]) for n, (a, b) in enumerate(weights)]
    for copy in copies:
        copy.start()
    far_kernel(
        count_ref,
        held_ref,
        query_ref,
        wk_ref,
        wv_ref,
        top_in,
        total_in,
        accum_in,
        top_ref,
        total_ref,
        accum_ref,
    )
    columns = []
    for head in range(HEADS):
        lanes = slice(head % 2 * ROWS, (head % 2 + 1) * ROWS)
        total = total_ref[head // 2 : head // 2 + 1, lanes]
        accum = accum_ref[head * HEAD_DIM : (head + 1) * HEAD_DIM, :]
        columns.append((accum / total).astype(BF16))
    attended_t = jnp.concatenate(columns, axis=0)
    copies[0].wait()
    mixed = x_ref[...].astype(F32) + lax.dot_general(
        attended_t, w_out_ref[...], (((0,), (0,)), ((), ())), preferred_element_type=F32
    )
    normed = layer_norm(mixed, g1_ref[...], b1_ref[...]).astype(BF16)
    copies[1].wait()
    hidden = jnp.maximum(
        jnp.dot(normed, w_up_ref[...], preferred_element_type=F32) + b_up_ref[...], 0.0
    ).astype(BF16)
    copies[2].wait()
    second = normed.astype(F32) + jnp.dot(hidden, w_down_ref[...], preferred_element_type=F32)
    out_ref[...] = layer_norm(second, g2_ref[...], b2_ref[...])


def finish(count, held, query, wk, wv, state, x, g1, b1, b_up, g2, b2, w_out, w_up, w_down):
    hbm = pl.BlockSpec(memory_space=pltpu.HBM)
    return pl.pallas_call(
        finish_kernel,
        in_specs=[SMEM] + [VMEM] * 13 + [hbm] * 3,
        out_specs=(VMEM,) * 4,
        out_shape=(jax.ShapeDtypeStruct((ROWS, D), F32),) + STATE_SHAPES,
        scratch_shapes=[
            pltpu.VMEM((D, D), BF16),
            pltpu.VMEM((D, FF), BF16),
            pltpu.VMEM((FF, D), BF16),
            pltpu.SemaphoreType.DMA((3,)),
        ],
        compiler_params=pltpu.CompilerParams(vmem_limit_bytes=44 * MIB),
        cost_estimate=pl.CostEstimate(flops=4 * 10**9, bytes_accessed=8 * MIB, transcendentals=10**6),
        name="finish",
    )(
        count,
        held,
        query,
        wk,
        wv,
        *state,
        x,
        g1[None],
        b1[None],
        b_up[None],
        g2[None],
        b2[None],
        w_out,
        w_up,
        w_down,
    )


def pair_lists(held, z_high, core):
    size = held.shape[1]
    planes = lax.axis_size("zhi")
    slot = jnp.arange(size, dtype=jnp.int32)
    key_group = slot % (size // CAP)
    distance = z_high - key_group // SLAB_GROUPS
    distance = jnp.where(core == 0, distance, -distance) % planes
    query_index = held // MEMBERS
    key_slot = (distance * SLAB_BLOCKS + key_group % SLAB_GROUPS * MEMBERS)[None, :] + held % MEMBERS
    ahead = (query_index[:, None, :] < query_index[:, :, None]) | (
        (query_index[:, None, :] == query_index[:, :, None]) & (slot[None, None, :] < slot[None, :, None])
    )
    place = jnp.sum(ahead.astype(jnp.int32), axis=-1)
    pairs = jnp.sum(jnp.where(place[:, None, :] == slot[None, :, None], key_slot[:, None, :], 0), axis=-1)
    pairs = jnp.concatenate([pairs.reshape(-1), jnp.zeros((SLOTS,), jnp.int32)])
    member = jnp.arange(MEMBERS, dtype=jnp.int32)[None, :, None]
    start = jnp.sum((query_index[:, None, :] < member).astype(jnp.int32), axis=-1)
    count = jnp.sum((query_index[:, None, :] == member).astype(jnp.int32), axis=-1)
    start = start + size * jnp.arange(SLAB_GROUPS, dtype=jnp.int32)[:, None]
    return start.reshape(-1), count.reshape(-1), pairs


def gather_rings(tiles):
    size = lax.axis_size("zhi")

    def move(value, step):
        pairs = [
            (2 * z + core, 2 * ((z + (step if core == 0 else -step)) % size) + core)
            for z in range(size)
            for core in range(2)
        ]
        return lax.ppermute(value, ("zhi", "core"), pairs)

    ahead, behind = [tiles], [tiles]
    for step in range(size // 2):
        ahead.append(move(ahead[-1], 1))
        if step < (size - 1) // 2:
            behind.append(move(behind[-1], -1))
    return ahead + behind[:0:-1]


def shift(x, step, size):
    pairs = [(i, i + step) for i in range(size) if 0 <= i + step < size]
    return lax.ppermute(x, AXES, pairs)


def on_device(
    node_feats,
    graph_ids,
    pair_tiles,
    pair_count,
    w_query,
    w_key,
    w_value,
    w_out,
    ln1_gain,
    ln1_bias,
    w_up,
    b_up,
    w_down,
    ln2_gain,
    ln2_bias,
):
    z_high, own = lax.axis_index("zhi"), lax.axis_index(SLAB)
    devices = lax.axis_size(AXES)

    def exchange(value):
        return lax.all_to_all(value, SLAB, split_axis=0, concat_axis=0, tiled=True)

    got = exchange(pack(node_feats, pair_tiles, pair_count))
    before = shift(node_feats, 1, devices)
    after = shift(node_feats, -1, devices)
    tiles, before, after = lax.optimization_barrier((got[:, :TILE_ROWS], before, after))
    gathered = gather_rings(tiles)
    codes = got[::MEMBERS, TILE_ROWS:, : pair_tiles.shape[1]].astype(jnp.int32)
    start, count, pairs = pair_lists(codes.reshape(SLAB_GROUPS, -1), z_high, lax.axis_index("core"))

    def mine(value):
        return lax.dynamic_slice_in_dim(value, own, 1, 0)

    fill = jnp.full((ROWS,), -1, jnp.int32)
    ids = jnp.concatenate([fill, graph_ids, fill])
    key_ids = lax.dynamic_slice_in_dim(ids, (z_high * SLAB_BLOCKS + own) * ROWS, 3 * ROWS, 0)
    query_ids = jnp.tile(key_ids[ROWS : 2 * ROWS], 2)[None, :]
    query, *state = near(
        before, node_feats, after, w_query, w_key, w_value, key_ids[:, None], query_ids
    )

    def fetch(at):
        held = exchange(select(start + jnp.minimum(at, count), pairs, gathered))
        return jnp.clip(mine(count) - at, 0, SLOTS), held

    def close(part, held, state):
        return finish(
            part,
            held,
            query,
            w_key,
            w_value,
            state,
            node_feats,
            ln1_gain,
            ln1_bias,
            b_up,
            ln2_gain,
            ln2_bias,
            w_out,
            w_up,
            w_down,
        )

    part, held = fetch(jnp.int32(0))
    out, *state = close(part, held, state)
    most = jnp.max(count)

    def go_on(state):
        def more(carry):
            at, state = carry
            part, held = fetch(at)
            return at + SLOTS, tuple(far(part, held, query, w_key, w_value, state))

        _, state = lax.while_loop(lambda carry: carry[0] < most, more, (jnp.int32(SLOTS), state))
        return close(jnp.zeros_like(part), held, state)[0]

    return lax.cond(most > SLOTS, go_on, lambda state: out, tuple(state))


def solution(mesh):
    inner = Mesh(mesh.devices.reshape(-1, 2, 2, 2, 4, 2), AXES)
    blk = ("zhi", "zlo", "ylo")
    in_specs = (P(AXES, None), P(), P(blk, None, None), P(blk, None)) + (P(),) * 11
    return jax.shard_map(
        on_device, mesh=inner, in_specs=in_specs, out_specs=P(AXES, None), check_vma=False
    )
```

```python
import jax
import jax.numpy as jnp
from jax import lax
from jax.experimental import pallas as pl
from jax.experimental.pallas import tpu as pltpu
from jax.sharding import Mesh
from jax.sharding import PartitionSpec as P

F32 = jnp.float32
BF16 = jnp.bfloat16

AXES = ("zhi", "zlo", "ylo", "yhi", "x", "core")
SLAB = ("zlo", "ylo", "yhi", "x", "core")
D = 512
FF = 1024
HEADS = 8
HEAD_DIM = 64
COUPLES = HEADS // 2
ROWS = 128
MEMBERS = 16
SLAB_GROUPS = 4
SLAB_BLOCKS = 64
CAP = 8
TILE_ROWS = 8
TILE_COLS = 128
COL_TILES = D // TILE_COLS
SLOTS = 16
GULP = 4
MIB = 1024 * 1024
FLOOR = -1e30

SMEM = pl.BlockSpec(memory_space=pltpu.SMEM)
VMEM = pl.BlockSpec(memory_space=pltpu.VMEM)


def absorb(state, keys, values, query_ref, mask, bias=()):
    new = []
    for couple in range(COUPLES):
        top, total, accum = state[couple]
        cols = slice(couple * 2 * HEAD_DIM, (couple + 1) * 2 * HEAD_DIM)
        scores = jnp.dot(keys[:, cols], query_ref[couple], preferred_element_type=F32)
        if mask is not None:
            scores = jnp.where(mask, scores, FLOOR)
        if bias:
            scores = jnp.concatenate(
                [scores[n * ROWS : (n + 1) * ROWS] + part for n, part in enumerate(bias)], axis=0
            )
        new_top = jnp.maximum(top, jnp.max(scores, axis=0, keepdims=True))
        decay = jnp.exp(top - new_top)
        prob = jnp.exp(scores - new_top)
        total = total * decay + jnp.sum(prob, axis=0, keepdims=True)
        part = lax.dot_general(
            values[:, cols],
            prob.astype(BF16),
            (((0,), (0,)), ((), ())),
            preferred_element_type=F32,
        )
        accum = jnp.concatenate(
            [
                accum[:HEAD_DIM] * decay[:, :ROWS] + part[:HEAD_DIM, :ROWS],
                accum[HEAD_DIM:] * decay[:, ROWS:] + part[HEAD_DIM:, ROWS:],
            ],
            axis=0,
        )
        new.append((new_top, total, accum))
    return new


def read_state(top_ref, total_ref, accum_ref):
    return [
        (
            top_ref[c : c + 1, :],
            total_ref[c : c + 1, :],
            accum_ref[c * 2 * HEAD_DIM : (c + 1) * 2 * HEAD_DIM, :],
        )
        for c in range(COUPLES)
    ]


def write_state(state, top_ref, total_ref, accum_ref):
    for c, (top, total, accum) in enumerate(state):
        top_ref[c : c + 1, :] = top
        total_ref[c : c + 1, :] = total
        accum_ref[c * 2 * HEAD_DIM : (c + 1) * 2 * HEAD_DIM, :] = accum


def project(x, weight_ref):
    return jnp.dot(x, weight_ref[...], preferred_element_type=F32).astype(BF16)


STATE_SHAPES = (
    jax.ShapeDtypeStruct((COUPLES, 2 * ROWS), F32),
    jax.ShapeDtypeStruct((COUPLES, 2 * ROWS), F32),
    jax.ShapeDtypeStruct((D, ROWS), F32),
)


def near_kernel(
    before_ref, x_ref, after_ref, wq_ref, wk_ref, wv_ref, kid_ref, qid_ref, query_ref, top_ref, total_ref, accum_ref
):
    x = x_ref[...]
    query = jnp.dot(x, wq_ref[...], preferred_element_type=F32).astype(BF16).astype(F32)
    query_t = (query.T * (1.0 / 8.0)).astype(BF16)
    zero = jnp.zeros((HEAD_DIM, ROWS), BF16)
    for couple in range(COUPLES):
        at = couple * 2 * HEAD_DIM
        first = query_t[at : at + HEAD_DIM]
        second = query_t[at + HEAD_DIM : at + 2 * HEAD_DIM]
        query_ref[couple] = jnp.concatenate(
            [jnp.concatenate([first, zero], axis=1), jnp.concatenate([zero, second], axis=1)], axis=0
        )
    state = [
        (
            jnp.full((1, 2 * ROWS), FLOOR, F32),
            jnp.zeros((1, 2 * ROWS), F32),
            jnp.zeros((2 * HEAD_DIM, ROWS), F32),
        )
    ] * COUPLES
    sources = jnp.concatenate([before_ref[...], x, after_ref[...]], axis=0)
    mask = kid_ref[...] == qid_ref[...]
    state = absorb(state, project(sources, wk_ref), project(sources, wv_ref), query_ref, mask)
    write_state(state, top_ref, total_ref, accum_ref)


def near(before, x, after, wq, wk, wv, key_ids, query_ids):
    return pl.pallas_call(
        near_kernel,
        out_shape=(jax.ShapeDtypeStruct((COUPLES, 2 * HEAD_DIM, 2 * ROWS), BF16),) + STATE_SHAPES,
        compiler_params=pltpu.CompilerParams(vmem_limit_bytes=32 * MIB),
        cost_estimate=pl.CostEstimate(flops=10**9, bytes_accessed=3 * MIB, transcendentals=400000),
        name="near",
    )(before, x, after, wq, wk, wv, key_ids, query_ids)


def pack_kernel(x_ref, tiles_ref, counts_ref, out_ref):
    x = x_ref[...].astype(F32)
    used = lax.broadcasted_iota(jnp.int32, tiles_ref.shape, 0) < counts_ref[...]
    codes = jnp.where(used, tiles_ref[...], MEMBERS * MEMBERS).astype(F32)
    codes = jnp.concatenate([codes, jnp.zeros((CAP, TILE_COLS - codes.shape[1]), F32)], axis=1)
    tiles = []
    for n in range(SLAB_BLOCKS):
        row, col = n // COL_TILES * TILE_ROWS, n % COL_TILES * TILE_COLS
        tiles.append(x[row : row + TILE_ROWS, col : col + TILE_COLS])
    for n in range(SLAB_BLOCKS):
        even = n // 2 * 2
        out_ref[n] = jnp.concatenate([tiles[even], tiles[even + 1], codes], axis=0).astype(BF16)


def pack(x, pair_tiles, pair_count):
    return pl.pallas_call(
        pack_kernel,
        out_shape=jax.ShapeDtypeStruct((SLAB_BLOCKS, 2 * TILE_ROWS + CAP, TILE_COLS), BF16),
        compiler_params=pltpu.CompilerParams(vmem_limit_bytes=60 * MIB),
        name="pack",
    )(x, pair_tiles[0].T, pair_count)


def select_kernel(core_ref, at_ref, list_ref, near_ref, one_ref, two_ref, three_ref, four_ref, swap_ref, out_ref, all_ref):
    core = core_ref[0]
    size = SLAB_BLOCKS
    half = size // 2
    for n, source in enumerate((near_ref, one_ref, two_ref, three_ref)):
        all_ref[n * size : (n + 1) * size] = source[core]
    all_ref[pl.ds(4 * size + core * half, half)] = four_ref[core]
    all_ref[pl.ds(4 * size + (1 - core) * half, half)] = swap_ref[3 * size :]
    for n in range(3):
        all_ref[(7 - n) * size : (8 - n) * size] = swap_ref[n * size : (n + 1) * size]

    def one(dest, carry):
        at = at_ref[dest]
        for slot in range(SLOTS):
            out_ref[dest, slot] = all_ref[list_ref[at + slot]]
        return carry

    lax.fori_loop(0, SLAB_BLOCKS, one, 0, unroll=4)


def select(core, at, pairs, gathered):
    return pl.pallas_call(
        select_kernel,
        in_specs=[SMEM] * 3 + [VMEM] * len(gathered),
        out_specs=VMEM,
        out_shape=jax.ShapeDtypeStruct((SLAB_BLOCKS, SLOTS, TILE_ROWS, TILE_COLS), BF16),
        scratch_shapes=[pltpu.VMEM((8 * SLAB_BLOCKS, TILE_ROWS, TILE_COLS), BF16)],
        compiler_params=pltpu.CompilerParams(vmem_limit_bytes=32 * MIB),
        cost_estimate=pl.CostEstimate(flops=0, bytes_accessed=8 * MIB, transcendentals=0),
        name="select",
    )(core, at, pairs, *gathered)


def gather_block(held_ref, slot):
    rows = []
    for r in range(ROWS // TILE_ROWS):
        tiles = [held_ref[r * COL_TILES + c, slot].astype(F32) for c in range(COL_TILES)]
        rows.append(jnp.concatenate(tiles, axis=1))
    return jnp.concatenate(rows, axis=0).astype(BF16)


def far_steps(count, held_ref, query_ref, wk_ref, wv_ref, state_refs):
    def step(i, carry):
        slots = [GULP * i + u for u in range(GULP)]
        x = jnp.concatenate([gather_block(held_ref, slot) for slot in slots], axis=0)
        bias = [jnp.where(slot < count, 0.0, FLOOR).astype(F32) for slot in slots]
        state = read_state(*state_refs)
        state = absorb(state, project(x, wk_ref), project(x, wv_ref), query_ref, None, bias)
        write_state(state, *state_refs)
        return carry

    lax.fori_loop(0, (count + GULP - 1) // GULP, step, 0)


def far_kernel(
    count_ref, held_ref, query_ref, wk_ref, wv_ref, top_in, total_in, accum_in, top_ref, total_ref, accum_ref
):
    top_ref[...] = top_in[...]
    total_ref[...] = total_in[...]
    accum_ref[...] = accum_in[...]
    far_steps(count_ref[0], held_ref, query_ref, wk_ref, wv_ref, (top_ref, total_ref, accum_ref))


def far(count, held, query, wk, wv, state):
    return pl.pallas_call(
        far_kernel,
        in_specs=[SMEM] + [VMEM] * 7,
        out_specs=(VMEM,) * 3,
        out_shape=STATE_SHAPES,
        compiler_params=pltpu.CompilerParams(vmem_limit_bytes=32 * MIB),
        name="far",
    )(count, held, query, wk, wv, *state)


def layer_norm(value, gain, bias):
    mean = jnp.mean(value, -1, keepdims=True)
    centred = value - mean
    spread = jnp.mean(centred * centred, -1, keepdims=True)
    return centred * lax.rsqrt(spread + 1e-05) * gain + bias


def finish_kernel(
    count_ref,
    held_ref,
    query_ref,
    wk_ref,
    wv_ref,
    top_in,
    total_in,
    accum_in,
    x_ref,
    g1_ref,
    b1_ref,
    b_up_ref,
    g2_ref,
    b2_ref,
    w_out_hbm,
    w_up_hbm,
    w_down_hbm,
    out_ref,
    top_ref,
    total_ref,
    accum_ref,
    w_out_ref,
    w_up_ref,
    w_down_ref,
    sems,
):
    weights = ((w_out_hbm, w_out_ref), (w_up_hbm, w_up_ref), (w_down_hbm, w_down_ref))
    copies = [pltpu.make_async_copy(a, b, sems.at[n]) for n, (a, b) in enumerate(weights)]
    for copy in copies:
        copy.start()
    far_kernel(
        count_ref,
        held_ref,
        query_ref,
        wk_ref,
        wv_ref,
        top_in,
        total_in,
        accum_in,
        top_ref,
        total_ref,
        accum_ref,
    )
    columns = []
    for head in range(HEADS):
        lanes = slice(head % 2 * ROWS, (head % 2 + 1) * ROWS)
        total = total_ref[head // 2 : head // 2 + 1, lanes]
        accum = accum_ref[head * HEAD_DIM : (head + 1) * HEAD_DIM, :]
        columns.append((accum / total).astype(BF16))
    attended_t = jnp.concatenate(columns, axis=0)
    copies[0].wait()
    mixed = x_ref[...].astype(F32) + lax.dot_general(
        attended_t, w_out_ref[...], (((0,), (0,)), ((), ())), preferred_element_type=F32
    )
    normed = layer_norm(mixed, g1_ref[...], b1_ref[...]).astype(BF16)
    copies[1].wait()
    hidden = jnp.maximum(
        jnp.dot(normed, w_up_ref[...], preferred_element_type=F32) + b_up_ref[...], 0.0
    ).astype(BF16)
    copies[2].wait()
    second = normed.astype(F32) + jnp.dot(hidden, w_down_ref[...], preferred_element_type=F32)
    out_ref[...] = layer_norm(second, g2_ref[...], b2_ref[...])


def finish(count, held, query, wk, wv, state, x, g1, b1, b_up, g2, b2, w_out, w_up, w_down):
    hbm = pl.BlockSpec(memory_space=pltpu.HBM)
    return pl.pallas_call(
        finish_kernel,
        in_specs=[SMEM] + [VMEM] * 13 + [hbm] * 3,
        out_specs=(VMEM,) * 4,
        out_shape=(jax.ShapeDtypeStruct((ROWS, D), F32),) + STATE_SHAPES,
        scratch_shapes=[
            pltpu.VMEM((D, D), BF16),
            pltpu.VMEM((D, FF), BF16),
            pltpu.VMEM((FF, D), BF16),
            pltpu.SemaphoreType.DMA((3,)),
        ],
        compiler_params=pltpu.CompilerParams(vmem_limit_bytes=44 * MIB),
        cost_estimate=pl.CostEstimate(flops=4 * 10**9, bytes_accessed=8 * MIB, transcendentals=10**6),
        name="finish",
    )(
        count,
        held,
        query,
        wk,
        wv,
        *state,
        x,
        g1[None],
        b1[None],
        b_up[None],
        g2[None],
        b2[None],
        w_out,
        w_up,
        w_down,
    )


def pair_lists(held, z_high, core):
    size = held.shape[1]
    planes = lax.axis_size("zhi")
    slot = jnp.arange(size, dtype=jnp.int32)
    key_group = slot % (size // CAP)
    distance = z_high - key_group // SLAB_GROUPS
    distance = jnp.where(core == 0, distance, -distance) % planes
    query_index = held // MEMBERS
    key_slot = (distance * SLAB_BLOCKS + key_group % SLAB_GROUPS * MEMBERS)[None, :] + held % MEMBERS
    ahead = (query_index[:, None, :] < query_index[:, :, None]) | (
        (query_index[:, None, :] == query_index[:, :, None]) & (slot[None, None, :] < slot[None, :, None])
    )
    place = jnp.sum(ahead.astype(jnp.int32), axis=-1)
    pairs = jnp.sum(jnp.where(place[:, None, :] == slot[None, :, None], key_slot[:, None, :], 0), axis=-1)
    pairs = jnp.concatenate([pairs.reshape(-1), jnp.zeros((SLOTS,), jnp.int32)])
    member = jnp.arange(MEMBERS, dtype=jnp.int32)[None, :, None]
    start = jnp.sum((query_index[:, None, :] < member).astype(jnp.int32), axis=-1)
    count = jnp.sum((query_index[:, None, :] == member).astype(jnp.int32), axis=-1)
    start = start + size * jnp.arange(SLAB_GROUPS, dtype=jnp.int32)[:, None]
    return start.reshape(-1), count.reshape(-1), pairs


def gather_planes(tiles, core):
    size = lax.axis_size("zhi")
    assert size == 8

    def move(value, step):
        pairs = [
            (2 * z + c, 2 * ((z + (step if c == 0 else -step)) % size) + c)
            for z in range(size)
            for c in range(2)
        ]
        return lax.ppermute(value, ("zhi", "core"), pairs)

    two = move(tiles, 2)
    one = move(tiles, 1)
    three = move(two, 1)
    half = SLAB_BLOCKS // 2
    four = move(lax.dynamic_slice_in_dim(two, core * half, half, 1), 2)
    others = [lax.dynamic_index_in_dim(v, 1 - core, 0, keepdims=False) for v in (one, two, three, four)]
    swap = lax.ppermute(jnp.concatenate(others, axis=0), "core", [(0, 1), (1, 0)])
    return tiles, one, two, three, four, swap


def shift(x, step, size):
    pairs = [(i, i + step) for i in range(size) if 0 <= i + step < size]
    return lax.ppermute(x, AXES, pairs)


def on_device(
    node_feats,
    graph_ids,
    pair_tiles,
    pair_count,
    w_query,
    w_key,
    w_value,
    w_out,
    ln1_gain,
    ln1_bias,
    w_up,
    b_up,
    w_down,
    ln2_gain,
    ln2_bias,
):
    z_high, own = lax.axis_index("zhi"), lax.axis_index(SLAB)
    devices = lax.axis_size(AXES)

    def exchange(value):
        return lax.all_to_all(value, SLAB, split_axis=0, concat_axis=0, tiled=True)

    got = exchange(pack(node_feats, pair_tiles, pair_count))
    before = shift(node_feats, 1, devices)
    after = shift(node_feats, -1, devices)
    tiles = jnp.stack([got[:, :TILE_ROWS], got[:, TILE_ROWS : 2 * TILE_ROWS]])
    tiles, before, after = lax.optimization_barrier((tiles, before, after))
    core = lax.axis_index("core")
    gathered = gather_planes(tiles, core)
    codes = got[::MEMBERS, 2 * TILE_ROWS :, : pair_tiles.shape[1]].astype(jnp.int32)
    start, count, pairs = pair_lists(codes.reshape(SLAB_GROUPS, -1), z_high, core)

    def mine(value):
        return lax.dynamic_slice_in_dim(value, own, 1, 0)

    fill = jnp.full((ROWS,), -1, jnp.int32)
    ids = jnp.concatenate([fill, graph_ids, fill])
    key_ids = lax.dynamic_slice_in_dim(ids, (z_high * SLAB_BLOCKS + own) * ROWS, 3 * ROWS, 0)
    query_ids = jnp.tile(key_ids[ROWS : 2 * ROWS], 2)[None, :]
    query, *state = near(
        before, node_feats, after, w_query, w_key, w_value, key_ids[:, None], query_ids
    )

    def fetch(at):
        held = exchange(select(core.reshape(1), start + jnp.minimum(at, count), pairs, gathered))
        return jnp.clip(mine(count) - at, 0, SLOTS), held

    def close(part, held, state):
        return finish(
            part,
            held,
            query,
            w_key,
            w_value,
            state,
            node_feats,
            ln1_gain,
            ln1_bias,
            b_up,
            ln2_gain,
            ln2_bias,
            w_out,
            w_up,
            w_down,
        )

    part, held = fetch(jnp.int32(0))
    out, *state = close(part, held, state)
    most = jnp.max(count)

    def go_on(state):
        def more(carry):
            at, state = carry
            part, held = fetch(at)
            return at + SLOTS, tuple(far(part, held, query, w_key, w_value, state))

        _, state = lax.while_loop(lambda carry: carry[0] < most, more, (jnp.int32(SLOTS), state))
        return close(jnp.zeros_like(part), held, state)[0]

    return lax.cond(most > SLOTS, go_on, lambda state: out, tuple(state))


def solution(mesh):
    inner = Mesh(mesh.devices.reshape(-1, 2, 2, 2, 4, 2), AXES)
    blk = ("zhi", "zlo", "ylo")
    in_specs = (P(AXES, None), P(), P(blk, None, None), P(blk, None)) + (P(),) * 11
    return jax.shard_map(
        on_device, mesh=inner, in_specs=in_specs, out_specs=P(AXES, None), check_vma=False
    )
```

```python
import jax
import jax.numpy as jnp
from jax import lax
from jax.experimental import pallas as pl
from jax.experimental.pallas import tpu as pltpu
from jax.sharding import Mesh
from jax.sharding import PartitionSpec as P

F32 = jnp.float32
BF16 = jnp.bfloat16

AXES = ("zhi", "zlo", "ylo", "yhi", "x", "core")
SLAB = ("zlo", "ylo", "yhi", "x", "core")
D = 512
FF = 1024
HEADS = 8
HEAD_DIM = 64
COUPLES = HEADS // 2
ROWS = 128
MEMBERS = 16
SLAB_GROUPS = 4
SLAB_BLOCKS = 64
CAP = 8
TILE_ROWS = 8
TILE_COLS = 128
COL_TILES = D // TILE_COLS
FIRST = 12
LATER = 4
GULP = 4
MIB = 1024 * 1024
FLOOR = -1e30

SMEM = pl.BlockSpec(memory_space=pltpu.SMEM)
VMEM = pl.BlockSpec(memory_space=pltpu.VMEM)


def absorb(state, keys, values, query_ref, mask, bias=()):
    new = []
    for couple in range(COUPLES):
        top, total, accum = state[couple]
        cols = slice(couple * 2 * HEAD_DIM, (couple + 1) * 2 * HEAD_DIM)
        scores = jnp.dot(keys[:, cols], query_ref[couple], preferred_element_type=F32)
        if mask is not None:
            scores = jnp.where(mask, scores, FLOOR)
        if bias:
            scores = jnp.concatenate(
                [scores[n * ROWS : (n + 1) * ROWS] + part for n, part in enumerate(bias)], axis=0
            )
        new_top = jnp.maximum(top, jnp.max(scores, axis=0, keepdims=True))
        decay = jnp.exp(top - new_top)
        prob = jnp.exp(scores - new_top)
        total = total * decay + jnp.sum(prob, axis=0, keepdims=True)
        part = lax.dot_general(
            values[:, cols],
            prob.astype(BF16),
            (((0,), (0,)), ((), ())),
            preferred_element_type=F32,
        )
        accum = jnp.concatenate(
            [
                accum[:HEAD_DIM] * decay[:, :ROWS] + part[:HEAD_DIM, :ROWS],
                accum[HEAD_DIM:] * decay[:, ROWS:] + part[HEAD_DIM:, ROWS:],
            ],
            axis=0,
        )
        new.append((new_top, total, accum))
    return new


def read_state(top_ref, total_ref, accum_ref):
    return [
        (
            top_ref[c : c + 1, :],
            total_ref[c : c + 1, :],
            accum_ref[c * 2 * HEAD_DIM : (c + 1) * 2 * HEAD_DIM, :],
        )
        for c in range(COUPLES)
    ]


def write_state(state, top_ref, total_ref, accum_ref):
    for c, (top, total, accum) in enumerate(state):
        top_ref[c : c + 1, :] = top
        total_ref[c : c + 1, :] = total
        accum_ref[c * 2 * HEAD_DIM : (c + 1) * 2 * HEAD_DIM, :] = accum


def project(x, weight_ref):
    return jnp.dot(x, weight_ref[...], preferred_element_type=F32).astype(BF16)


STATE_SHAPES = (
    jax.ShapeDtypeStruct((COUPLES, 2 * ROWS), F32),
    jax.ShapeDtypeStruct((COUPLES, 2 * ROWS), F32),
    jax.ShapeDtypeStruct((D, ROWS), F32),
)


def near_kernel(
    before_ref, x_ref, after_ref, wq_ref, wk_ref, wv_ref, kid_ref, qid_ref, query_ref, top_ref, total_ref, accum_ref
):
    x = x_ref[...]
    query = jnp.dot(x, wq_ref[...], preferred_element_type=F32).astype(BF16).astype(F32)
    query_t = (query.T * (1.0 / 8.0)).astype(BF16)
    zero = jnp.zeros((HEAD_DIM, ROWS), BF16)
    for couple in range(COUPLES):
        at = couple * 2 * HEAD_DIM
        first = query_t[at : at + HEAD_DIM]
        second = query_t[at + HEAD_DIM : at + 2 * HEAD_DIM]
        query_ref[couple] = jnp.concatenate(
            [jnp.concatenate([first, zero], axis=1), jnp.concatenate([zero, second], axis=1)], axis=0
        )
    state = [
        (
            jnp.full((1, 2 * ROWS), FLOOR, F32),
            jnp.zeros((1, 2 * ROWS), F32),
            jnp.zeros((2 * HEAD_DIM, ROWS), F32),
        )
    ] * COUPLES
    sources = jnp.concatenate([before_ref[...], x, after_ref[...]], axis=0)
    mask = kid_ref[...] == qid_ref[...]
    state = absorb(state, project(sources, wk_ref), project(sources, wv_ref), query_ref, mask)
    write_state(state, top_ref, total_ref, accum_ref)


def near(before, x, after, wq, wk, wv, key_ids, query_ids):
    return pl.pallas_call(
        near_kernel,
        out_shape=(jax.ShapeDtypeStruct((COUPLES, 2 * HEAD_DIM, 2 * ROWS), BF16),) + STATE_SHAPES,
        compiler_params=pltpu.CompilerParams(vmem_limit_bytes=32 * MIB),
        cost_estimate=pl.CostEstimate(flops=10**9, bytes_accessed=3 * MIB, transcendentals=400000),
        name="near",
    )(before, x, after, wq, wk, wv, key_ids, query_ids)


def pack_kernel(x_ref, tiles_ref, counts_ref, out_ref):
    x = x_ref[...].astype(F32)
    used = lax.broadcasted_iota(jnp.int32, tiles_ref.shape, 0) < counts_ref[...]
    codes = jnp.where(used, tiles_ref[...], MEMBERS * MEMBERS).astype(F32)
    codes = jnp.concatenate([codes, jnp.zeros((CAP, TILE_COLS - codes.shape[1]), F32)], axis=1)
    for n in range(SLAB_BLOCKS):
        row, col = n // COL_TILES * TILE_ROWS, n % COL_TILES * TILE_COLS
        tile = x[row : row + TILE_ROWS, col : col + TILE_COLS]
        out_ref[n] = jnp.concatenate([tile, codes], axis=0).astype(BF16)


def pack(x, pair_tiles, pair_count):
    return pl.pallas_call(
        pack_kernel,
        out_shape=jax.ShapeDtypeStruct((SLAB_BLOCKS, TILE_ROWS + CAP, TILE_COLS), BF16),
        compiler_params=pltpu.CompilerParams(vmem_limit_bytes=60 * MIB),
        name="pack",
    )(x, pair_tiles[0].T, pair_count)


def select_kernel(at_ref, count_ref, list_ref, *refs):
    sources, out_ref, all_ref = refs[:-2], refs[-2], refs[-1]
    width = out_ref.shape[1]
    out_ref[...] = jnp.zeros_like(out_ref)
    for n, source in enumerate(sources):
        all_ref[n * SLAB_BLOCKS : (n + 1) * SLAB_BLOCKS] = source[...]

    def one(dest, carry):
        at = at_ref[dest]
        count = count_ref[dest]
        for begin in range(0, width, GULP):

            @pl.when(count > begin)
            def _():
                for slot in range(begin, begin + GULP):
                    out_ref[dest, slot] = all_ref[list_ref[at + slot]]

        return carry

    lax.fori_loop(0, SLAB_BLOCKS, one, 0, unroll=2)


def select(width, at, count, pairs, gathered):
    return pl.pallas_call(
        select_kernel,
        in_specs=[SMEM] * 3 + [VMEM] * len(gathered),
        out_specs=VMEM,
        out_shape=jax.ShapeDtypeStruct((SLAB_BLOCKS, width, TILE_ROWS, TILE_COLS), BF16),
        scratch_shapes=[pltpu.VMEM((len(gathered) * SLAB_BLOCKS, TILE_ROWS, TILE_COLS), BF16)],
        compiler_params=pltpu.CompilerParams(vmem_limit_bytes=32 * MIB),
        cost_estimate=pl.CostEstimate(flops=0, bytes_accessed=8 * MIB, transcendentals=0),
        name="select",
    )(at, count, pairs, *gathered)


def gather_block(held_ref, slot):
    rows = []
    for r in range(ROWS // TILE_ROWS):
        tiles = [held_ref[r * COL_TILES + c, slot].astype(F32) for c in range(COL_TILES)]
        rows.append(jnp.concatenate(tiles, axis=1))
    return jnp.concatenate(rows, axis=0).astype(BF16)


def far_steps(count, held_ref, query_ref, wk_ref, wv_ref, state_refs):
    def step(i, carry):
        slots = [GULP * i + u for u in range(GULP)]
        x = jnp.concatenate([gather_block(held_ref, slot) for slot in slots], axis=0)
        bias = [jnp.where(slot < count, 0.0, FLOOR).astype(F32) for slot in slots]
        state = read_state(*state_refs)
        state = absorb(state, project(x, wk_ref), project(x, wv_ref), query_ref, None, bias)
        write_state(state, *state_refs)
        return carry

    lax.fori_loop(0, (count + GULP - 1) // GULP, step, 0)


def far_kernel(
    count_ref, held_ref, query_ref, wk_ref, wv_ref, top_in, total_in, accum_in, top_ref, total_ref, accum_ref
):
    top_ref[...] = top_in[...]
    total_ref[...] = total_in[...]
    accum_ref[...] = accum_in[...]
    far_steps(count_ref[0], held_ref, query_ref, wk_ref, wv_ref, (top_ref, total_ref, accum_ref))


def far(count, held, query, wk, wv, state):
    return pl.pallas_call(
        far_kernel,
        in_specs=[SMEM] + [VMEM] * 7,
        out_specs=(VMEM,) * 3,
        out_shape=STATE_SHAPES,
        compiler_params=pltpu.CompilerParams(vmem_limit_bytes=32 * MIB),
        cost_estimate=pl.CostEstimate(flops=10**9, bytes_accessed=4 * MIB, transcendentals=10**6),
        name="far",
    )(count, held, query, wk, wv, *state)


def layer_norm(value, gain, bias):
    mean = jnp.mean(value, -1, keepdims=True)
    centred = value - mean
    spread = jnp.mean(centred * centred, -1, keepdims=True)
    return centred * lax.rsqrt(spread + 1e-05) * gain + bias


def finish_kernel(
    count_ref,
    held_ref,
    query_ref,
    wk_ref,
    wv_ref,
    top_in,
    total_in,
    accum_in,
    x_ref,
    g1_ref,
    b1_ref,
    b_up_ref,
    g2_ref,
    b2_ref,
    w_out_hbm,
    w_up_hbm,
    w_down_hbm,
    out_ref,
    top_ref,
    total_ref,
    accum_ref,
    w_out_ref,
    w_up_ref,
    w_down_ref,
    sems,
):
    weights = ((w_out_hbm, w_out_ref), (w_up_hbm, w_up_ref), (w_down_hbm, w_down_ref))
    copies = [pltpu.make_async_copy(a, b, sems.at[n]) for n, (a, b) in enumerate(weights)]
    for copy in copies:
        copy.start()
    far_kernel(
        count_ref,
        held_ref,
        query_ref,
        wk_ref,
        wv_ref,
        top_in,
        total_in,
        accum_in,
        top_ref,
        total_ref,
        accum_ref,
    )
    columns = []
    for head in range(HEADS):
        lanes = slice(head % 2 * ROWS, (head % 2 + 1) * ROWS)
        total = total_ref[head // 2 : head // 2 + 1, lanes]
        accum = accum_ref[head * HEAD_DIM : (head + 1) * HEAD_DIM, :]
        columns.append((accum / total).astype(BF16))
    attended_t = jnp.concatenate(columns, axis=0)
    copies[0].wait()
    mixed = x_ref[...].astype(F32) + lax.dot_general(
        attended_t, w_out_ref[...], (((0,), (0,)), ((), ())), preferred_element_type=F32
    )
    normed = layer_norm(mixed, g1_ref[...], b1_ref[...]).astype(BF16)
    copies[1].wait()
    hidden = jnp.maximum(
        jnp.dot(normed, w_up_ref[...], preferred_element_type=F32) + b_up_ref[...], 0.0
    ).astype(BF16)
    copies[2].wait()
    second = normed.astype(F32) + jnp.dot(hidden, w_down_ref[...], preferred_element_type=F32)
    out_ref[...] = layer_norm(second, g2_ref[...], b2_ref[...])


def finish(count, held, query, wk, wv, state, x, g1, b1, b_up, g2, b2, w_out, w_up, w_down):
    hbm = pl.BlockSpec(memory_space=pltpu.HBM)
    return pl.pallas_call(
        finish_kernel,
        in_specs=[SMEM] + [VMEM] * 13 + [hbm] * 3,
        out_specs=(VMEM,) * 4,
        out_shape=(jax.ShapeDtypeStruct((ROWS, D), F32),) + STATE_SHAPES,
        scratch_shapes=[
            pltpu.VMEM((D, D), BF16),
            pltpu.VMEM((D, FF), BF16),
            pltpu.VMEM((FF, D), BF16),
            pltpu.SemaphoreType.DMA((3,)),
        ],
        compiler_params=pltpu.CompilerParams(vmem_limit_bytes=44 * MIB),
        cost_estimate=pl.CostEstimate(flops=4 * 10**9, bytes_accessed=8 * MIB, transcendentals=10**6),
        name="finish",
    )(
        count,
        held,
        query,
        wk,
        wv,
        *state,
        x,
        g1[None],
        b1[None],
        b_up[None],
        g2[None],
        b2[None],
        w_out,
        w_up,
        w_down,
    )


def pair_lists(held, z_high, core):
    size = held.shape[1]
    planes = lax.axis_size("zhi")
    slot = jnp.arange(size, dtype=jnp.int32)
    key_group = slot % (size // CAP)
    distance = z_high - key_group // SLAB_GROUPS
    distance = jnp.where(core == 0, distance, -distance) % planes
    query_index = held // MEMBERS
    key_slot = (distance * SLAB_BLOCKS + key_group % SLAB_GROUPS * MEMBERS)[None, :] + held % MEMBERS
    ahead = (query_index[:, None, :] < query_index[:, :, None]) | (
        (query_index[:, None, :] == query_index[:, :, None]) & (slot[None, None, :] < slot[None, :, None])
    )
    place = jnp.sum(ahead.astype(jnp.int32), axis=-1)
    pairs = jnp.sum(jnp.where(place[:, None, :] == slot[None, :, None], key_slot[:, None, :], 0), axis=-1)
    pairs = jnp.concatenate([pairs.reshape(-1), jnp.zeros((FIRST,), jnp.int32)])
    member = jnp.arange(MEMBERS, dtype=jnp.int32)[None, :, None]
    start = jnp.sum((query_index[:, None, :] < member).astype(jnp.int32), axis=-1)
    count = jnp.sum((query_index[:, None, :] == member).astype(jnp.int32), axis=-1)
    start = start + size * jnp.arange(SLAB_GROUPS, dtype=jnp.int32)[:, None]
    return start.reshape(-1), count.reshape(-1), pairs


def gather_rings(tiles):
    size = lax.axis_size("zhi")

    def move(value, step):
        pairs = [
            (2 * z + core, 2 * ((z + (step if core == 0 else -step)) % size) + core)
            for z in range(size)
            for core in range(2)
        ]
        return lax.ppermute(value, ("zhi", "core"), pairs)

    ahead, behind = [tiles], [tiles]
    for step in range(size // 2):
        ahead.append(move(ahead[-1], 1))
        if step < (size - 1) // 2:
            behind.append(move(behind[-1], -1))
    return ahead + behind[:0:-1]


def shift(x, step, size):
    pairs = [(i, i + step) for i in range(size) if 0 <= i + step < size]
    return lax.ppermute(x, AXES, pairs)


def on_device(
    node_feats,
    graph_ids,
    pair_tiles,
    pair_count,
    w_query,
    w_key,
    w_value,
    w_out,
    ln1_gain,
    ln1_bias,
    w_up,
    b_up,
    w_down,
    ln2_gain,
    ln2_bias,
):
    z_high, own = lax.axis_index("zhi"), lax.axis_index(SLAB)
    devices = lax.axis_size(AXES)

    def exchange(value):
        return lax.all_to_all(value, SLAB, split_axis=0, concat_axis=0, tiled=True)

    got = exchange(pack(node_feats, pair_tiles, pair_count))
    before = shift(node_feats, 1, devices)
    after = shift(node_feats, -1, devices)
    tiles, before, after = lax.optimization_barrier((got[:, :TILE_ROWS], before, after))
    gathered = gather_rings(tiles)
    codes = got[::MEMBERS, TILE_ROWS:, : pair_tiles.shape[1]].astype(jnp.int32)
    start, count, pairs = pair_lists(codes.reshape(SLAB_GROUPS, -1), z_high, lax.axis_index("core"))

    def mine(value):
        return lax.dynamic_slice_in_dim(value, own, 1, 0)

    fill = jnp.full((ROWS,), -1, jnp.int32)
    ids = jnp.concatenate([fill, graph_ids, fill])
    key_ids = lax.dynamic_slice_in_dim(ids, (z_high * SLAB_BLOCKS + own) * ROWS, 3 * ROWS, 0)
    query_ids = jnp.tile(key_ids[ROWS : 2 * ROWS], 2)[None, :]
    def choose(at, width, start):
        here = jnp.clip(count - at, 0, width)
        return mine(here), select(width, start + jnp.minimum(at, count), here, pairs, gathered)

    first_part, first_send = choose(0, FIRST, start)
    first_send, before = lax.optimization_barrier((first_send, before))
    first_held = exchange(first_send)
    query, *state = near(
        before, node_feats, after, w_query, w_key, w_value, key_ids[:, None], query_ids
    )
    query, later_start = lax.optimization_barrier((query, start))
    part, send = choose(FIRST, LATER, later_start)
    held = exchange(send)
    state = far(first_part, first_held, query, w_key, w_value, state)

    def close(part, held, state):
        return finish(
            part,
            held,
            query,
            w_key,
            w_value,
            state,
            node_feats,
            ln1_gain,
            ln1_bias,
            b_up,
            ln2_gain,
            ln2_bias,
            w_out,
            w_up,
            w_down,
        )

    out, *state = close(part, held, state)
    most = jnp.max(count)

    def go_on(state):
        def more(carry):
            at, state = carry
            part, send = choose(at, FIRST, start)
            return at + FIRST, tuple(far(part, exchange(send), query, w_key, w_value, state))

        _, state = lax.while_loop(
            lambda carry: carry[0] < most, more, (jnp.int32(FIRST + LATER), state)
        )
        return close(jnp.zeros_like(part), held, state)[0]

    return lax.cond(most > FIRST + LATER, go_on, lambda state: out, tuple(state))


def solution(mesh):
    inner = Mesh(mesh.devices.reshape(-1, 2, 2, 2, 4, 2), AXES)
    blk = ("zhi", "zlo", "ylo")
    in_specs = (P(AXES, None), P(), P(blk, None, None), P(blk, None)) + (P(),) * 11
    return jax.shard_map(
        on_device, mesh=inner, in_specs=in_specs, out_specs=P(AXES, None), check_vma=False
    )
```

```python
import jax
import jax.numpy as jnp
from jax import lax
from jax.experimental import pallas as pl
from jax.experimental.pallas import tpu as pltpu
from jax.sharding import Mesh
from jax.sharding import PartitionSpec as P

F32 = jnp.float32
BF16 = jnp.bfloat16

AXES = ("zhi", "zlo", "ylo", "yhi", "x", "core")
SLAB = ("zlo", "ylo", "yhi", "x", "core")
D = 512
FF = 1024
HEADS = 8
HEAD_DIM = 64
COUPLES = HEADS // 2
ROWS = 128
MEMBERS = 16
SLAB_GROUPS = 4
SLAB_BLOCKS = 64
CAP = 8
TILE_ROWS = 8
TILE_COLS = 128
COL_TILES = D // TILE_COLS
SLOTS = 15
GULP = 5
MIB = 1024 * 1024
FLOOR = -1e30

SMEM = pl.BlockSpec(memory_space=pltpu.SMEM)
VMEM = pl.BlockSpec(memory_space=pltpu.VMEM)


def absorb(state, keys, values, query_ref, mask=None, bias=()):
    bias = bias or (None,)
    size = keys.shape[0] // len(bias)
    new = []
    for couple in range(COUPLES):
        top, total, accum = state[couple]
        cols = slice(couple * 2 * HEAD_DIM, (couple + 1) * 2 * HEAD_DIM)
        scores = [
            jnp.dot(keys[n * size : (n + 1) * size, cols], query_ref[couple], preferred_element_type=F32)
            for n in range(len(bias))
        ]
        if mask is not None:
            scores = [jnp.where(mask, scores[0], FLOOR)]
        new_top = top
        for part, shift in zip(scores, bias):
            best = jnp.max(part, axis=0, keepdims=True)
            new_top = jnp.maximum(new_top, best if shift is None else best + shift)
        decay = jnp.exp(top - new_top)
        total = total * decay
        probs = []
        for part, shift in zip(scores, bias):
            prob = jnp.exp(part - (new_top if shift is None else new_top - shift))
            total = total + jnp.sum(prob, axis=0, keepdims=True)
            probs.append(prob.astype(BF16))
        part = lax.dot_general(
            values[:, cols],
            jnp.concatenate(probs, axis=0),
            (((0,), (0,)), ((), ())),
            preferred_element_type=F32,
        )
        accum = jnp.concatenate(
            [
                accum[:HEAD_DIM] * decay[:, :ROWS] + part[:HEAD_DIM, :ROWS],
                accum[HEAD_DIM:] * decay[:, ROWS:] + part[HEAD_DIM:, ROWS:],
            ],
            axis=0,
        )
        new.append((new_top, total, accum))
    return new


def read_state(top_ref, total_ref, accum_ref):
    return [
        (
            top_ref[c : c + 1, :],
            total_ref[c : c + 1, :],
            accum_ref[c * 2 * HEAD_DIM : (c + 1) * 2 * HEAD_DIM, :],
        )
        for c in range(COUPLES)
    ]


def write_state(state, top_ref, total_ref, accum_ref):
    for c, (top, total, accum) in enumerate(state):
        top_ref[c : c + 1, :] = top
        total_ref[c : c + 1, :] = total
        accum_ref[c * 2 * HEAD_DIM : (c + 1) * 2 * HEAD_DIM, :] = accum


def project(x, weight_ref):
    return jnp.dot(x, weight_ref[...], preferred_element_type=F32).astype(BF16)


STATE_SHAPES = (
    jax.ShapeDtypeStruct((COUPLES, 2 * ROWS), F32),
    jax.ShapeDtypeStruct((COUPLES, 2 * ROWS), F32),
    jax.ShapeDtypeStruct((D, ROWS), F32),
)


def near_kernel(
    beside_ref, x_ref, across_ref, wq_ref, wk_ref, wv_ref, kid_ref, qid_ref, query_ref, top_ref, total_ref, accum_ref
):
    x = x_ref[...]
    query = jnp.dot(x, wq_ref[...], preferred_element_type=F32).astype(BF16).astype(F32)
    query_t = (query.T * (1.0 / 8.0)).astype(BF16)
    zero = jnp.zeros((HEAD_DIM, ROWS), BF16)
    for couple in range(COUPLES):
        at = couple * 2 * HEAD_DIM
        first = query_t[at : at + HEAD_DIM]
        second = query_t[at + HEAD_DIM : at + 2 * HEAD_DIM]
        query_ref[couple] = jnp.concatenate(
            [jnp.concatenate([first, zero], axis=1), jnp.concatenate([zero, second], axis=1)], axis=0
        )
    state = [
        (
            jnp.full((1, 2 * ROWS), FLOOR, F32),
            jnp.zeros((1, 2 * ROWS), F32),
            jnp.zeros((2 * HEAD_DIM, ROWS), F32),
        )
    ] * COUPLES
    sources = jnp.concatenate([beside_ref[...], x, across_ref[...]], axis=0)
    mask = kid_ref[...] == qid_ref[...]
    state = absorb(state, project(sources, wk_ref), project(sources, wv_ref), query_ref, mask)
    write_state(state, top_ref, total_ref, accum_ref)


def near(beside, x, across, wq, wk, wv, key_ids, query_ids):
    return pl.pallas_call(
        near_kernel,
        out_shape=(jax.ShapeDtypeStruct((COUPLES, 2 * HEAD_DIM, 2 * ROWS), BF16),) + STATE_SHAPES,
        compiler_params=pltpu.CompilerParams(vmem_limit_bytes=32 * MIB),
        cost_estimate=pl.CostEstimate(flops=10**9, bytes_accessed=3 * MIB, transcendentals=400000),
        name="near",
    )(beside, x, across, wq, wk, wv, key_ids, query_ids)


def pack_kernel(x_ref, tiles_ref, counts_ref, out_ref):
    x = x_ref[...].astype(F32)
    used = lax.broadcasted_iota(jnp.int32, tiles_ref.shape, 0) < counts_ref[...]
    codes = jnp.where(used, tiles_ref[...], MEMBERS * MEMBERS).astype(F32)
    codes = jnp.concatenate([codes, jnp.zeros((CAP, TILE_COLS - codes.shape[1]), F32)], axis=1)
    for n in range(SLAB_BLOCKS):
        row, col = n // COL_TILES * TILE_ROWS, n % COL_TILES * TILE_COLS
        tile = x[row : row + TILE_ROWS, col : col + TILE_COLS]
        out_ref[n] = jnp.concatenate([tile, codes], axis=0).astype(BF16)


def pack(x, pair_tiles, pair_count):
    return pl.pallas_call(
        pack_kernel,
        out_shape=jax.ShapeDtypeStruct((SLAB_BLOCKS, TILE_ROWS + CAP, TILE_COLS), BF16),
        compiler_params=pltpu.CompilerParams(vmem_limit_bytes=60 * MIB),
        name="pack",
    )(x, pair_tiles[0].T, pair_count)


def select_kernel(at_ref, list_ref, *refs):
    sources, out_ref, all_ref = refs[:-2], refs[-2], refs[-1]
    at = 0
    for source in sources:
        all_ref[at : at + source.shape[0]] = source[...]
        at += source.shape[0]

    def one(dest, carry):
        at = at_ref[dest]
        for slot in range(SLOTS):
            out_ref[dest, slot] = all_ref[list_ref[at + slot]]
        return carry

    lax.fori_loop(0, SLAB_BLOCKS, one, 0, unroll=4)


def select(at, pairs, gathered):
    return pl.pallas_call(
        select_kernel,
        in_specs=[SMEM] * 2 + [VMEM] * len(gathered),
        out_specs=VMEM,
        out_shape=jax.ShapeDtypeStruct((SLAB_BLOCKS, SLOTS, TILE_ROWS, TILE_COLS), BF16),
        scratch_shapes=[pltpu.VMEM((sum(g.shape[0] for g in gathered), TILE_ROWS, TILE_COLS), BF16)],
        compiler_params=pltpu.CompilerParams(vmem_limit_bytes=32 * MIB),
        cost_estimate=pl.CostEstimate(flops=0, bytes_accessed=8 * MIB, transcendentals=0),
        name="select",
    )(at, pairs, *gathered)


def gather_block(held_ref, slot):
    rows = []
    for r in range(ROWS // TILE_ROWS):
        tiles = [held_ref[r * COL_TILES + c, slot].astype(F32) for c in range(COL_TILES)]
        rows.append(jnp.concatenate(tiles, axis=1))
    return jnp.concatenate(rows, axis=0).astype(BF16)


def far_steps(count, held_ref, query_ref, wk_ref, wv_ref, state_refs):
    def step(i, carry):
        slots = [GULP * i + u for u in range(GULP)]
        x = jnp.concatenate([gather_block(held_ref, slot) for slot in slots], axis=0)
        bias = [jnp.where(slot < count, 0.0, FLOOR).astype(F32) for slot in slots]
        state = read_state(*state_refs)
        state = absorb(state, project(x, wk_ref), project(x, wv_ref), query_ref, bias=bias)
        write_state(state, *state_refs)
        return carry

    lax.fori_loop(0, (count + GULP - 1) // GULP, step, 0)


def far_kernel(
    count_ref, held_ref, query_ref, wk_ref, wv_ref, top_in, total_in, accum_in, top_ref, total_ref, accum_ref
):
    top_ref[...] = top_in[...]
    total_ref[...] = total_in[...]
    accum_ref[...] = accum_in[...]
    far_steps(count_ref[0], held_ref, query_ref, wk_ref, wv_ref, (top_ref, total_ref, accum_ref))


def far(count, held, query, wk, wv, state):
    return pl.pallas_call(
        far_kernel,
        in_specs=[SMEM] + [VMEM] * 7,
        out_specs=(VMEM,) * 3,
        out_shape=STATE_SHAPES,
        compiler_params=pltpu.CompilerParams(vmem_limit_bytes=32 * MIB),
        name="far",
    )(count, held, query, wk, wv, *state)


def layer_norm(value, gain, bias):
    mean = jnp.mean(value, -1, keepdims=True)
    centred = value - mean
    spread = jnp.mean(centred * centred, -1, keepdims=True)
    return centred * lax.rsqrt(spread + 1e-05) * gain + bias


def finish_kernel(
    count_ref,
    held_ref,
    query_ref,
    wk_ref,
    wv_ref,
    top_in,
    total_in,
    accum_in,
    x_ref,
    g1_ref,
    b1_ref,
    b_up_ref,
    g2_ref,
    b2_ref,
    w_out_hbm,
    w_up_hbm,
    w_down_hbm,
    out_ref,
    top_ref,
    total_ref,
    accum_ref,
    w_out_ref,
    w_up_ref,
    w_down_ref,
    sems,
):
    weights = ((w_out_hbm, w_out_ref), (w_up_hbm, w_up_ref), (w_down_hbm, w_down_ref))
    copies = [pltpu.make_async_copy(a, b, sems.at[n]) for n, (a, b) in enumerate(weights)]
    for copy in copies:
        copy.start()
    far_kernel(
        count_ref,
        held_ref,
        query_ref,
        wk_ref,
        wv_ref,
        top_in,
        total_in,
        accum_in,
        top_ref,
        total_ref,
        accum_ref,
    )
    columns = []
    for head in range(HEADS):
        lanes = slice(head % 2 * ROWS, (head % 2 + 1) * ROWS)
        total = total_ref[head // 2 : head // 2 + 1, lanes]
        accum = accum_ref[head * HEAD_DIM : (head + 1) * HEAD_DIM, :]
        columns.append((accum / total).astype(BF16))
    attended_t = jnp.concatenate(columns, axis=0)
    copies[0].wait()
    mixed = x_ref[...].astype(F32) + lax.dot_general(
        attended_t, w_out_ref[...], (((0,), (0,)), ((), ())), preferred_element_type=F32
    )
    normed = layer_norm(mixed, g1_ref[...], b1_ref[...]).astype(BF16)
    copies[1].wait()
    hidden = jnp.maximum(
        jnp.dot(normed, w_up_ref[...], preferred_element_type=F32) + b_up_ref[...], 0.0
    ).astype(BF16)
    copies[2].wait()
    second = normed.astype(F32) + jnp.dot(hidden, w_down_ref[...], preferred_element_type=F32)
    out_ref[...] = layer_norm(second, g2_ref[...], b2_ref[...])


def finish(count, held, query, wk, wv, state, x, g1, b1, b_up, g2, b2, w_out, w_up, w_down):
    hbm = pl.BlockSpec(memory_space=pltpu.HBM)
    return pl.pallas_call(
        finish_kernel,
        in_specs=[SMEM] + [VMEM] * 13 + [hbm] * 3,
        out_specs=(VMEM,) * 4,
        out_shape=(jax.ShapeDtypeStruct((ROWS, D), F32),) + STATE_SHAPES,
        scratch_shapes=[
            pltpu.VMEM((D, D), BF16),
            pltpu.VMEM((D, FF), BF16),
            pltpu.VMEM((FF, D), BF16),
            pltpu.SemaphoreType.DMA((3,)),
        ],
        compiler_params=pltpu.CompilerParams(vmem_limit_bytes=44 * MIB),
        cost_estimate=pl.CostEstimate(flops=4 * 10**9, bytes_accessed=8 * MIB, transcendentals=10**6),
        name="finish",
    )(
        count,
        held,
        query,
        wk,
        wv,
        *state,
        x,
        g1[None],
        b1[None],
        b_up[None],
        g2[None],
        b2[None],
        w_out,
        w_up,
        w_down,
    )


def pair_lists(held, z_high, core):
    size = held.shape[1]
    planes = lax.axis_size("zhi")
    slot = jnp.arange(size, dtype=jnp.int32)
    key_group = slot % (size // CAP)
    distance = z_high - key_group // SLAB_GROUPS
    distance = jnp.where(core == 0, distance, -distance) % planes
    query_index = held // MEMBERS
    key_slot = (distance * SLAB_BLOCKS + key_group % SLAB_GROUPS * MEMBERS)[None, :] + held % MEMBERS
    ahead = (query_index[:, None, :] < query_index[:, :, None]) | (
        (query_index[:, None, :] == query_index[:, :, None]) & (slot[None, None, :] < slot[None, :, None])
    )
    place = jnp.sum(ahead.astype(jnp.int32), axis=-1)
    pairs = jnp.sum(jnp.where(place[:, None, :] == slot[None, :, None], key_slot[:, None, :], 0), axis=-1)
    pairs = jnp.concatenate([pairs.reshape(-1), jnp.zeros((SLOTS,), jnp.int32)])
    member = jnp.arange(MEMBERS, dtype=jnp.int32)[None, :, None]
    start = jnp.sum((query_index[:, None, :] < member).astype(jnp.int32), axis=-1)
    count = jnp.sum((query_index[:, None, :] == member).astype(jnp.int32), axis=-1)
    start = start + size * jnp.arange(SLAB_GROUPS, dtype=jnp.int32)[:, None]
    return start.reshape(-1), count.reshape(-1), pairs


def gather_rings(tiles):
    size = lax.axis_size("zhi")

    def move(value, step):
        pairs = [
            (2 * z + core, 2 * ((z + (step if core == 0 else -step)) % size) + core)
            for z in range(size)
            for core in range(2)
        ]
        return lax.ppermute(value, ("zhi", "core"), pairs)

    ahead, behind = [tiles], [tiles]
    for step in range(size // 2):
        ahead.append(move(ahead[-1], 1))
        if step < (size - 1) // 2:
            behind.append(move(behind[-1], -1))
    return ahead + behind[:0:-1]


def swap(x, pairs):
    return lax.ppermute(x, AXES, [p for a, b in pairs for p in ((a, b), (b, a))])


def on_device(
    node_feats,
    graph_ids,
    pair_tiles,
    pair_count,
    w_query,
    w_key,
    w_value,
    w_out,
    ln1_gain,
    ln1_bias,
    w_up,
    b_up,
    w_down,
    ln2_gain,
    ln2_bias,
):
    z_high, own = lax.axis_index("zhi"), lax.axis_index(SLAB)
    devices = lax.axis_size(AXES)

    def exchange(value):
        return lax.all_to_all(value, SLAB, split_axis=0, concat_axis=0, tiled=True)

    got = exchange(pack(node_feats, pair_tiles, pair_count))
    beside = swap(node_feats, [(i, i + 1) for i in range(0, devices, 2)])
    across = swap(node_feats, [(i, i + 1) for i in range(1, devices - 1, 2)])
    tiles, beside, across = lax.optimization_barrier((got[:, :TILE_ROWS], beside, across))
    core = lax.axis_index("core")
    gathered = gather_rings(tiles)
    codes = got[::MEMBERS, TILE_ROWS:, : pair_tiles.shape[1]].astype(jnp.int32)
    start, count, pairs = pair_lists(codes.reshape(SLAB_GROUPS, -1), z_high, core)

    def mine(value):
        return lax.dynamic_slice_in_dim(value, own, 1, 0)

    fill = jnp.full((ROWS,), -1, jnp.int32)
    ids = jnp.concatenate([fill, graph_ids, fill])
    key_ids = lax.dynamic_slice_in_dim(ids, (z_high * SLAB_BLOCKS + own) * ROWS, 3 * ROWS, 0)
    query_ids = jnp.tile(key_ids[ROWS : 2 * ROWS], 2)[None, :]
    turned = key_ids.reshape(3, ROWS)[::-1].reshape(-1)
    key_ids = jnp.where(core == 0, turned, key_ids)
    query, *state = near(
        beside, node_feats, across, w_query, w_key, w_value, key_ids[:, None], query_ids
    )

    def fetch(at):
        held = exchange(select(start + jnp.minimum(at, count), pairs, gathered))
        return jnp.clip(mine(count) - at, 0, SLOTS), held

    def close(part, held, state):
        return finish(
            part,
            held,
            query,
            w_key,
            w_value,
            state,
            node_feats,
            ln1_gain,
            ln1_bias,
            b_up,
            ln2_gain,
            ln2_bias,
            w_out,
            w_up,
            w_down,
        )

    part, held = fetch(jnp.int32(0))
    out, *state = close(part, held, state)
    most = jnp.max(count)

    def go_on(state):
        def more(carry):
            at, state = carry
            part, held = fetch(at)
            return at + SLOTS, tuple(far(part, held, query, w_key, w_value, state))

        _, state = lax.while_loop(lambda carry: carry[0] < most, more, (jnp.int32(SLOTS), state))
        return close(jnp.zeros_like(part), held, state)[0]

    return lax.cond(most > SLOTS, go_on, lambda state: out, tuple(state))


def solution(mesh):
    inner = Mesh(mesh.devices.reshape(-1, 2, 2, 2, 4, 2), AXES)
    blk = ("zhi", "zlo", "ylo")
    in_specs = (P(AXES, None), P(), P(blk, None, None), P(blk, None)) + (P(),) * 11
    return jax.shard_map(
        on_device, mesh=inner, in_specs=in_specs, out_specs=P(AXES, None), check_vma=False
    )
```

```python
import jax
import jax.numpy as jnp
from jax import lax
from jax.experimental import pallas as pl
from jax.experimental.pallas import tpu as pltpu
from jax.sharding import Mesh
from jax.sharding import PartitionSpec as P

F32 = jnp.float32
BF16 = jnp.bfloat16

AXES = ("zhi", "zlo", "ylo", "yhi", "x", "core")
SLAB = ("zlo", "ylo", "yhi", "x", "core")
D = 512
FF = 1024
HEADS = 8
HEAD_DIM = 64
COUPLES = HEADS // 2
ROWS = 128
MEMBERS = 16
SLAB_GROUPS = 4
SLAB_BLOCKS = 64
CAP = 8
TILE_ROWS = 8
TILE_COLS = 128
COL_TILES = D // TILE_COLS
SLOTS = 15
GULP = 5
MIB = 1024 * 1024
FLOOR = -1e30

SMEM = pl.BlockSpec(memory_space=pltpu.SMEM)
VMEM = pl.BlockSpec(memory_space=pltpu.VMEM)


def absorb(state, keys, values, query_ref, mask=None, bias=()):
    bias = bias or (None,)
    size = keys.shape[0] // len(bias)
    new = []
    for couple in range(COUPLES):
        top, total, accum = state[couple]
        cols = slice(couple * 2 * HEAD_DIM, (couple + 1) * 2 * HEAD_DIM)
        scores = [
            jnp.dot(keys[n * size : (n + 1) * size, cols], query_ref[couple], preferred_element_type=F32)
            for n in range(len(bias))
        ]
        if mask is not None:
            scores = [jnp.where(mask, scores[0], FLOOR)]
        new_top = top
        for part, shift in zip(scores, bias):
            best = jnp.max(part, axis=0, keepdims=True)
            new_top = jnp.maximum(new_top, best if shift is None else best + shift)
        decay = jnp.exp(top - new_top)
        total = total * decay
        probs = []
        for part, shift in zip(scores, bias):
            prob = jnp.exp(part - (new_top if shift is None else new_top - shift))
            total = total + jnp.sum(prob, axis=0, keepdims=True)
            probs.append(prob.astype(BF16))
        part = lax.dot_general(
            values[:, cols],
            jnp.concatenate(probs, axis=0),
            (((0,), (0,)), ((), ())),
            preferred_element_type=F32,
        )
        accum = jnp.concatenate(
            [
                accum[:HEAD_DIM] * decay[:, :ROWS] + part[:HEAD_DIM, :ROWS],
                accum[HEAD_DIM:] * decay[:, ROWS:] + part[HEAD_DIM:, ROWS:],
            ],
            axis=0,
        )
        new.append((new_top, total, accum))
    return new


def read_state(top_ref, total_ref, accum_ref):
    return [
        (
            top_ref[c : c + 1, :],
            total_ref[c : c + 1, :],
            accum_ref[c * 2 * HEAD_DIM : (c + 1) * 2 * HEAD_DIM, :],
        )
        for c in range(COUPLES)
    ]


def write_state(state, top_ref, total_ref, accum_ref):
    for c, (top, total, accum) in enumerate(state):
        top_ref[c : c + 1, :] = top
        total_ref[c : c + 1, :] = total
        accum_ref[c * 2 * HEAD_DIM : (c + 1) * 2 * HEAD_DIM, :] = accum


def project(x, weight_ref):
    return jnp.dot(x, weight_ref[...], preferred_element_type=F32).astype(BF16)


STATE_SHAPES = (
    jax.ShapeDtypeStruct((COUPLES, 2 * ROWS), F32),
    jax.ShapeDtypeStruct((COUPLES, 2 * ROWS), F32),
    jax.ShapeDtypeStruct((D, ROWS), F32),
)


def near_kernel(
    beside_ref, x_ref, across_ref, wq_ref, wk_ref, wv_ref, kid_ref, qid_ref, query_ref, top_ref, total_ref, accum_ref
):
    x = x_ref[...]
    query = jnp.dot(x, wq_ref[...], preferred_element_type=F32).astype(BF16).astype(F32)
    query_t = (query.T * (1.0 / 8.0)).astype(BF16)
    zero = jnp.zeros((HEAD_DIM, ROWS), BF16)
    for couple in range(COUPLES):
        at = couple * 2 * HEAD_DIM
        first = query_t[at : at + HEAD_DIM]
        second = query_t[at + HEAD_DIM : at + 2 * HEAD_DIM]
        query_ref[couple] = jnp.concatenate(
            [jnp.concatenate([first, zero], axis=1), jnp.concatenate([zero, second], axis=1)], axis=0
        )
    state = [
        (
            jnp.full((1, 2 * ROWS), FLOOR, F32),
            jnp.zeros((1, 2 * ROWS), F32),
            jnp.zeros((2 * HEAD_DIM, ROWS), F32),
        )
    ] * COUPLES
    sources = jnp.concatenate([beside_ref[...], x, across_ref[...]], axis=0)
    mask = kid_ref[...] == qid_ref[...]
    state = absorb(state, project(sources, wk_ref), project(sources, wv_ref), query_ref, mask)
    write_state(state, top_ref, total_ref, accum_ref)


def near(beside, x, across, wq, wk, wv, key_ids, query_ids):
    return pl.pallas_call(
        near_kernel,
        out_shape=(jax.ShapeDtypeStruct((COUPLES, 2 * HEAD_DIM, 2 * ROWS), BF16),) + STATE_SHAPES,
        compiler_params=pltpu.CompilerParams(vmem_limit_bytes=32 * MIB),
        cost_estimate=pl.CostEstimate(flops=10**9, bytes_accessed=3 * MIB, transcendentals=400000),
        name="near",
    )(beside, x, across, wq, wk, wv, key_ids, query_ids)


def pack_kernel(x_ref, tiles_ref, counts_ref, out_ref):
    x = x_ref[...].astype(F32)
    used = lax.broadcasted_iota(jnp.int32, tiles_ref.shape, 0) < counts_ref[...]
    codes = jnp.where(used, tiles_ref[...], MEMBERS * MEMBERS).astype(F32)
    codes = jnp.concatenate([codes, jnp.zeros((CAP, TILE_COLS - codes.shape[1]), F32)], axis=1)
    for n in range(SLAB_BLOCKS):
        row, col = n // COL_TILES * TILE_ROWS, n % COL_TILES * TILE_COLS
        tile = x[row : row + TILE_ROWS, col : col + TILE_COLS]
        out_ref[n] = jnp.concatenate([tile, codes], axis=0).astype(BF16)


def pack(x, pair_tiles, pair_count):
    return pl.pallas_call(
        pack_kernel,
        out_shape=jax.ShapeDtypeStruct((SLAB_BLOCKS, TILE_ROWS + CAP, TILE_COLS), BF16),
        compiler_params=pltpu.CompilerParams(vmem_limit_bytes=60 * MIB),
        name="pack",
    )(x, pair_tiles[0].T, pair_count)


def select_kernel(at_ref, list_ref, *refs):
    sources, out_ref, all_ref = refs[:-2], refs[-2], refs[-1]
    for n, source in enumerate(sources):
        all_ref[n * SLAB_BLOCKS : (n + 1) * SLAB_BLOCKS] = source[...]

    def one(dest, carry):
        at = at_ref[dest]
        for slot in range(SLOTS):
            out_ref[dest, slot] = all_ref[list_ref[at + slot]]
        return carry

    lax.fori_loop(0, SLAB_BLOCKS, one, 0, unroll=4)


def select(at, pairs, gathered):
    return pl.pallas_call(
        select_kernel,
        in_specs=[SMEM] * 2 + [VMEM] * len(gathered),
        out_specs=VMEM,
        out_shape=jax.ShapeDtypeStruct((SLAB_BLOCKS, SLOTS, TILE_ROWS, TILE_COLS), BF16),
        scratch_shapes=[pltpu.VMEM((len(gathered) * SLAB_BLOCKS, TILE_ROWS, TILE_COLS), BF16)],
        compiler_params=pltpu.CompilerParams(vmem_limit_bytes=32 * MIB),
        cost_estimate=pl.CostEstimate(flops=0, bytes_accessed=12 * MIB, transcendentals=0),
        name="select",
    )(at, pairs, *gathered)


def patch_kernel(first_ref, last_ref, at_ref, list_ref, far_ref, held_ref, out_ref):
    out_ref[...] = held_ref[...]

    def one(dest, carry):
        at = at_ref[dest]

        def put(slot, carry):
            out_ref[dest, slot] = far_ref[lax.rem(list_ref[at + slot], SLAB_BLOCKS)]
            return carry

        return lax.fori_loop(first_ref[dest], last_ref[dest], put, carry)

    lax.fori_loop(0, SLAB_BLOCKS, one, 0)


def patch(first, last, at, pairs, far_tiles, held):
    return pl.pallas_call(
        patch_kernel,
        in_specs=[SMEM] * 4 + [VMEM] * 2,
        out_specs=VMEM,
        out_shape=jax.ShapeDtypeStruct(held.shape, held.dtype),
        compiler_params=pltpu.CompilerParams(vmem_limit_bytes=32 * MIB),
        name="patch",
    )(first, last, at, pairs, far_tiles, held)


def gather_block(held_ref, slot):
    rows = []
    for r in range(ROWS // TILE_ROWS):
        tiles = [held_ref[r * COL_TILES + c, slot].astype(F32) for c in range(COL_TILES)]
        rows.append(jnp.concatenate(tiles, axis=1))
    return jnp.concatenate(rows, axis=0).astype(BF16)


def far_steps(count, held_ref, query_ref, wk_ref, wv_ref, state_refs):
    def step(i, carry):
        slots = [GULP * i + u for u in range(GULP)]
        x = jnp.concatenate([gather_block(held_ref, slot) for slot in slots], axis=0)
        bias = [jnp.where(slot < count, 0.0, FLOOR).astype(F32) for slot in slots]
        state = read_state(*state_refs)
        state = absorb(state, project(x, wk_ref), project(x, wv_ref), query_ref, bias=bias)
        write_state(state, *state_refs)
        return carry

    lax.fori_loop(0, (count + GULP - 1) // GULP, step, 0)


def far_kernel(
    count_ref, held_ref, query_ref, wk_ref, wv_ref, top_in, total_in, accum_in, top_ref, total_ref, accum_ref
):
    top_ref[...] = top_in[...]
    total_ref[...] = total_in[...]
    accum_ref[...] = accum_in[...]
    far_steps(count_ref[0], held_ref, query_ref, wk_ref, wv_ref, (top_ref, total_ref, accum_ref))


def far(count, held, query, wk, wv, state):
    return pl.pallas_call(
        far_kernel,
        in_specs=[SMEM] + [VMEM] * 7,
        out_specs=(VMEM,) * 3,
        out_shape=STATE_SHAPES,
        compiler_params=pltpu.CompilerParams(vmem_limit_bytes=32 * MIB),
        name="far",
    )(count, held, query, wk, wv, *state)


def layer_norm(value, gain, bias):
    mean = jnp.mean(value, -1, keepdims=True)
    centred = value - mean
    spread = jnp.mean(centred * centred, -1, keepdims=True)
    return centred * lax.rsqrt(spread + 1e-05) * gain + bias


def finish_kernel(
    count_ref,
    held_ref,
    query_ref,
    wk_ref,
    wv_ref,
    top_in,
    total_in,
    accum_in,
    x_ref,
    g1_ref,
    b1_ref,
    b_up_ref,
    g2_ref,
    b2_ref,
    w_out_hbm,
    w_up_hbm,
    w_down_hbm,
    out_ref,
    top_ref,
    total_ref,
    accum_ref,
    w_out_ref,
    w_up_ref,
    w_down_ref,
    sems,
):
    weights = ((w_out_hbm, w_out_ref), (w_up_hbm, w_up_ref), (w_down_hbm, w_down_ref))
    copies = [pltpu.make_async_copy(a, b, sems.at[n]) for n, (a, b) in enumerate(weights)]
    for copy in copies:
        copy.start()
    far_kernel(
        count_ref,
        held_ref,
        query_ref,
        wk_ref,
        wv_ref,
        top_in,
        total_in,
        accum_in,
        top_ref,
        total_ref,
        accum_ref,
    )
    columns = []
    for head in range(HEADS):
        lanes = slice(head % 2 * ROWS, (head % 2 + 1) * ROWS)
        total = total_ref[head // 2 : head // 2 + 1, lanes]
        accum = accum_ref[head * HEAD_DIM : (head + 1) * HEAD_DIM, :]
        columns.append((accum / total).astype(BF16))
    attended_t = jnp.concatenate(columns, axis=0)
    copies[0].wait()
    mixed = x_ref[...].astype(F32) + lax.dot_general(
        attended_t, w_out_ref[...], (((0,), (0,)), ((), ())), preferred_element_type=F32
    )
    normed = layer_norm(mixed, g1_ref[...], b1_ref[...]).astype(BF16)
    copies[1].wait()
    hidden = jnp.maximum(
        jnp.dot(normed, w_up_ref[...], preferred_element_type=F32) + b_up_ref[...], 0.0
    ).astype(BF16)
    copies[2].wait()
    second = normed.astype(F32) + jnp.dot(hidden, w_down_ref[...], preferred_element_type=F32)
    out_ref[...] = layer_norm(second, g2_ref[...], b2_ref[...])


def finish(count, held, query, wk, wv, state, x, g1, b1, b_up, g2, b2, w_out, w_up, w_down):
    hbm = pl.BlockSpec(memory_space=pltpu.HBM)
    return pl.pallas_call(
        finish_kernel,
        in_specs=[SMEM] + [VMEM] * 13 + [hbm] * 3,
        out_specs=(VMEM,) * 4,
        out_shape=(jax.ShapeDtypeStruct((ROWS, D), F32),) + STATE_SHAPES,
        scratch_shapes=[
            pltpu.VMEM((D, D), BF16),
            pltpu.VMEM((D, FF), BF16),
            pltpu.VMEM((FF, D), BF16),
            pltpu.SemaphoreType.DMA((3,)),
        ],
        compiler_params=pltpu.CompilerParams(vmem_limit_bytes=44 * MIB),
        cost_estimate=pl.CostEstimate(flops=4 * 10**9, bytes_accessed=8 * MIB, transcendentals=10**6),
        name="finish",
    )(
        count,
        held,
        query,
        wk,
        wv,
        *state,
        x,
        g1[None],
        b1[None],
        b_up[None],
        g2[None],
        b2[None],
        w_out,
        w_up,
        w_down,
    )


def pair_lists(held, z_high, core):
    size = held.shape[1]
    planes = lax.axis_size("zhi")
    slot = jnp.arange(size, dtype=jnp.int32)
    key_group = slot % (size // CAP)
    distance = z_high - key_group // SLAB_GROUPS
    distance = jnp.where(core == 0, distance, -distance) % planes
    order = held // MEMBERS * 2 + (distance == planes // 2).astype(jnp.int32)[None, :]
    key_slot = (distance * SLAB_BLOCKS + key_group % SLAB_GROUPS * MEMBERS)[None, :] + held % MEMBERS
    ahead = (order[:, None, :] < order[:, :, None]) | (
        (order[:, None, :] == order[:, :, None]) & (slot[None, None, :] < slot[None, :, None])
    )
    place = jnp.sum(ahead.astype(jnp.int32), axis=-1)
    pairs = jnp.sum(jnp.where(place[:, None, :] == slot[None, :, None], key_slot[:, None, :], 0), axis=-1)
    pairs = jnp.concatenate([pairs.reshape(-1), jnp.zeros((SLOTS,), jnp.int32)])
    member = 2 * jnp.arange(MEMBERS, dtype=jnp.int32)[None, :, None]
    order = order[:, None, :]
    start = jnp.sum((order < member).astype(jnp.int32), axis=-1)
    early = jnp.sum((order == member).astype(jnp.int32), axis=-1)
    count = early + jnp.sum((order == member + 1).astype(jnp.int32), axis=-1)
    start = start + size * jnp.arange(SLAB_GROUPS, dtype=jnp.int32)[:, None]
    return start.reshape(-1), early.reshape(-1), count.reshape(-1), pairs


def gather_rings(tiles):
    size = lax.axis_size("zhi")

    def move(value, step):
        pairs = [
            (2 * z + core, 2 * ((z + (step if core == 0 else -step)) % size) + core)
            for z in range(size)
            for core in range(2)
        ]
        return lax.ppermute(value, ("zhi", "core"), pairs)

    ahead, behind = [tiles], [tiles]
    for step in range(size // 2):
        ahead.append(move(ahead[-1], 1))
        if step < (size - 1) // 2:
            behind.append(move(behind[-1], -1))
    return ahead[:-1] + [tiles] + behind[:0:-1], ahead[-1]


def swap(x, pairs):
    return lax.ppermute(x, AXES, [p for a, b in pairs for p in ((a, b), (b, a))])


def on_device(
    node_feats,
    graph_ids,
    pair_tiles,
    pair_count,
    w_query,
    w_key,
    w_value,
    w_out,
    ln1_gain,
    ln1_bias,
    w_up,
    b_up,
    w_down,
    ln2_gain,
    ln2_bias,
):
    z_high, own = lax.axis_index("zhi"), lax.axis_index(SLAB)
    devices = lax.axis_size(AXES)

    def exchange(value):
        return lax.all_to_all(value, SLAB, split_axis=0, concat_axis=0, tiled=True)

    got = exchange(pack(node_feats, pair_tiles, pair_count))
    beside = swap(node_feats, [(i, i + 1) for i in range(0, devices, 2)])
    across = swap(node_feats, [(i, i + 1) for i in range(1, devices - 1, 2)])
    tiles, beside, across = lax.optimization_barrier((got[:, :TILE_ROWS], beside, across))
    core = lax.axis_index("core")
    gathered, far_tiles = gather_rings(tiles)
    codes = got[::MEMBERS, TILE_ROWS:, : pair_tiles.shape[1]].astype(jnp.int32)
    start, early, count, pairs = pair_lists(codes.reshape(SLAB_GROUPS, -1), z_high, core)

    def mine(value):
        return lax.dynamic_slice_in_dim(value, own, 1, 0)

    fill = jnp.full((ROWS,), -1, jnp.int32)
    ids = jnp.concatenate([fill, graph_ids, fill])
    key_ids = lax.dynamic_slice_in_dim(ids, (z_high * SLAB_BLOCKS + own) * ROWS, 3 * ROWS, 0)
    query_ids = jnp.tile(key_ids[ROWS : 2 * ROWS], 2)[None, :]
    turned = key_ids.reshape(3, ROWS)[::-1].reshape(-1)
    key_ids = jnp.where(core == 0, turned, key_ids)
    query, *state = near(
        beside, node_feats, across, w_query, w_key, w_value, key_ids[:, None], query_ids
    )

    def fetch(at):
        here = start + jnp.minimum(at, count)
        first = jnp.clip(early - at, 0, SLOTS)
        last = jnp.clip(count - at, 0, SLOTS)
        held = patch(first, last, here, pairs, far_tiles, select(here, pairs, gathered))
        return mine(last), exchange(held)

    def close(part, held, state):
        return finish(
            part,
            held,
            query,
            w_key,
            w_value,
            state,
            node_feats,
            ln1_gain,
            ln1_bias,
            b_up,
            ln2_gain,
            ln2_bias,
            w_out,
            w_up,
            w_down,
        )

    part, held = fetch(jnp.int32(0))
    out, *state = close(part, held, state)
    most = jnp.max(count)

    def go_on(state):
        def more(carry):
            at, state = carry
            part, held = fetch(at)
            return at + SLOTS, tuple(far(part, held, query, w_key, w_value, state))

        _, state = lax.while_loop(lambda carry: carry[0] < most, more, (jnp.int32(SLOTS), state))
        return close(jnp.zeros_like(part), held, state)[0]

    return lax.cond(most > SLOTS, go_on, lambda state: out, tuple(state))


def solution(mesh):
    inner = Mesh(mesh.devices.reshape(-1, 2, 2, 2, 4, 2), AXES)
    blk = ("zhi", "zlo", "ylo")
    in_specs = (P(AXES, None), P(), P(blk, None, None), P(blk, None)) + (P(),) * 11
    return jax.shard_map(
        on_device, mesh=inner, in_specs=in_specs, out_specs=P(AXES, None), check_vma=False
    )
```

```python
import jax
import jax.numpy as jnp
from jax import lax
from jax.experimental import pallas as pl
from jax.experimental.pallas import tpu as pltpu
from jax.sharding import Mesh
from jax.sharding import PartitionSpec as P

F32 = jnp.float32
BF16 = jnp.bfloat16

AXES = ("zhi", "zlo", "ylo", "yhi", "x", "core")
SLAB = ("zlo", "ylo", "yhi", "x", "core")
D = 512
FF = 1024
HEADS = 8
HEAD_DIM = 64
COUPLES = HEADS // 2
ROWS = 128
MEMBERS = 16
SLAB_GROUPS = 4
SLAB_BLOCKS = 64
CAP = 8
TILE_ROWS = 8
TILE_COLS = 128
COL_TILES = D // TILE_COLS
SLOTS = 15
GULP = 5
MIB = 1024 * 1024
FLOOR = -1e30

SMEM = pl.BlockSpec(memory_space=pltpu.SMEM)
VMEM = pl.BlockSpec(memory_space=pltpu.VMEM)


def absorb(state, keys, values, query_ref, mask=None, bias=()):
    bias = bias or (None,)
    size = keys.shape[0] // len(bias)
    new = []
    for couple in range(COUPLES):
        top, total, accum = state[couple]
        cols = slice(couple * 2 * HEAD_DIM, (couple + 1) * 2 * HEAD_DIM)
        scores = [
            jnp.dot(keys[n * size : (n + 1) * size, cols], query_ref[couple], preferred_element_type=F32)
            for n in range(len(bias))
        ]
        if mask is not None:
            scores = [jnp.where(mask, scores[0], FLOOR)]
        new_top = top
        for part, shift in zip(scores, bias):
            best = jnp.max(part, axis=0, keepdims=True)
            new_top = jnp.maximum(new_top, best if shift is None else best + shift)
        decay = jnp.exp(top - new_top)
        total = total * decay
        probs = []
        for part, shift in zip(scores, bias):
            prob = jnp.exp(part - (new_top if shift is None else new_top - shift))
            total = total + jnp.sum(prob, axis=0, keepdims=True)
            probs.append(prob.astype(BF16))
        part = lax.dot_general(
            values[:, cols],
            jnp.concatenate(probs, axis=0),
            (((0,), (0,)), ((), ())),
            preferred_element_type=F32,
        )
        accum = jnp.concatenate(
            [
                accum[:HEAD_DIM] * decay[:, :ROWS] + part[:HEAD_DIM, :ROWS],
                accum[HEAD_DIM:] * decay[:, ROWS:] + part[HEAD_DIM:, ROWS:],
            ],
            axis=0,
        )
        new.append((new_top, total, accum))
    return new


def read_state(top_ref, total_ref, accum_ref):
    return [
        (
            top_ref[c : c + 1, :],
            total_ref[c : c + 1, :],
            accum_ref[c * 2 * HEAD_DIM : (c + 1) * 2 * HEAD_DIM, :],
        )
        for c in range(COUPLES)
    ]


def write_state(state, top_ref, total_ref, accum_ref):
    for c, (top, total, accum) in enumerate(state):
        top_ref[c : c + 1, :] = top
        total_ref[c : c + 1, :] = total
        accum_ref[c * 2 * HEAD_DIM : (c + 1) * 2 * HEAD_DIM, :] = accum


def project(x, weight_ref):
    return jnp.dot(x, weight_ref[...], preferred_element_type=F32).astype(BF16)


STATE_SHAPES = (
    jax.ShapeDtypeStruct((COUPLES, 2 * ROWS), F32),
    jax.ShapeDtypeStruct((COUPLES, 2 * ROWS), F32),
    jax.ShapeDtypeStruct((D, ROWS), F32),
)


def near_kernel(
    beside_ref, x_ref, across_ref, wq_ref, wk_ref, wv_ref, kid_ref, qid_ref, query_ref, top_ref, total_ref, accum_ref
):
    x = x_ref[...]
    query = jnp.dot(x, wq_ref[...], preferred_element_type=F32).astype(BF16).astype(F32)
    query_t = (query.T * (1.0 / 8.0)).astype(BF16)
    zero = jnp.zeros((HEAD_DIM, ROWS), BF16)
    for couple in range(COUPLES):
        at = couple * 2 * HEAD_DIM
        first = query_t[at : at + HEAD_DIM]
        second = query_t[at + HEAD_DIM : at + 2 * HEAD_DIM]
        query_ref[couple] = jnp.concatenate(
            [jnp.concatenate([first, zero], axis=1), jnp.concatenate([zero, second], axis=1)], axis=0
        )
    state = [
        (
            jnp.full((1, 2 * ROWS), FLOOR, F32),
            jnp.zeros((1, 2 * ROWS), F32),
            jnp.zeros((2 * HEAD_DIM, ROWS), F32),
        )
    ] * COUPLES
    sources = jnp.concatenate([beside_ref[...], x, across_ref[...]], axis=0)
    mask = kid_ref[...] == qid_ref[...]
    state = absorb(state, project(sources, wk_ref), project(sources, wv_ref), query_ref, mask)
    write_state(state, top_ref, total_ref, accum_ref)


def near(beside, x, across, wq, wk, wv, key_ids, query_ids):
    return pl.pallas_call(
        near_kernel,
        out_shape=(jax.ShapeDtypeStruct((COUPLES, 2 * HEAD_DIM, 2 * ROWS), BF16),) + STATE_SHAPES,
        compiler_params=pltpu.CompilerParams(vmem_limit_bytes=32 * MIB),
        cost_estimate=pl.CostEstimate(flops=10**9, bytes_accessed=3 * MIB, transcendentals=400000),
        name="near",
    )(beside, x, across, wq, wk, wv, key_ids, query_ids)


def pack_kernel(x_ref, tiles_ref, counts_ref, out_ref):
    x = x_ref[...].astype(F32)
    used = lax.broadcasted_iota(jnp.int32, tiles_ref.shape, 0) < counts_ref[...]
    codes = jnp.where(used, tiles_ref[...], MEMBERS * MEMBERS).astype(F32)
    codes = jnp.concatenate([codes, jnp.zeros((CAP, TILE_COLS - codes.shape[1]), F32)], axis=1)
    for n in range(SLAB_BLOCKS):
        row, col = n // COL_TILES * TILE_ROWS, n % COL_TILES * TILE_COLS
        tile = x[row : row + TILE_ROWS, col : col + TILE_COLS]
        out_ref[n] = jnp.concatenate([tile, codes], axis=0).astype(BF16)


def pack(x, pair_tiles, pair_count):
    return pl.pallas_call(
        pack_kernel,
        out_shape=jax.ShapeDtypeStruct((SLAB_BLOCKS, TILE_ROWS + CAP, TILE_COLS), BF16),
        compiler_params=pltpu.CompilerParams(vmem_limit_bytes=60 * MIB),
        name="pack",
    )(x, pair_tiles[0].T, pair_count)


def select_kernel(at_ref, list_ref, *refs):
    sources, out_ref, all_ref = refs[:-2], refs[-2], refs[-1]
    at = 0
    for source in sources:
        all_ref[at : at + source.shape[0]] = source[...]
        at += source.shape[0]

    def one(dest, carry):
        at = at_ref[dest]
        for slot in range(SLOTS):
            out_ref[dest, slot] = all_ref[list_ref[at + slot]]
        return carry

    lax.fori_loop(0, SLAB_BLOCKS, one, 0, unroll=4)


def select(at, pairs, gathered):
    return pl.pallas_call(
        select_kernel,
        in_specs=[SMEM] * 2 + [VMEM] * len(gathered),
        out_specs=VMEM,
        out_shape=jax.ShapeDtypeStruct((SLAB_BLOCKS, SLOTS, TILE_ROWS, TILE_COLS), BF16),
        scratch_shapes=[pltpu.VMEM((sum(g.shape[0] for g in gathered), TILE_ROWS, TILE_COLS), BF16)],
        compiler_params=pltpu.CompilerParams(vmem_limit_bytes=32 * MIB),
        cost_estimate=pl.CostEstimate(flops=0, bytes_accessed=8 * MIB, transcendentals=0),
        name="select",
    )(at, pairs, *gathered)


def gather_block(held_ref, slot):
    rows = []
    for r in range(ROWS // TILE_ROWS):
        tiles = [held_ref[r * COL_TILES + c, slot].astype(F32) for c in range(COL_TILES)]
        rows.append(jnp.concatenate(tiles, axis=1))
    return jnp.concatenate(rows, axis=0).astype(BF16)


def far_steps(count, held_ref, query_ref, wk_ref, wv_ref, state_refs):
    def step(i, carry):
        slots = [GULP * i + u for u in range(GULP)]
        x = jnp.concatenate([gather_block(held_ref, slot) for slot in slots], axis=0)
        bias = [jnp.where(slot < count, 0.0, FLOOR).astype(F32) for slot in slots]
        state = read_state(*state_refs)
        state = absorb(state, project(x, wk_ref), project(x, wv_ref), query_ref, bias=bias)
        write_state(state, *state_refs)
        return carry

    lax.fori_loop(0, (count + GULP - 1) // GULP, step, 0)


def far_kernel(
    count_ref, held_ref, query_ref, wk_ref, wv_ref, top_in, total_in, accum_in, top_ref, total_ref, accum_ref
):
    top_ref[...] = top_in[...]
    total_ref[...] = total_in[...]
    accum_ref[...] = accum_in[...]
    far_steps(count_ref[0], held_ref, query_ref, wk_ref, wv_ref, (top_ref, total_ref, accum_ref))


def far(count, held, query, wk, wv, state):
    return pl.pallas_call(
        far_kernel,
        in_specs=[SMEM] + [VMEM] * 7,
        out_specs=(VMEM,) * 3,
        out_shape=STATE_SHAPES,
        compiler_params=pltpu.CompilerParams(vmem_limit_bytes=32 * MIB),
        name="far",
    )(count, held, query, wk, wv, *state)


def layer_norm(value, gain, bias):
    mean = jnp.mean(value, -1, keepdims=True)
    centred = value - mean
    spread = jnp.mean(centred * centred, -1, keepdims=True)
    return centred * lax.rsqrt(spread + 1e-05) * gain + bias


def finish_kernel(
    count_ref,
    held_ref,
    query_ref,
    wk_ref,
    wv_ref,
    top_in,
    total_in,
    accum_in,
    x_ref,
    g1_ref,
    b1_ref,
    b_up_ref,
    g2_ref,
    b2_ref,
    w_out_hbm,
    w_up_hbm,
    w_down_hbm,
    out_ref,
    top_ref,
    total_ref,
    accum_ref,
    w_out_ref,
    w_up_ref,
    w_down_ref,
    sems,
):
    weights = ((w_out_hbm, w_out_ref), (w_up_hbm, w_up_ref), (w_down_hbm, w_down_ref))
    copies = [pltpu.make_async_copy(a, b, sems.at[n]) for n, (a, b) in enumerate(weights)]
    for copy in copies:
        copy.start()
    far_kernel(
        count_ref,
        held_ref,
        query_ref,
        wk_ref,
        wv_ref,
        top_in,
        total_in,
        accum_in,
        top_ref,
        total_ref,
        accum_ref,
    )
    columns = []
    for head in range(HEADS):
        lanes = slice(head % 2 * ROWS, (head % 2 + 1) * ROWS)
        total = total_ref[head // 2 : head // 2 + 1, lanes]
        accum = accum_ref[head * HEAD_DIM : (head + 1) * HEAD_DIM, :]
        columns.append((accum / total).astype(BF16))
    attended_t = jnp.concatenate(columns, axis=0)
    copies[0].wait()
    mixed = x_ref[...].astype(F32) + lax.dot_general(
        attended_t, w_out_ref[...], (((0,), (0,)), ((), ())), preferred_element_type=F32
    )
    normed = layer_norm(mixed, g1_ref[...], b1_ref[...]).astype(BF16)
    copies[1].wait()
    hidden = jnp.maximum(
        jnp.dot(normed, w_up_ref[...], preferred_element_type=F32) + b_up_ref[...], 0.0
    ).astype(BF16)
    copies[2].wait()
    second = normed.astype(F32) + jnp.dot(hidden, w_down_ref[...], preferred_element_type=F32)
    out_ref[...] = layer_norm(second, g2_ref[...], b2_ref[...])


def finish(count, held, query, wk, wv, state, x, g1, b1, b_up, g2, b2, w_out, w_up, w_down):
    hbm = pl.BlockSpec(memory_space=pltpu.HBM)
    return pl.pallas_call(
        finish_kernel,
        in_specs=[SMEM] + [VMEM] * 13 + [hbm] * 3,
        out_specs=(VMEM,) * 4,
        out_shape=(jax.ShapeDtypeStruct((ROWS, D), F32),) + STATE_SHAPES,
        scratch_shapes=[
            pltpu.VMEM((D, D), BF16),
            pltpu.VMEM((D, FF), BF16),
            pltpu.VMEM((FF, D), BF16),
            pltpu.SemaphoreType.DMA((3,)),
        ],
        compiler_params=pltpu.CompilerParams(vmem_limit_bytes=44 * MIB),
        cost_estimate=pl.CostEstimate(flops=4 * 10**9, bytes_accessed=8 * MIB, transcendentals=10**6),
        name="finish",
    )(
        count,
        held,
        query,
        wk,
        wv,
        *state,
        x,
        g1[None],
        b1[None],
        b_up[None],
        g2[None],
        b2[None],
        w_out,
        w_up,
        w_down,
    )


def pair_lists(held, z_high, core):
    size = held.shape[1]
    planes = lax.axis_size("zhi")
    slot = jnp.arange(size, dtype=jnp.int32)
    key_group = slot % (size // CAP)
    distance = z_high - key_group // SLAB_GROUPS
    distance = jnp.where(core == 0, distance, -distance) % planes
    query_index = held // MEMBERS
    key_slot = (distance * SLAB_BLOCKS + key_group % SLAB_GROUPS * MEMBERS)[None, :] + held % MEMBERS
    ahead = (query_index[:, None, :] < query_index[:, :, None]) | (
        (query_index[:, None, :] == query_index[:, :, None]) & (slot[None, None, :] < slot[None, :, None])
    )
    place = jnp.sum(ahead.astype(jnp.int32), axis=-1)
    pairs = jnp.sum(jnp.where(place[:, None, :] == slot[None, :, None], key_slot[:, None, :], 0), axis=-1)
    pairs = jnp.concatenate([pairs.reshape(-1), jnp.zeros((SLOTS,), jnp.int32)])
    member = jnp.arange(MEMBERS, dtype=jnp.int32)[None, :, None]
    start = jnp.sum((query_index[:, None, :] < member).astype(jnp.int32), axis=-1)
    count = jnp.sum((query_index[:, None, :] == member).astype(jnp.int32), axis=-1)
    start = start + size * jnp.arange(SLAB_GROUPS, dtype=jnp.int32)[:, None]
    return start.reshape(-1), count.reshape(-1), pairs


def gather_rings(tiles, codes):
    size = lax.axis_size("zhi")

    def move(value, step):
        pairs = [
            (2 * z + core, 2 * ((z + (step if core == 0 else -step)) % size) + core)
            for z in range(size)
            for core in range(2)
        ]
        return lax.ppermute(value, ("zhi", "core"), pairs)

    ahead, behind = [tiles], [tiles]
    for step in range(size // 2):
        if step == size // 2 - 1:
            ahead[-1], codes = lax.optimization_barrier((ahead[-1], codes))
        ahead.append(move(ahead[-1], 1))
        if step < (size - 1) // 2:
            behind.append(move(behind[-1], -1))
    return ahead + behind[:0:-1], codes


def swap(x, pairs):
    return lax.ppermute(x, AXES, [p for a, b in pairs for p in ((a, b), (b, a))])


def on_device(
    node_feats,
    graph_ids,
    pair_tiles,
    pair_count,
    w_query,
    w_key,
    w_value,
    w_out,
    ln1_gain,
    ln1_bias,
    w_up,
    b_up,
    w_down,
    ln2_gain,
    ln2_bias,
):
    z_high, own = lax.axis_index("zhi"), lax.axis_index(SLAB)
    devices = lax.axis_size(AXES)

    def exchange(value):
        return lax.all_to_all(value, SLAB, split_axis=0, concat_axis=0, tiled=True)

    got = exchange(pack(node_feats, pair_tiles, pair_count))
    beside = swap(node_feats, [(i, i + 1) for i in range(0, devices, 2)])
    across = swap(node_feats, [(i, i + 1) for i in range(1, devices - 1, 2)])
    tiles, beside, across = lax.optimization_barrier((got[:, :TILE_ROWS], beside, across))
    core = lax.axis_index("core")
    codes = got[::MEMBERS, TILE_ROWS:, : pair_tiles.shape[1]].astype(jnp.int32)
    gathered, codes = gather_rings(tiles, codes)
    start, count, pairs = pair_lists(codes.reshape(SLAB_GROUPS, -1), z_high, core)

    def mine(value):
        return lax.dynamic_slice_in_dim(value, own, 1, 0)

    fill = jnp.full((ROWS,), -1, jnp.int32)
    ids = jnp.concatenate([fill, graph_ids, fill])
    key_ids = lax.dynamic_slice_in_dim(ids, (z_high * SLAB_BLOCKS + own) * ROWS, 3 * ROWS, 0)
    query_ids = jnp.tile(key_ids[ROWS : 2 * ROWS], 2)[None, :]
    turned = key_ids.reshape(3, ROWS)[::-1].reshape(-1)
    key_ids = jnp.where(core == 0, turned, key_ids)
    query, *state = near(
        beside, node_feats, across, w_query, w_key, w_value, key_ids[:, None], query_ids
    )

    def fetch(at):
        held = exchange(select(start + jnp.minimum(at, count), pairs, gathered))
        return jnp.clip(mine(count) - at, 0, SLOTS), held

    def close(part, held, state):
        return finish(
            part,
            held,
            query,
            w_key,
            w_value,
            state,
            node_feats,
            ln1_gain,
            ln1_bias,
            b_up,
            ln2_gain,
            ln2_bias,
            w_out,
            w_up,
            w_down,
        )

    part, held = fetch(jnp.int32(0))
    out, *state = close(part, held, state)
    most = jnp.max(count)

    def go_on(state):
        def more(carry):
            at, state = carry
            part, held = fetch(at)
            return at + SLOTS, tuple(far(part, held, query, w_key, w_value, state))

        _, state = lax.while_loop(lambda carry: carry[0] < most, more, (jnp.int32(SLOTS), state))
        return close(jnp.zeros_like(part), held, state)[0]

    return lax.cond(most > SLOTS, go_on, lambda state: out, tuple(state))


def solution(mesh):
    inner = Mesh(mesh.devices.reshape(-1, 2, 2, 2, 4, 2), AXES)
    blk = ("zhi", "zlo", "ylo")
    in_specs = (P(AXES, None), P(), P(blk, None, None), P(blk, None)) + (P(),) * 11
    return jax.shard_map(
        on_device, mesh=inner, in_specs=in_specs, out_specs=P(AXES, None), check_vma=False
    )
```

```python
import jax
import jax.numpy as jnp
from jax import lax
from jax.experimental import pallas as pl
from jax.experimental.pallas import tpu as pltpu
from jax.sharding import Mesh
from jax.sharding import PartitionSpec as P

F32 = jnp.float32
BF16 = jnp.bfloat16

AXES = ("zhi", "zlo", "ylo", "yhi", "x", "core")
SLAB = ("zlo", "ylo", "yhi", "x", "core")
D = 512
FF = 1024
HEADS = 8
HEAD_DIM = 64
COUPLES = HEADS // 2
ROWS = 128
MEMBERS = 16
SLAB_GROUPS = 4
SLAB_BLOCKS = 64
CAP = 8
TILE_ROWS = 8
TILE_COLS = 128
COL_TILES = D // TILE_COLS
SLOTS = 15
GULP = 5
MIB = 1024 * 1024
FLOOR = -1e30

SMEM = pl.BlockSpec(memory_space=pltpu.SMEM)
VMEM = pl.BlockSpec(memory_space=pltpu.VMEM)


def absorb(state, keys, values, query_ref, mask=None, bias=()):
    bias = bias or (None,)
    size = keys.shape[0] // len(bias)
    new = []
    for couple in range(COUPLES):
        top, total, accum = state[couple]
        cols = slice(couple * 2 * HEAD_DIM, (couple + 1) * 2 * HEAD_DIM)
        scores = [
            jnp.dot(keys[n * size : (n + 1) * size, cols], query_ref[couple], preferred_element_type=F32)
            for n in range(len(bias))
        ]
        if mask is not None:
            scores = [jnp.where(mask, scores[0], FLOOR)]
        new_top = top
        for part, shift in zip(scores, bias):
            best = jnp.max(part, axis=0, keepdims=True)
            new_top = jnp.maximum(new_top, best if shift is None else best + shift)
        decay = jnp.exp(top - new_top)
        total = total * decay
        probs = []
        for part, shift in zip(scores, bias):
            prob = jnp.exp(part - (new_top if shift is None else new_top - shift))
            total = total + jnp.sum(prob, axis=0, keepdims=True)
            probs.append(prob.astype(BF16))
        part = lax.dot_general(
            values[:, cols],
            jnp.concatenate(probs, axis=0),
            (((0,), (0,)), ((), ())),
            preferred_element_type=F32,
        )
        accum = jnp.concatenate(
            [
                accum[:HEAD_DIM] * decay[:, :ROWS] + part[:HEAD_DIM, :ROWS],
                accum[HEAD_DIM:] * decay[:, ROWS:] + part[HEAD_DIM:, ROWS:],
            ],
            axis=0,
        )
        new.append((new_top, total, accum))
    return new


def read_state(top_ref, total_ref, accum_ref):
    return [
        (
            top_ref[c : c + 1, :],
            total_ref[c : c + 1, :],
            accum_ref[c * 2 * HEAD_DIM : (c + 1) * 2 * HEAD_DIM, :],
        )
        for c in range(COUPLES)
    ]


def write_state(state, top_ref, total_ref, accum_ref):
    for c, (top, total, accum) in enumerate(state):
        top_ref[c : c + 1, :] = top
        total_ref[c : c + 1, :] = total
        accum_ref[c * 2 * HEAD_DIM : (c + 1) * 2 * HEAD_DIM, :] = accum


def project(x, weight_ref):
    return jnp.dot(x, weight_ref[...], preferred_element_type=F32).astype(BF16)


STATE_SHAPES = (
    jax.ShapeDtypeStruct((COUPLES, 2 * ROWS), F32),
    jax.ShapeDtypeStruct((COUPLES, 2 * ROWS), F32),
    jax.ShapeDtypeStruct((D, ROWS), F32),
)


def near_kernel(
    beside_ref, x_ref, across_ref, wq_ref, wk_ref, wv_ref, kid_ref, qid_ref, query_ref, top_ref, total_ref, accum_ref
):
    x = x_ref[...]
    query = jnp.dot(x, wq_ref[...], preferred_element_type=F32).astype(BF16).astype(F32)
    query_t = (query.T * (1.0 / 8.0)).astype(BF16)
    zero = jnp.zeros((HEAD_DIM, ROWS), BF16)
    for couple in range(COUPLES):
        at = couple * 2 * HEAD_DIM
        first = query_t[at : at + HEAD_DIM]
        second = query_t[at + HEAD_DIM : at + 2 * HEAD_DIM]
        query_ref[couple] = jnp.concatenate(
            [jnp.concatenate([first, zero], axis=1), jnp.concatenate([zero, second], axis=1)], axis=0
        )
    state = [
        (
            jnp.full((1, 2 * ROWS), FLOOR, F32),
            jnp.zeros((1, 2 * ROWS), F32),
            jnp.zeros((2 * HEAD_DIM, ROWS), F32),
        )
    ] * COUPLES
    sources = jnp.concatenate([beside_ref[...], x, across_ref[...]], axis=0)
    mask = kid_ref[...] == qid_ref[...]
    state = absorb(state, project(sources, wk_ref), project(sources, wv_ref), query_ref, mask)
    write_state(state, top_ref, total_ref, accum_ref)


def near(beside, x, across, wq, wk, wv, key_ids, query_ids):
    return pl.pallas_call(
        near_kernel,
        out_shape=(jax.ShapeDtypeStruct((COUPLES, 2 * HEAD_DIM, 2 * ROWS), BF16),) + STATE_SHAPES,
        compiler_params=pltpu.CompilerParams(vmem_limit_bytes=32 * MIB),
        cost_estimate=pl.CostEstimate(flops=10**9, bytes_accessed=3 * MIB, transcendentals=400000),
        name="near",
    )(beside, x, across, wq, wk, wv, key_ids, query_ids)


def pack_kernel(x_ref, tiles_ref, counts_ref, out_ref):
    x = x_ref[...].astype(F32)
    used = lax.broadcasted_iota(jnp.int32, tiles_ref.shape, 0) < counts_ref[...]
    codes = jnp.where(used, tiles_ref[...], MEMBERS * MEMBERS).astype(F32)
    codes = jnp.concatenate([codes, jnp.zeros((CAP, TILE_COLS - codes.shape[1]), F32)], axis=1)
    for n in range(SLAB_BLOCKS):
        row, col = n // COL_TILES * TILE_ROWS, n % COL_TILES * TILE_COLS
        tile = x[row : row + TILE_ROWS, col : col + TILE_COLS]
        out_ref[n] = jnp.concatenate([tile, codes], axis=0).astype(BF16)


def pack(x, pair_tiles, pair_count):
    return pl.pallas_call(
        pack_kernel,
        out_shape=jax.ShapeDtypeStruct((SLAB_BLOCKS, TILE_ROWS + CAP, TILE_COLS), BF16),
        compiler_params=pltpu.CompilerParams(vmem_limit_bytes=60 * MIB),
        name="pack",
    )(x, pair_tiles[0].T, pair_count)


def select_kernel(at_ref, list_ref, *refs):
    sources, out_ref, all_ref = refs[:-2], refs[-2], refs[-1]
    at = 0
    for source in sources:
        all_ref[at : at + source.shape[0]] = source[...]
        at += source.shape[0]

    def one(dest, carry):
        at = at_ref[dest]
        for slot in range(SLOTS):
            out_ref[dest, slot] = all_ref[list_ref[at + slot]]
        return carry

    lax.fori_loop(0, SLAB_BLOCKS, one, 0, unroll=4)


def select(at, pairs, gathered):
    return pl.pallas_call(
        select_kernel,
        in_specs=[SMEM] * 2 + [VMEM] * len(gathered),
        out_specs=VMEM,
        out_shape=jax.ShapeDtypeStruct((SLAB_BLOCKS, SLOTS, TILE_ROWS, TILE_COLS), BF16),
        scratch_shapes=[pltpu.VMEM((sum(g.shape[0] for g in gathered), TILE_ROWS, TILE_COLS), BF16)],
        compiler_params=pltpu.CompilerParams(vmem_limit_bytes=32 * MIB),
        cost_estimate=pl.CostEstimate(flops=0, bytes_accessed=8 * MIB, transcendentals=0),
        name="select",
    )(at, pairs, *gathered)


def gather_block(held_ref, slot):
    rows = []
    for r in range(ROWS // TILE_ROWS):
        tiles = [held_ref[r * COL_TILES + c, slot].astype(F32) for c in range(COL_TILES)]
        rows.append(jnp.concatenate(tiles, axis=1))
    return jnp.concatenate(rows, axis=0).astype(BF16)


def far_steps(count, held_ref, query_ref, wk_ref, wv_ref, state_refs):
    def step(i, carry):
        slots = [GULP * i + u for u in range(GULP)]
        x = jnp.concatenate([gather_block(held_ref, slot) for slot in slots], axis=0)
        bias = [jnp.where(slot < count, 0.0, FLOOR).astype(F32) for slot in slots]
        state = read_state(*state_refs)
        state = absorb(state, project(x, wk_ref), project(x, wv_ref), query_ref, bias=bias)
        write_state(state, *state_refs)
        return carry

    lax.fori_loop(0, (count + GULP - 1) // GULP, step, 0)


def far_kernel(
    count_ref, held_ref, query_ref, wk_ref, wv_ref, top_in, total_in, accum_in, top_ref, total_ref, accum_ref
):
    top_ref[...] = top_in[...]
    total_ref[...] = total_in[...]
    accum_ref[...] = accum_in[...]
    far_steps(count_ref[0], held_ref, query_ref, wk_ref, wv_ref, (top_ref, total_ref, accum_ref))


def far(count, held, query, wk, wv, state):
    return pl.pallas_call(
        far_kernel,
        in_specs=[SMEM] + [VMEM] * 7,
        out_specs=(VMEM,) * 3,
        out_shape=STATE_SHAPES,
        compiler_params=pltpu.CompilerParams(vmem_limit_bytes=32 * MIB),
        name="far",
    )(count, held, query, wk, wv, *state)


def layer_norm(value, gain, bias):
    mean = jnp.mean(value, -1, keepdims=True)
    centred = value - mean
    spread = jnp.mean(centred * centred, -1, keepdims=True)
    return centred * lax.rsqrt(spread + 1e-05) * gain + bias


def finish_kernel(
    count_ref,
    held_ref,
    query_ref,
    wk_ref,
    wv_ref,
    top_in,
    total_in,
    accum_in,
    x_ref,
    g1_ref,
    b1_ref,
    b_up_ref,
    g2_ref,
    b2_ref,
    w_out_hbm,
    w_up_hbm,
    w_down_hbm,
    out_ref,
    top_ref,
    total_ref,
    accum_ref,
    w_out_ref,
    w_up_ref,
    w_down_ref,
    sems,
):
    weights = ((w_out_hbm, w_out_ref), (w_up_hbm, w_up_ref), (w_down_hbm, w_down_ref))
    copies = [pltpu.make_async_copy(a, b, sems.at[n]) for n, (a, b) in enumerate(weights)]
    for copy in copies:
        copy.start()
    far_kernel(
        count_ref,
        held_ref,
        query_ref,
        wk_ref,
        wv_ref,
        top_in,
        total_in,
        accum_in,
        top_ref,
        total_ref,
        accum_ref,
    )
    columns = []
    for head in range(HEADS):
        lanes = slice(head % 2 * ROWS, (head % 2 + 1) * ROWS)
        total = total_ref[head // 2 : head // 2 + 1, lanes]
        accum = accum_ref[head * HEAD_DIM : (head + 1) * HEAD_DIM, :]
        columns.append((accum / total).astype(BF16))
    attended_t = jnp.concatenate(columns, axis=0)
    copies[0].wait()
    mixed = x_ref[...].astype(F32) + lax.dot_general(
        attended_t, w_out_ref[...], (((0,), (0,)), ((), ())), preferred_element_type=F32
    )
    normed = layer_norm(mixed, g1_ref[...], b1_ref[...]).astype(BF16)
    copies[1].wait()
    hidden = jnp.maximum(
        jnp.dot(normed, w_up_ref[...], preferred_element_type=F32) + b_up_ref[...], 0.0
    ).astype(BF16)
    copies[2].wait()
    second = normed.astype(F32) + jnp.dot(hidden, w_down_ref[...], preferred_element_type=F32)
    out_ref[...] = layer_norm(second, g2_ref[...], b2_ref[...])


def finish(count, held, query, wk, wv, state, x, g1, b1, b_up, g2, b2, w_out, w_up, w_down):
    hbm = pl.BlockSpec(memory_space=pltpu.HBM)
    return pl.pallas_call(
        finish_kernel,
        in_specs=[SMEM] + [VMEM] * 13 + [hbm] * 3,
        out_specs=(VMEM,) * 4,
        out_shape=(jax.ShapeDtypeStruct((ROWS, D), F32),) + STATE_SHAPES,
        scratch_shapes=[
            pltpu.VMEM((D, D), BF16),
            pltpu.VMEM((D, FF), BF16),
            pltpu.VMEM((FF, D), BF16),
            pltpu.SemaphoreType.DMA((3,)),
        ],
        compiler_params=pltpu.CompilerParams(vmem_limit_bytes=44 * MIB),
        cost_estimate=pl.CostEstimate(flops=4 * 10**9, bytes_accessed=8 * MIB, transcendentals=10**6),
        name="finish",
    )(
        count,
        held,
        query,
        wk,
        wv,
        *state,
        x,
        g1[None],
        b1[None],
        b_up[None],
        g2[None],
        b2[None],
        w_out,
        w_up,
        w_down,
    )


def pair_lists(held, z_high, core):
    size = held.shape[1]
    planes = lax.axis_size("zhi")
    slot = jnp.arange(size, dtype=jnp.int32)
    key_group = slot % (size // CAP)
    distance = z_high - key_group // SLAB_GROUPS
    distance = jnp.where(core == 0, distance, -distance) % planes
    query_index = held // MEMBERS
    key_slot = (distance * SLAB_BLOCKS + key_group % SLAB_GROUPS * MEMBERS)[None, :] + held % MEMBERS
    ahead = (query_index[:, None, :] < query_index[:, :, None]) | (
        (query_index[:, None, :] == query_index[:, :, None]) & (slot[None, None, :] < slot[None, :, None])
    )
    place = jnp.sum(ahead.astype(jnp.int32), axis=-1)
    pairs = jnp.sum(jnp.where(place[:, None, :] == slot[None, :, None], key_slot[:, None, :], 0), axis=-1)
    pairs = jnp.concatenate([pairs.reshape(-1), jnp.zeros((SLOTS,), jnp.int32)])
    member = jnp.arange(MEMBERS, dtype=jnp.int32)[None, :, None]
    start = jnp.sum((query_index[:, None, :] < member).astype(jnp.int32), axis=-1)
    count = jnp.sum((query_index[:, None, :] == member).astype(jnp.int32), axis=-1)
    start = start + size * jnp.arange(SLAB_GROUPS, dtype=jnp.int32)[:, None]
    return start.reshape(-1), count.reshape(-1), pairs


def gather_rings(tiles, codes):
    size = lax.axis_size("zhi")

    def move(value, step):
        pairs = [
            (2 * z + core, 2 * ((z + (step if core == 0 else -step)) % size) + core)
            for z in range(size)
            for core in range(2)
        ]
        return lax.ppermute(value, ("zhi", "core"), pairs)

    ahead, behind = [tiles], [tiles]
    for step in range(size // 2):
        ahead.append(move(ahead[-1], 1))
        if step < (size - 1) // 2:
            behind.append(move(behind[-1], -1))
    behind[-1], codes = lax.optimization_barrier((behind[-1], codes))
    return ahead + behind[:0:-1], codes


def swap(x, pairs):
    return lax.ppermute(x, AXES, [p for a, b in pairs for p in ((a, b), (b, a))])


def on_device(
    node_feats,
    graph_ids,
    pair_tiles,
    pair_count,
    w_query,
    w_key,
    w_value,
    w_out,
    ln1_gain,
    ln1_bias,
    w_up,
    b_up,
    w_down,
    ln2_gain,
    ln2_bias,
):
    z_high, own = lax.axis_index("zhi"), lax.axis_index(SLAB)
    devices = lax.axis_size(AXES)

    def exchange(value):
        return lax.all_to_all(value, SLAB, split_axis=0, concat_axis=0, tiled=True)

    got = exchange(pack(node_feats, pair_tiles, pair_count))
    beside = swap(node_feats, [(i, i + 1) for i in range(0, devices, 2)])
    across = swap(node_feats, [(i, i + 1) for i in range(1, devices - 1, 2)])
    tiles, beside, across = lax.optimization_barrier((got[:, :TILE_ROWS], beside, across))
    core = lax.axis_index("core")
    codes = got[::MEMBERS, TILE_ROWS:, : pair_tiles.shape[1]].astype(jnp.int32)
    gathered, codes = gather_rings(tiles, codes)
    start, count, pairs = pair_lists(codes.reshape(SLAB_GROUPS, -1), z_high, core)

    def mine(value):
        return lax.dynamic_slice_in_dim(value, own, 1, 0)

    fill = jnp.full((ROWS,), -1, jnp.int32)
    ids = jnp.concatenate([fill, graph_ids, fill])
    key_ids = lax.dynamic_slice_in_dim(ids, (z_high * SLAB_BLOCKS + own) * ROWS, 3 * ROWS, 0)
    query_ids = jnp.tile(key_ids[ROWS : 2 * ROWS], 2)[None, :]
    turned = key_ids.reshape(3, ROWS)[::-1].reshape(-1)
    key_ids = jnp.where(core == 0, turned, key_ids)
    query, *state = near(
        beside, node_feats, across, w_query, w_key, w_value, key_ids[:, None], query_ids
    )

    def fetch(at):
        held = exchange(select(start + jnp.minimum(at, count), pairs, gathered))
        return jnp.clip(mine(count) - at, 0, SLOTS), held

    def close(part, held, state):
        return finish(
            part,
            held,
            query,
            w_key,
            w_value,
            state,
            node_feats,
            ln1_gain,
            ln1_bias,
            b_up,
            ln2_gain,
            ln2_bias,
            w_out,
            w_up,
            w_down,
        )

    part, held = fetch(jnp.int32(0))
    out, *state = close(part, held, state)
    most = jnp.max(count)

    def go_on(state):
        def more(carry):
            at, state = carry
            part, held = fetch(at)
            return at + SLOTS, tuple(far(part, held, query, w_key, w_value, state))

        _, state = lax.while_loop(lambda carry: carry[0] < most, more, (jnp.int32(SLOTS), state))
        return close(jnp.zeros_like(part), held, state)[0]

    return lax.cond(most > SLOTS, go_on, lambda state: out, tuple(state))


def solution(mesh):
    inner = Mesh(mesh.devices.reshape(-1, 2, 2, 2, 4, 2), AXES)
    blk = ("zhi", "zlo", "ylo")
    in_specs = (P(AXES, None), P(), P(blk, None, None), P(blk, None)) + (P(),) * 11
    return jax.shard_map(
        on_device, mesh=inner, in_specs=in_specs, out_specs=P(AXES, None), check_vma=False
    )
```

```python
import jax
import jax.numpy as jnp
from jax import lax
from jax.experimental import pallas as pl
from jax.experimental.pallas import tpu as pltpu
from jax.sharding import Mesh
from jax.sharding import PartitionSpec as P

F32 = jnp.float32
BF16 = jnp.bfloat16

AXES = ("zhi", "zlo", "ylo", "yhi", "x", "core")
SLAB = ("zlo", "ylo", "yhi", "x", "core")
D = 512
FF = 1024
HEADS = 8
HEAD_DIM = 64
COUPLES = HEADS // 2
ROWS = 128
MEMBERS = 16
SLAB_GROUPS = 4
SLAB_BLOCKS = 64
CAP = 8
TILE_ROWS = 8
TILE_COLS = 128
COL_TILES = D // TILE_COLS
SLOTS = 15
GULP = 5
MIB = 1024 * 1024
FLOOR = -1e30

SMEM = pl.BlockSpec(memory_space=pltpu.SMEM)
VMEM = pl.BlockSpec(memory_space=pltpu.VMEM)


def absorb(state, keys, values, query_ref, mask=None, bias=()):
    bias = bias or (None,)
    size = keys.shape[0] // len(bias)
    new = []
    for couple in range(COUPLES):
        top, total, accum = state[couple]
        cols = slice(couple * 2 * HEAD_DIM, (couple + 1) * 2 * HEAD_DIM)
        scores = [
            jnp.dot(keys[n * size : (n + 1) * size, cols], query_ref[couple], preferred_element_type=F32)
            for n in range(len(bias))
        ]
        if mask is not None:
            scores = [jnp.where(mask, scores[0], FLOOR)]
        new_top = top
        for part, shift in zip(scores, bias):
            best = jnp.max(part, axis=0, keepdims=True)
            new_top = jnp.maximum(new_top, best if shift is None else best + shift)
        decay = jnp.exp(top - new_top)
        total = total * decay
        probs = []
        for part, shift in zip(scores, bias):
            prob = jnp.exp(part - (new_top if shift is None else new_top - shift))
            total = total + jnp.sum(prob, axis=0, keepdims=True)
            probs.append(prob.astype(BF16))
        part = lax.dot_general(
            values[:, cols],
            jnp.concatenate(probs, axis=0),
            (((0,), (0,)), ((), ())),
            preferred_element_type=F32,
        )
        accum = jnp.concatenate(
            [
                accum[:HEAD_DIM] * decay[:, :ROWS] + part[:HEAD_DIM, :ROWS],
                accum[HEAD_DIM:] * decay[:, ROWS:] + part[HEAD_DIM:, ROWS:],
            ],
            axis=0,
        )
        new.append((new_top, total, accum))
    return new


def read_state(top_ref, total_ref, accum_ref):
    return [
        (
            top_ref[c : c + 1, :],
            total_ref[c : c + 1, :],
            accum_ref[c * 2 * HEAD_DIM : (c + 1) * 2 * HEAD_DIM, :],
        )
        for c in range(COUPLES)
    ]


def write_state(state, top_ref, total_ref, accum_ref):
    for c, (top, total, accum) in enumerate(state):
        top_ref[c : c + 1, :] = top
        total_ref[c : c + 1, :] = total
        accum_ref[c * 2 * HEAD_DIM : (c + 1) * 2 * HEAD_DIM, :] = accum


def project(x, weight_ref):
    return jnp.dot(x, weight_ref[...], preferred_element_type=F32).astype(BF16)


STATE_SHAPES = (
    jax.ShapeDtypeStruct((COUPLES, 2 * ROWS), F32),
    jax.ShapeDtypeStruct((COUPLES, 2 * ROWS), F32),
    jax.ShapeDtypeStruct((D, ROWS), F32),
)


def near_kernel(
    beside_ref, x_ref, across_ref, wq_ref, wk_ref, wv_ref, kid_ref, qid_ref, query_ref, top_ref, total_ref, accum_ref
):
    x = x_ref[...]
    query = jnp.dot(x, wq_ref[...], preferred_element_type=F32).astype(BF16).astype(F32)
    query_t = (query.T * (1.0 / 8.0)).astype(BF16)
    zero = jnp.zeros((HEAD_DIM, ROWS), BF16)
    for couple in range(COUPLES):
        at = couple * 2 * HEAD_DIM
        first = query_t[at : at + HEAD_DIM]
        second = query_t[at + HEAD_DIM : at + 2 * HEAD_DIM]
        query_ref[couple] = jnp.concatenate(
            [jnp.concatenate([first, zero], axis=1), jnp.concatenate([zero, second], axis=1)], axis=0
        )
    state = [
        (
            jnp.full((1, 2 * ROWS), FLOOR, F32),
            jnp.zeros((1, 2 * ROWS), F32),
            jnp.zeros((2 * HEAD_DIM, ROWS), F32),
        )
    ] * COUPLES
    sources = jnp.concatenate([beside_ref[...], x, across_ref[...]], axis=0)
    mask = kid_ref[...] == qid_ref[...]
    state = absorb(state, project(sources, wk_ref), project(sources, wv_ref), query_ref, mask)
    write_state(state, top_ref, total_ref, accum_ref)


def near(beside, x, across, wq, wk, wv, key_ids, query_ids):
    return pl.pallas_call(
        near_kernel,
        out_shape=(jax.ShapeDtypeStruct((COUPLES, 2 * HEAD_DIM, 2 * ROWS), BF16),) + STATE_SHAPES,
        compiler_params=pltpu.CompilerParams(vmem_limit_bytes=32 * MIB),
        cost_estimate=pl.CostEstimate(flops=10**9, bytes_accessed=3 * MIB, transcendentals=400000),
        name="near",
    )(beside, x, across, wq, wk, wv, key_ids, query_ids)


def pack_kernel(x_ref, tiles_ref, counts_ref, out_ref):
    x = x_ref[...].astype(F32)
    used = lax.broadcasted_iota(jnp.int32, tiles_ref.shape, 0) < counts_ref[...]
    codes = jnp.where(used, tiles_ref[...], MEMBERS * MEMBERS).astype(F32)
    codes = jnp.concatenate([codes, jnp.zeros((CAP, TILE_COLS - codes.shape[1]), F32)], axis=1)
    for n in range(SLAB_BLOCKS):
        row, col = n // COL_TILES * TILE_ROWS, n % COL_TILES * TILE_COLS
        tile = x[row : row + TILE_ROWS, col : col + TILE_COLS]
        out_ref[n] = jnp.concatenate([tile, codes], axis=0).astype(BF16)


def pack(x, pair_tiles, pair_count):
    return pl.pallas_call(
        pack_kernel,
        out_shape=jax.ShapeDtypeStruct((SLAB_BLOCKS, TILE_ROWS + CAP, TILE_COLS), BF16),
        compiler_params=pltpu.CompilerParams(vmem_limit_bytes=60 * MIB),
        name="pack",
    )(x, pair_tiles[0].T, pair_count)


def select_kernel(at_ref, start_ref, count_ref, list_ref, *refs):
    sources, out_ref, all_ref = refs[:-2], refs[-2], refs[-1]
    at = 0
    for source in sources:
        all_ref[at : at + source.shape[0]] = source[...]
        at += source.shape[0]

    def one(dest, carry):
        group, member = dest // MEMBERS, dest % MEMBERS
        at = start_ref[group, member] + jnp.minimum(at_ref[0], count_ref[group, member])
        for slot in range(SLOTS):
            out_ref[dest, slot] = all_ref[list_ref[group, at + slot]]
        return carry

    lax.fori_loop(0, SLAB_BLOCKS, one, 0, unroll=4)


def select(at, start, count, pairs, gathered):
    return pl.pallas_call(
        select_kernel,
        in_specs=[SMEM] * 4 + [VMEM] * len(gathered),
        out_specs=VMEM,
        out_shape=jax.ShapeDtypeStruct((SLAB_BLOCKS, SLOTS, TILE_ROWS, TILE_COLS), BF16),
        scratch_shapes=[pltpu.VMEM((sum(g.shape[0] for g in gathered), TILE_ROWS, TILE_COLS), BF16)],
        compiler_params=pltpu.CompilerParams(vmem_limit_bytes=32 * MIB),
        cost_estimate=pl.CostEstimate(flops=0, bytes_accessed=8 * MIB, transcendentals=0),
        name="select",
    )(at, start, count, pairs, *gathered)


def gather_block(held_ref, slot):
    rows = []
    for r in range(ROWS // TILE_ROWS):
        tiles = [held_ref[r * COL_TILES + c, slot].astype(F32) for c in range(COL_TILES)]
        rows.append(jnp.concatenate(tiles, axis=1))
    return jnp.concatenate(rows, axis=0).astype(BF16)


def far_steps(count, held_ref, query_ref, wk_ref, wv_ref, state_refs):
    def step(i, carry):
        slots = [GULP * i + u for u in range(GULP)]
        x = jnp.concatenate([gather_block(held_ref, slot) for slot in slots], axis=0)
        bias = [jnp.where(slot < count, 0.0, FLOOR).astype(F32) for slot in slots]
        state = read_state(*state_refs)
        state = absorb(state, project(x, wk_ref), project(x, wv_ref), query_ref, bias=bias)
        write_state(state, *state_refs)
        return carry

    lax.fori_loop(0, (count + GULP - 1) // GULP, step, 0)


def far_kernel(
    count_ref, held_ref, query_ref, wk_ref, wv_ref, top_in, total_in, accum_in, top_ref, total_ref, accum_ref
):
    top_ref[...] = top_in[...]
    total_ref[...] = total_in[...]
    accum_ref[...] = accum_in[...]
    far_steps(count_ref[0], held_ref, query_ref, wk_ref, wv_ref, (top_ref, total_ref, accum_ref))


def far(count, held, query, wk, wv, state):
    return pl.pallas_call(
        far_kernel,
        in_specs=[SMEM] + [VMEM] * 7,
        out_specs=(VMEM,) * 3,
        out_shape=STATE_SHAPES,
        compiler_params=pltpu.CompilerParams(vmem_limit_bytes=32 * MIB),
        name="far",
    )(count, held, query, wk, wv, *state)


def layer_norm(value, gain, bias):
    mean = jnp.mean(value, -1, keepdims=True)
    centred = value - mean
    spread = jnp.mean(centred * centred, -1, keepdims=True)
    return centred * lax.rsqrt(spread + 1e-05) * gain + bias


def finish_kernel(
    count_ref,
    held_ref,
    query_ref,
    wk_ref,
    wv_ref,
    top_in,
    total_in,
    accum_in,
    x_ref,
    g1_ref,
    b1_ref,
    b_up_ref,
    g2_ref,
    b2_ref,
    w_out_hbm,
    w_up_hbm,
    w_down_hbm,
    out_ref,
    top_ref,
    total_ref,
    accum_ref,
    w_out_ref,
    w_up_ref,
    w_down_ref,
    sems,
):
    weights = ((w_out_hbm, w_out_ref), (w_up_hbm, w_up_ref), (w_down_hbm, w_down_ref))
    copies = [pltpu.make_async_copy(a, b, sems.at[n]) for n, (a, b) in enumerate(weights)]
    for copy in copies:
        copy.start()
    far_kernel(
        count_ref,
        held_ref,
        query_ref,
        wk_ref,
        wv_ref,
        top_in,
        total_in,
        accum_in,
        top_ref,
        total_ref,
        accum_ref,
    )
    columns = []
    for head in range(HEADS):
        lanes = slice(head % 2 * ROWS, (head % 2 + 1) * ROWS)
        total = total_ref[head // 2 : head // 2 + 1, lanes]
        accum = accum_ref[head * HEAD_DIM : (head + 1) * HEAD_DIM, :]
        columns.append((accum / total).astype(BF16))
    attended_t = jnp.concatenate(columns, axis=0)
    copies[0].wait()
    mixed = x_ref[...].astype(F32) + lax.dot_general(
        attended_t, w_out_ref[...], (((0,), (0,)), ((), ())), preferred_element_type=F32
    )
    normed = layer_norm(mixed, g1_ref[...], b1_ref[...]).astype(BF16)
    copies[1].wait()
    hidden = jnp.maximum(
        jnp.dot(normed, w_up_ref[...], preferred_element_type=F32) + b_up_ref[...], 0.0
    ).astype(BF16)
    copies[2].wait()
    second = normed.astype(F32) + jnp.dot(hidden, w_down_ref[...], preferred_element_type=F32)
    out_ref[...] = layer_norm(second, g2_ref[...], b2_ref[...])


def finish(count, held, query, wk, wv, state, x, g1, b1, b_up, g2, b2, w_out, w_up, w_down):
    hbm = pl.BlockSpec(memory_space=pltpu.HBM)
    return pl.pallas_call(
        finish_kernel,
        in_specs=[SMEM] + [VMEM] * 13 + [hbm] * 3,
        out_specs=(VMEM,) * 4,
        out_shape=(jax.ShapeDtypeStruct((ROWS, D), F32),) + STATE_SHAPES,
        scratch_shapes=[
            pltpu.VMEM((D, D), BF16),
            pltpu.VMEM((D, FF), BF16),
            pltpu.VMEM((FF, D), BF16),
            pltpu.SemaphoreType.DMA((3,)),
        ],
        compiler_params=pltpu.CompilerParams(vmem_limit_bytes=44 * MIB),
        cost_estimate=pl.CostEstimate(flops=4 * 10**9, bytes_accessed=8 * MIB, transcendentals=10**6),
        name="finish",
    )(
        count,
        held,
        query,
        wk,
        wv,
        *state,
        x,
        g1[None],
        b1[None],
        b_up[None],
        g2[None],
        b2[None],
        w_out,
        w_up,
        w_down,
    )


def pair_lists(held, z_high, core):
    size = held.shape[1]
    planes = lax.axis_size("zhi")
    slot = jnp.arange(size, dtype=jnp.int32)
    key_group = slot % (size // CAP)
    distance = z_high - key_group // SLAB_GROUPS
    distance = jnp.where(core == 0, distance, -distance) % planes
    query_index = held // MEMBERS
    key_slot = (distance * SLAB_BLOCKS + key_group % SLAB_GROUPS * MEMBERS)[None, :] + held % MEMBERS
    ahead = (query_index[:, None, :] < query_index[:, :, None]) | (
        (query_index[:, None, :] == query_index[:, :, None]) & (slot[None, None, :] < slot[None, :, None])
    )
    place = jnp.sum(ahead.astype(jnp.int32), axis=-1)
    pairs = jnp.sum(jnp.where(place[:, None, :] == slot[None, :, None], key_slot[:, None, :], 0), axis=-1)
    pairs = jnp.pad(pairs, ((0, 0), (0, SLOTS)))
    member = jnp.arange(MEMBERS, dtype=jnp.int32)[None, :, None]
    start = jnp.sum((query_index[:, None, :] < member).astype(jnp.int32), axis=-1)
    count = jnp.sum((query_index[:, None, :] == member).astype(jnp.int32), axis=-1)
    return start, count, pairs


def gather_rings(tiles):
    size = lax.axis_size("zhi")

    def move(value, step):
        pairs = [
            (2 * z + core, 2 * ((z + (step if core == 0 else -step)) % size) + core)
            for z in range(size)
            for core in range(2)
        ]
        return lax.ppermute(value, ("zhi", "core"), pairs)

    ahead, behind = [tiles], [tiles]
    for step in range(size // 2):
        ahead.append(move(ahead[-1], 1))
        if step < (size - 1) // 2:
            behind.append(move(behind[-1], -1))
    return ahead + behind[:0:-1]


def swap(x, pairs):
    return lax.ppermute(x, AXES, [p for a, b in pairs for p in ((a, b), (b, a))])


def on_device(
    node_feats,
    graph_ids,
    pair_tiles,
    pair_count,
    w_query,
    w_key,
    w_value,
    w_out,
    ln1_gain,
    ln1_bias,
    w_up,
    b_up,
    w_down,
    ln2_gain,
    ln2_bias,
):
    z_high, own = lax.axis_index("zhi"), lax.axis_index(SLAB)
    devices = lax.axis_size(AXES)

    def exchange(value):
        return lax.all_to_all(value, SLAB, split_axis=0, concat_axis=0, tiled=True)

    got = exchange(pack(node_feats, pair_tiles, pair_count))
    beside = swap(node_feats, [(i, i + 1) for i in range(0, devices, 2)])
    across = swap(node_feats, [(i, i + 1) for i in range(1, devices - 1, 2)])
    tiles, beside, across = lax.optimization_barrier((got[:, :TILE_ROWS], beside, across))
    core = lax.axis_index("core")
    gathered = gather_rings(tiles)
    codes = got[::MEMBERS, TILE_ROWS:, : pair_tiles.shape[1]].astype(jnp.int32)
    start, count, pairs = pair_lists(codes.reshape(SLAB_GROUPS, -1), z_high, core)

    def mine(value):
        return lax.dynamic_slice_in_dim(value.reshape(-1), own, 1, 0)

    fill = jnp.full((ROWS,), -1, jnp.int32)
    ids = jnp.concatenate([fill, graph_ids, fill])
    key_ids = lax.dynamic_slice_in_dim(ids, (z_high * SLAB_BLOCKS + own) * ROWS, 3 * ROWS, 0)
    query_ids = jnp.tile(key_ids[ROWS : 2 * ROWS], 2)[None, :]
    turned = key_ids.reshape(3, ROWS)[::-1].reshape(-1)
    key_ids = jnp.where(core == 0, turned, key_ids)
    query, *state = near(
        beside, node_feats, across, w_query, w_key, w_value, key_ids[:, None], query_ids
    )

    def fetch(at):
        held = exchange(select(at.reshape(1), start, count, pairs, gathered))
        return jnp.clip(mine(count) - at, 0, SLOTS), held

    def close(part, held, state):
        return finish(
            part,
            held,
            query,
            w_key,
            w_value,
            state,
            node_feats,
            ln1_gain,
            ln1_bias,
            b_up,
            ln2_gain,
            ln2_bias,
            w_out,
            w_up,
            w_down,
        )

    part, held = fetch(jnp.int32(0))
    out, *state = close(part, held, state)
    most = jnp.max(count)

    def go_on(state):
        def more(carry):
            at, state = carry
            part, held = fetch(at)
            return at + SLOTS, tuple(far(part, held, query, w_key, w_value, state))

        _, state = lax.while_loop(lambda carry: carry[0] < most, more, (jnp.int32(SLOTS), state))
        return close(jnp.zeros_like(part), held, state)[0]

    return lax.cond(most > SLOTS, go_on, lambda state: out, tuple(state))


def solution(mesh):
    inner = Mesh(mesh.devices.reshape(-1, 2, 2, 2, 4, 2), AXES)
    blk = ("zhi", "zlo", "ylo")
    in_specs = (P(AXES, None), P(), P(blk, None, None), P(blk, None)) + (P(),) * 11
    return jax.shard_map(
        on_device, mesh=inner, in_specs=in_specs, out_specs=P(AXES, None), check_vma=False
    )
```

```python
import jax
import jax.numpy as jnp
from jax import lax
from jax.experimental import pallas as pl
from jax.experimental.pallas import tpu as pltpu
from jax.sharding import Mesh
from jax.sharding import PartitionSpec as P

F32 = jnp.float32
BF16 = jnp.bfloat16

AXES = ("zhi", "zlo", "ylo", "yhi", "x", "core")
SLAB = ("zlo", "ylo", "yhi", "x", "core")
D = 512
FF = 1024
HEADS = 8
HEAD_DIM = 64
COUPLES = HEADS // 2
ROWS = 128
MEMBERS = 16
SLAB_GROUPS = 4
SLAB_BLOCKS = 64
CAP = 8
TILE_ROWS = 8
TILE_COLS = 128
COL_TILES = D // TILE_COLS
SLOTS = 15
GULP = 5
MIB = 1024 * 1024
FLOOR = -1e30

SMEM = pl.BlockSpec(memory_space=pltpu.SMEM)
VMEM = pl.BlockSpec(memory_space=pltpu.VMEM)


def absorb(state, keys, values, query_ref, mask=None, bias=()):
    bias = bias or (None,)
    size = keys.shape[0] // len(bias)
    new = []
    for couple in range(COUPLES):
        top, total, accum = state[couple]
        cols = slice(couple * 2 * HEAD_DIM, (couple + 1) * 2 * HEAD_DIM)
        scores = [
            jnp.dot(keys[n * size : (n + 1) * size, cols], query_ref[couple], preferred_element_type=F32)
            for n in range(len(bias))
        ]
        if mask is not None:
            scores = [jnp.where(mask, scores[0], FLOOR)]
        new_top = top
        for part, shift in zip(scores, bias):
            best = jnp.max(part, axis=0, keepdims=True)
            new_top = jnp.maximum(new_top, best if shift is None else best + shift)
        decay = jnp.exp(top - new_top)
        total = total * decay
        probs = []
        for part, shift in zip(scores, bias):
            prob = jnp.exp(part - (new_top if shift is None else new_top - shift))
            total = total + jnp.sum(prob, axis=0, keepdims=True)
            probs.append(prob.astype(BF16))
        part = lax.dot_general(
            values[:, cols],
            jnp.concatenate(probs, axis=0),
            (((0,), (0,)), ((), ())),
            preferred_element_type=F32,
        )
        accum = jnp.concatenate(
            [
                accum[:HEAD_DIM] * decay[:, :ROWS] + part[:HEAD_DIM, :ROWS],
                accum[HEAD_DIM:] * decay[:, ROWS:] + part[HEAD_DIM:, ROWS:],
            ],
            axis=0,
        )
        new.append((new_top, total, accum))
    return new


def read_state(top_ref, total_ref, accum_ref):
    return [
        (
            top_ref[c : c + 1, :],
            total_ref[c : c + 1, :],
            accum_ref[c * 2 * HEAD_DIM : (c + 1) * 2 * HEAD_DIM, :],
        )
        for c in range(COUPLES)
    ]


def write_state(state, top_ref, total_ref, accum_ref):
    for c, (top, total, accum) in enumerate(state):
        top_ref[c : c + 1, :] = top
        total_ref[c : c + 1, :] = total
        accum_ref[c * 2 * HEAD_DIM : (c + 1) * 2 * HEAD_DIM, :] = accum


def project(x, weight_ref):
    return jnp.dot(x, weight_ref[...], preferred_element_type=F32).astype(BF16)


STATE_SHAPES = (
    jax.ShapeDtypeStruct((COUPLES, 2 * ROWS), F32),
    jax.ShapeDtypeStruct((COUPLES, 2 * ROWS), F32),
    jax.ShapeDtypeStruct((D, ROWS), F32),
)


def near_kernel(
    beside_ref, x_ref, across_ref, wq_ref, wk_ref, wv_ref, kid_ref, qid_ref, query_ref, top_ref, total_ref, accum_ref
):
    x = x_ref[...]
    query = jnp.dot(x, wq_ref[...], preferred_element_type=F32).astype(BF16).astype(F32)
    query_t = (query.T * (1.0 / 8.0)).astype(BF16)
    zero = jnp.zeros((HEAD_DIM, ROWS), BF16)
    for couple in range(COUPLES):
        at = couple * 2 * HEAD_DIM
        first = query_t[at : at + HEAD_DIM]
        second = query_t[at + HEAD_DIM : at + 2 * HEAD_DIM]
        query_ref[couple] = jnp.concatenate(
            [jnp.concatenate([first, zero], axis=1), jnp.concatenate([zero, second], axis=1)], axis=0
        )
    state = [
        (
            jnp.full((1, 2 * ROWS), FLOOR, F32),
            jnp.zeros((1, 2 * ROWS), F32),
            jnp.zeros((2 * HEAD_DIM, ROWS), F32),
        )
    ] * COUPLES
    sources = jnp.concatenate([beside_ref[...], x, across_ref[...]], axis=0)
    mask = kid_ref[...] == qid_ref[...]
    state = absorb(state, project(sources, wk_ref), project(sources, wv_ref), query_ref, mask)
    write_state(state, top_ref, total_ref, accum_ref)


def near(beside, x, across, wq, wk, wv, key_ids, query_ids):
    return pl.pallas_call(
        near_kernel,
        out_shape=(jax.ShapeDtypeStruct((COUPLES, 2 * HEAD_DIM, 2 * ROWS), BF16),) + STATE_SHAPES,
        compiler_params=pltpu.CompilerParams(vmem_limit_bytes=32 * MIB),
        cost_estimate=pl.CostEstimate(flops=10**9, bytes_accessed=3 * MIB, transcendentals=400000),
        name="near",
    )(beside, x, across, wq, wk, wv, key_ids, query_ids)


def pack_kernel(x_ref, tiles_ref, counts_ref, out_ref):
    x = x_ref[...].astype(F32)
    used = lax.broadcasted_iota(jnp.int32, tiles_ref.shape, 0) < counts_ref[...]
    codes = jnp.where(used, tiles_ref[...], MEMBERS * MEMBERS).astype(F32)
    codes = jnp.concatenate([codes, jnp.zeros((CAP, TILE_COLS - codes.shape[1]), F32)], axis=1)
    for n in range(SLAB_BLOCKS):
        row, col = n // COL_TILES * TILE_ROWS, n % COL_TILES * TILE_COLS
        tile = x[row : row + TILE_ROWS, col : col + TILE_COLS]
        out_ref[n] = jnp.concatenate([tile, codes], axis=0).astype(BF16)


def pack(x, pair_tiles, pair_count):
    return pl.pallas_call(
        pack_kernel,
        out_shape=jax.ShapeDtypeStruct((SLAB_BLOCKS, TILE_ROWS + CAP, TILE_COLS), BF16),
        compiler_params=pltpu.CompilerParams(vmem_limit_bytes=60 * MIB),
        name="pack",
    )(x, pair_tiles[0].T, pair_count)


def select_kernel(at_ref, start_ref, count_ref, list_ref, *refs):
    sources, out_ref, all_ref = refs[:-2], refs[-2], refs[-1]
    at = 0
    for source in sources:
        all_ref[at : at + source.shape[0]] = source[...]
        at += source.shape[0]

    per_group = (list_ref.shape[0] - SLOTS) // SLAB_GROUPS

    def one(dest, carry):
        group, member = dest // MEMBERS, dest % MEMBERS
        at = start_ref[group, member] + jnp.minimum(at_ref[0], count_ref[group, member])
        at = at + group * per_group
        for slot in range(SLOTS):
            out_ref[dest, slot] = all_ref[list_ref[at + slot]]
        return carry

    lax.fori_loop(0, SLAB_BLOCKS, one, 0, unroll=4)


def select(at, start, count, pairs, gathered):
    return pl.pallas_call(
        select_kernel,
        in_specs=[SMEM] * 4 + [VMEM] * len(gathered),
        out_specs=VMEM,
        out_shape=jax.ShapeDtypeStruct((SLAB_BLOCKS, SLOTS, TILE_ROWS, TILE_COLS), BF16),
        scratch_shapes=[pltpu.VMEM((sum(g.shape[0] for g in gathered), TILE_ROWS, TILE_COLS), BF16)],
        compiler_params=pltpu.CompilerParams(vmem_limit_bytes=32 * MIB),
        cost_estimate=pl.CostEstimate(flops=0, bytes_accessed=8 * MIB, transcendentals=0),
        name="select",
    )(at, start, count, pairs, *gathered)


def gather_block(held_ref, slot):
    rows = []
    for r in range(ROWS // TILE_ROWS):
        tiles = [held_ref[r * COL_TILES + c, slot].astype(F32) for c in range(COL_TILES)]
        rows.append(jnp.concatenate(tiles, axis=1))
    return jnp.concatenate(rows, axis=0).astype(BF16)


def far_steps(count, held_ref, query_ref, wk_ref, wv_ref, state_refs):
    def step(i, carry):
        slots = [GULP * i + u for u in range(GULP)]
        x = jnp.concatenate([gather_block(held_ref, slot) for slot in slots], axis=0)
        bias = [jnp.where(slot < count, 0.0, FLOOR).astype(F32) for slot in slots]
        state = read_state(*state_refs)
        state = absorb(state, project(x, wk_ref), project(x, wv_ref), query_ref, bias=bias)
        write_state(state, *state_refs)
        return carry

    lax.fori_loop(0, (count + GULP - 1) // GULP, step, 0)


def far_kernel(
    count_ref, held_ref, query_ref, wk_ref, wv_ref, top_in, total_in, accum_in, top_ref, total_ref, accum_ref
):
    top_ref[...] = top_in[...]
    total_ref[...] = total_in[...]
    accum_ref[...] = accum_in[...]
    far_steps(count_ref[0], held_ref, query_ref, wk_ref, wv_ref, (top_ref, total_ref, accum_ref))


def far(count, held, query, wk, wv, state):
    return pl.pallas_call(
        far_kernel,
        in_specs=[SMEM] + [VMEM] * 7,
        out_specs=(VMEM,) * 3,
        out_shape=STATE_SHAPES,
        compiler_params=pltpu.CompilerParams(vmem_limit_bytes=32 * MIB),
        name="far",
    )(count, held, query, wk, wv, *state)


def layer_norm(value, gain, bias):
    mean = jnp.mean(value, -1, keepdims=True)
    centred = value - mean
    spread = jnp.mean(centred * centred, -1, keepdims=True)
    return centred * lax.rsqrt(spread + 1e-05) * gain + bias


def finish_kernel(
    count_ref,
    held_ref,
    query_ref,
    wk_ref,
    wv_ref,
    top_in,
    total_in,
    accum_in,
    x_ref,
    g1_ref,
    b1_ref,
    b_up_ref,
    g2_ref,
    b2_ref,
    w_out_hbm,
    w_up_hbm,
    w_down_hbm,
    out_ref,
    top_ref,
    total_ref,
    accum_ref,
    w_out_ref,
    w_up_ref,
    w_down_ref,
    sems,
):
    weights = ((w_out_hbm, w_out_ref), (w_up_hbm, w_up_ref), (w_down_hbm, w_down_ref))
    copies = [pltpu.make_async_copy(a, b, sems.at[n]) for n, (a, b) in enumerate(weights)]
    for copy in copies:
        copy.start()
    far_kernel(
        count_ref,
        held_ref,
        query_ref,
        wk_ref,
        wv_ref,
        top_in,
        total_in,
        accum_in,
        top_ref,
        total_ref,
        accum_ref,
    )
    columns = []
    for head in range(HEADS):
        lanes = slice(head % 2 * ROWS, (head % 2 + 1) * ROWS)
        total = total_ref[head // 2 : head // 2 + 1, lanes]
        accum = accum_ref[head * HEAD_DIM : (head + 1) * HEAD_DIM, :]
        columns.append((accum / total).astype(BF16))
    attended_t = jnp.concatenate(columns, axis=0)
    copies[0].wait()
    mixed = x_ref[...].astype(F32) + lax.dot_general(
        attended_t, w_out_ref[...], (((0,), (0,)), ((), ())), preferred_element_type=F32
    )
    normed = layer_norm(mixed, g1_ref[...], b1_ref[...]).astype(BF16)
    copies[1].wait()
    hidden = jnp.maximum(
        jnp.dot(normed, w_up_ref[...], preferred_element_type=F32) + b_up_ref[...], 0.0
    ).astype(BF16)
    copies[2].wait()
    second = normed.astype(F32) + jnp.dot(hidden, w_down_ref[...], preferred_element_type=F32)
    out_ref[...] = layer_norm(second, g2_ref[...], b2_ref[...])


def finish(count, held, query, wk, wv, state, x, g1, b1, b_up, g2, b2, w_out, w_up, w_down):
    hbm = pl.BlockSpec(memory_space=pltpu.HBM)
    return pl.pallas_call(
        finish_kernel,
        in_specs=[SMEM] + [VMEM] * 13 + [hbm] * 3,
        out_specs=(VMEM,) * 4,
        out_shape=(jax.ShapeDtypeStruct((ROWS, D), F32),) + STATE_SHAPES,
        scratch_shapes=[
            pltpu.VMEM((D, D), BF16),
            pltpu.VMEM((D, FF), BF16),
            pltpu.VMEM((FF, D), BF16),
            pltpu.SemaphoreType.DMA((3,)),
        ],
        compiler_params=pltpu.CompilerParams(vmem_limit_bytes=44 * MIB),
        cost_estimate=pl.CostEstimate(flops=4 * 10**9, bytes_accessed=8 * MIB, transcendentals=10**6),
        name="finish",
    )(
        count,
        held,
        query,
        wk,
        wv,
        *state,
        x,
        g1[None],
        b1[None],
        b_up[None],
        g2[None],
        b2[None],
        w_out,
        w_up,
        w_down,
    )


def pair_lists(held, z_high, core):
    size = held.shape[1]
    planes = lax.axis_size("zhi")
    slot = jnp.arange(size, dtype=jnp.int32)
    key_group = slot % (size // CAP)
    distance = z_high - key_group // SLAB_GROUPS
    distance = jnp.where(core == 0, distance, -distance) % planes
    query_index = held // MEMBERS
    key_slot = (distance * SLAB_BLOCKS + key_group % SLAB_GROUPS * MEMBERS)[None, :] + held % MEMBERS
    ahead = (query_index[:, None, :] < query_index[:, :, None]) | (
        (query_index[:, None, :] == query_index[:, :, None]) & (slot[None, None, :] < slot[None, :, None])
    )
    place = jnp.sum(ahead.astype(jnp.int32), axis=-1)
    pairs = jnp.sum(jnp.where(place[:, None, :] == slot[None, :, None], key_slot[:, None, :], 0), axis=-1)
    pairs = jnp.concatenate([pairs.reshape(-1), jnp.zeros((SLOTS,), jnp.int32)])
    member = jnp.arange(MEMBERS, dtype=jnp.int32)[None, :, None]
    start = jnp.sum((query_index[:, None, :] < member).astype(jnp.int32), axis=-1)
    count = jnp.sum((query_index[:, None, :] == member).astype(jnp.int32), axis=-1)
    return start, count, pairs


def gather_rings(tiles):
    size = lax.axis_size("zhi")

    def move(value, step):
        pairs = [
            (2 * z + core, 2 * ((z + (step if core == 0 else -step)) % size) + core)
            for z in range(size)
            for core in range(2)
        ]
        return lax.ppermute(value, ("zhi", "core"), pairs)

    ahead, behind = [tiles], [tiles]
    for step in range(size // 2):
        ahead.append(move(ahead[-1], 1))
        if step < (size - 1) // 2:
            behind.append(move(behind[-1], -1))
    return ahead + behind[:0:-1]


def swap(x, pairs):
    return lax.ppermute(x, AXES, [p for a, b in pairs for p in ((a, b), (b, a))])


def on_device(
    node_feats,
    graph_ids,
    pair_tiles,
    pair_count,
    w_query,
    w_key,
    w_value,
    w_out,
    ln1_gain,
    ln1_bias,
    w_up,
    b_up,
    w_down,
    ln2_gain,
    ln2_bias,
):
    z_high, own = lax.axis_index("zhi"), lax.axis_index(SLAB)
    devices = lax.axis_size(AXES)

    def exchange(value):
        return lax.all_to_all(value, SLAB, split_axis=0, concat_axis=0, tiled=True)

    got = exchange(pack(node_feats, pair_tiles, pair_count))
    beside = swap(node_feats, [(i, i + 1) for i in range(0, devices, 2)])
    across = swap(node_feats, [(i, i + 1) for i in range(1, devices - 1, 2)])
    tiles, beside, across = lax.optimization_barrier((got[:, :TILE_ROWS], beside, across))
    core = lax.axis_index("core")
    gathered = gather_rings(tiles)
    codes = got[::MEMBERS, TILE_ROWS:, : pair_tiles.shape[1]].astype(jnp.int32)
    start, count, pairs = pair_lists(codes.reshape(SLAB_GROUPS, -1), z_high, core)

    def mine(value):
        return lax.dynamic_slice_in_dim(value.reshape(-1), own, 1, 0)

    fill = jnp.full((ROWS,), -1, jnp.int32)
    ids = jnp.concatenate([fill, graph_ids, fill])
    key_ids = lax.dynamic_slice_in_dim(ids, (z_high * SLAB_BLOCKS + own) * ROWS, 3 * ROWS, 0)
    query_ids = jnp.tile(key_ids[ROWS : 2 * ROWS], 2)[None, :]
    turned = key_ids.reshape(3, ROWS)[::-1].reshape(-1)
    key_ids = jnp.where(core == 0, turned, key_ids)
    query, *state = near(
        beside, node_feats, across, w_query, w_key, w_value, key_ids[:, None], query_ids
    )

    def fetch(at):
        held = exchange(select(at.reshape(1), start, count, pairs, gathered))
        return jnp.clip(mine(count) - at, 0, SLOTS), held

    def close(part, held, state):
        return finish(
            part,
            held,
            query,
            w_key,
            w_value,
            state,
            node_feats,
            ln1_gain,
            ln1_bias,
            b_up,
            ln2_gain,
            ln2_bias,
            w_out,
            w_up,
            w_down,
        )

    part, held = fetch(jnp.int32(0))
    out, *state = close(part, held, state)
    most = jnp.max(count)

    def go_on(state):
        def more(carry):
            at, state = carry
            part, held = fetch(at)
            return at + SLOTS, tuple(far(part, held, query, w_key, w_value, state))

        _, state = lax.while_loop(lambda carry: carry[0] < most, more, (jnp.int32(SLOTS), state))
        return close(jnp.zeros_like(part), held, state)[0]

    return lax.cond(most > SLOTS, go_on, lambda state: out, tuple(state))


def solution(mesh):
    inner = Mesh(mesh.devices.reshape(-1, 2, 2, 2, 4, 2), AXES)
    blk = ("zhi", "zlo", "ylo")
    in_specs = (P(AXES, None), P(), P(blk, None, None), P(blk, None)) + (P(),) * 11
    return jax.shard_map(
        on_device, mesh=inner, in_specs=in_specs, out_specs=P(AXES, None), check_vma=False
    )
```
